256 devices in a mesh: dp: 4 (over x_lo, core), fsdp: 64 (over z, y, x_hi).
Axes of the slice: x: 4 (x_hi: 2, x_lo: 2; x = x_hi * 2 + x_lo), y: 4, z: 8, core: 2. Of those that a mesh axis runs over, the one named last changes fastest.
Arguments:
- train_hidden: bfloat16 [65536, 5120], P('fsdp'), may hold values from -6 to 6
- index_hidden: bfloat16 [4096, 5120], P('dp', 'fsdp'), may hold values from -6 to 6
- index_resid: bfloat16 [4096, 2048], P('fsdp', 'dp'), may hold values from -6 to 6
- basis: float32 [8, 5120, 2048], P(None, 'fsdp', 'dp'), may hold values from -6 to 6
Outputs:
- new_basis: float32 [1, 5120, 2048], P(None, 'fsdp', 'dp')
- hessenberg: float32 [1, 9], replicated
- projections: float32 [128, 9], P('dp')
The draws below stay inside these ranges and needn't reach their ends.
All inputs are finite; a program needn't handle non-finite values.
Results may differ from the reference program's by a relative error of at most 0.011.
Values may be sent and summed in bfloat16 or wider, within the bound.
A program may use at most 128 MiB of HBM per device.

```python
import jax
import jax.numpy as jnp
from jax import lax

D = 2048
FF = 5120
EX_TOK = 32
K = 8
ITERS = 1
TOKENS = 65536
EXAMPLES = 128
ITOKENS = 4096


def block_scale(key, dims, cuts, low, largest):
    loudness = 1.0
    for axis_at, parts in cuts:
        heights = jax.random.uniform(jax.random.fold_in(jax.random.fold_in(key, 6), axis_at), (parts,), jnp.float32, low / len(cuts), largest / len(cuts))
        loudness = loudness * jnp.repeat(jnp.exp(heights), dims[axis_at] // parts).reshape((-1,) + (1,) * (len(dims) - 1 - axis_at))
    return loudness


def bell_draw(rng, shape, scale, most, shards=(), kind=jnp.bfloat16):
    values = scale * jax.random.normal(rng, shape, jnp.float32)
    if shards:
        values = values * block_scale(rng, shape, shards, -0.22, 0.18)
    return jnp.clip(values, -most, most).astype(kind)


def setup_inputs(seed: int = 0) -> dict:
    splits = jax.random.split(jax.random.key(seed), 5)
    train_hidden = bell_draw(splits[0], (TOKENS, FF), 1.0, 6.0, ((0, 64),))
    index_hidden = bell_draw(splits[1], (ITOKENS, FF), 1.0, 6.0, ((0, 4), (1, 64)))
    index_resid = bell_draw(splits[2], (ITOKENS, D), 1.0, 6.0, ((0, 64), (1, 4)))
    basis = bell_draw(splits[3], (K, FF, D), 1.0, 6.0, ((1, 64), (2, 4)), jnp.float32)
    return {"train_hidden": train_hidden, "index_hidden": index_hidden, "index_resid": index_resid, "basis": basis}


def reference(train_hidden, index_hidden, index_resid, basis):
    mean_scale = 1.0 / (FF * D)

    def hessian_apply(direction):
        image = jnp.dot(train_hidden, direction.astype(jnp.bfloat16), preferred_element_type=jnp.float32).astype(jnp.bfloat16)
        curved = lax.dot_general(train_hidden, image, (((0,), (0,)), ((), ())), preferred_element_type=jnp.float32)
        return curved / TOKENS
    vectors = [basis[position] for position in range(K)]
    direction = basis[K - 1]
    columns = []
    fresh = []
    for step in range(ITERS):
        curved = hessian_apply(direction)
        coeffs = jnp.stack([jnp.sum(vector * curved) for vector in vectors]) * mean_scale
        orth = curved
        for position in range(len(vectors)):
            orth = orth - coeffs[position] * vectors[position]
        beta = jnp.sqrt(jnp.sum(orth * orth) * mean_scale)
        direction = orth / beta
        padding = jnp.zeros((K + ITERS - len(vectors) - 1,), jnp.float32)
        columns.append(jnp.concatenate([coeffs, beta[None], padding]))
        vectors.append(direction)
        fresh.append(direction)
    wide_hidden = index_hidden.astype(jnp.float32)
    projected = []
    for vector in vectors:
        narrow = vector.astype(jnp.bfloat16)
        mapped = lax.dot_general(index_resid, narrow, (((1,), (1,)), ((), ())), preferred_element_type=jnp.float32)
        per_token = lax.optimization_barrier(jnp.sum(mapped * wide_hidden, axis=1))
        projected.append(lax.optimization_barrier(jnp.sum(per_token.reshape(EXAMPLES, EX_TOK), axis=1)))
    projections = jnp.stack(projected, axis=1) * (FF * D) ** (-0.5)
    return (jnp.stack(fresh), jnp.stack(columns), projections)
```

```python
import functools

import jax
import jax.numpy as jnp
from jax import lax
from jax.experimental import pallas as pl
from jax.experimental.pallas import tpu as pltpu
from jax.sharding import PartitionSpec as P

D = 2048
FF = 5120
TOKENS = 65536
EX_TOK = 32
K = 8
NZ, NY = 8, 4
BLK = 80
WID = 512
ROWS_A, ROWS_B = 32, 48
MESH = pl.DeviceIdType.MESH
BF = jnp.bfloat16
F32 = jnp.float32
SIGNS = (1, -1)


def half_of(sign):
    return 0 if sign > 0 else 1


def wrap(delta, size):
    delta %= size
    return delta - size if delta > size // 2 else delta


def parts_of(kind, hop, own):
    if hop == 1 and own:
        return ("o", "t")
    return ("f",)


def link_of(msg):
    kind = msg[0]
    if kind in ("Az", "az"):
        return ("z", msg[2])
    if kind in ("Ay", "ay", "Ry", "RY"):
        return ("y", msg[1])
    if kind in ("Bz", "bz", "Rz", "RZ"):
        return ("z", msg[1])
    if kind in ("By", "by"):
        return ("y", msg[2])
    if kind in ("qx", "vx", "hx", "xa", "xb", "hl"):
        return ("x", 0)
    return ("c", 0) if kind == "hc" else (kind, msg[1])


def kilobytes(msg):
    kind = msg[0]
    a, b = 2 * ROWS_A, 2 * ROWS_B
    if kind == "Ay":
        return a / 2 if msg[3] in ("o", "t") or msg[2] == 2 else a
    if kind == "Az":
        return a / 2 if msg[4] in ("o", "t") or msg[3] == 4 else a
    if kind == "Bz":
        return b / 2 if msg[3] in ("o", "t") or msg[2] == 4 else b
    if kind == "By":
        return b / 2 if msg[4] in ("o", "t") or msg[3] == 2 else b
    if kind == "az":
        return a / 2 if msg[3] == 4 else a
    if kind == "ay":
        return a / 2 if msg[2] == 2 else a
    if kind == "bz":
        return b / 2 if msg[2] == 4 else b
    if kind == "by":
        return b / 2 if msg[3] == 2 else b
    if kind == "Ry":
        return 16 if msg[2] == 2 else 32
    if kind == "Rz":
        return 16 if msg[2] == 4 else 32
    if kind == "RZ":
        return 64 if msg[2] == 4 else 128
    if kind == "RY":
        return 128 if msg[2] == 2 else 256
    return {"qx": 80, "vx": 560, "hx": 80, "hl": 160, "hc": 320, "xa": a, "xb": b}.get(kind, 8)


def build():
    tasks = {}

    def task(name, needs=(), after=(), cost=0.0, sends=()):
        needs, sends = list(needs), list(sends)
        tasks[name] = (needs, list(after), cost + 0.05 * len(needs) + 0.1 * len(sends), sends)

    first = []
    for s in SIGNS:
        first += [("Bz", s, 1), ("Ay", s, 1)]
    for s in SIGNS:
        first += [("Az", 0, s, 1), ("By", 0, s, 1)]
    task(
        ("start",),
        cost=0.5,
        sends=[("qx",)] + [m + ("o",) for m in first]
        + [("Rz", s, 1) for s in SIGNS] + [("Ry", s, 1) for s in SIGNS],
    )
    task(("qx",), [("qx",)], [("start",)], sends=[m + ("t",) for m in first])
    for s in SIGNS:
        task(
            ("Ay", s),
            [("Ay", s, 1, "o"), ("Ay", s, 1, "t")],
            [("qx",)],
            sends=[("Ay", s, 2, "f")] + [("Az", wrap(-s, NY), u, 1, "f") for u in SIGNS],
        )
    task(
        ("Ay2",),
        [("Ay", s, 2, "f") for s in SIGNS],
        [("Ay", s) for s in SIGNS],
        sends=[("Az", 2, u, 1, "f") for u in SIGNS],
    )
    for dy in (0, 1, -1, 2):
        for s in SIGNS:
            for h in (1, 2, 3):
                task(
                    ("Az", dy, s, h),
                    [("Az", dy, s, h, p) for p in parts_of("Az", h, dy == 0)],
                    sends=[("Az", dy, s, h + 1, "f")],
                )
    for s in SIGNS:
        for h in (1, 2, 3):
            task(
                ("Bz", s, h),
                [("Bz", s, h, p) for p in parts_of("Bz", h, True)],
                sends=[("Bz", s, h + 1, "f")] + [("By", wrap(-s * h, NZ), u, 1, "f") for u in SIGNS],
            )
    task(
        ("Bz4",), [("Bz", s, 4, "f") for s in SIGNS], sends=[("By", 4, u, 1, "f") for u in SIGNS]
    )
    for dz in range(-3, 5):
        for s in SIGNS:
            task(
                ("By", dz, s),
                [("By", dz, s, 1, p) for p in parts_of("By", 1, dz == 0)],
                sends=[("By", dz, s, 2, "f")],
            )
    late = [("Az", dy, s, 3) for dy in (0, 1, -1, 2) for s in SIGNS]
    late += [("By", dz, s) for dz in range(-3, 5) for s in SIGNS]
    for s in SIGNS:
        task(("Ry", s), [("Ry", s, 1)], sends=[("Ry", s, 2)])
        for h in (1, 2, 3):
            task(("Rz", s, h), [("Rz", s, h)], sends=[("Rz", s, h + 1)])
            task(("RZ", s, h), [("RZ", s, h)], sends=[("RZ", s, h + 1)])
        task(("RY", s), [("RY", s, 1)], sends=[("RY", s, 2)])
    task(
        ("RZ0",),
        [("Ry", s, 2) for s in SIGNS],
        [("Ry", s) for s in SIGNS] + late,
        sends=[("RZ", s, 1) for s in SIGNS],
    )
    task(
        ("RY0",),
        [("Rz", s, 4) for s in SIGNS],
        [("Rz", s, h) for s in SIGNS for h in (1, 2, 3)] + late,
        sends=[("RY", s, 1) for s in SIGNS],
    )
    task(("vx",), after=[("qx",)], cost=0.6, sends=[("vx",)])
    task(("hx",), after=[("qx",)], cost=1.0, sends=[("hx",)])
    task(("hl",), [("hx",)], [("hx",)], sends=[("hl",)])
    task(("hc",), [("hl",)], [("hl",)], sends=[("hc",)])
    task(("gram",), after=[("qx",)], cost=2.0)
    for g, planes in enumerate(PLANES):
        needs, after = [], [("m1", g - 1)] if g else [("load",)]
        for dz in planes:
            for s in SIGNS:
                needs.append(("By", dz, s, 2, "f"))
                after.append(("By", dz, s))
            if dz == 0:
                after += [("Ay", s) for s in SIGNS] + [("Ay2",)]
            elif dz == 4:
                needs += [("Az", dy, s, 4, "f") for dy in (0, 1, -1, 2) for s in SIGNS]
                after.append(("Bz4",))
            else:
                s = -1 if dz > 0 else 1
                after += [("Az", dy, s, abs(dz)) for dy in (0, 1, -1, 2)] + [("Bz", s, abs(dz))]
        task(("m1", g), needs, after, cost=1.1 * len(planes))
    task(("load",), after=[("start",)], cost=0.1)
    task(("img",), after=[("m1", len(PLANES) - 1)], cost=0.5)
    for n, dz in enumerate(ORDER):
        task(("m2", dz), after=[("img",)] + ([("m2", ORDER[n - 1])] if n else []), cost=0.95)
    for dy in (0, 1, -1, 2):
        task(("az", dy, 4), after=[("m2", 4)], cost=0.1, sends=[("az", dy, s, 4) for s in SIGNS])
        for s in SIGNS:
            for d in (3, 2, 1):
                task(
                    ("az", dy, s, d),
                    [("az", dy, s, d + 1)],
                    [("m2", s * d)],
                    cost=0.1,
                    sends=[("az", dy, s, d)],
                )
        task(("az", dy, 0), [("az", dy, s, 1) for s in SIGNS], [("m2", 0)], cost=0.15)
    task(("ay", 2), after=[("az", 2, 0)], cost=0.1, sends=[("ay", s, 2) for s in SIGNS])
    for s in SIGNS:
        task(("ay", s, 1), [("ay", s, 2)], [("az", s, 0)], cost=0.1, sends=[("ay", s, 1)])
    task(
        ("xa",), [("ay", s, 1) for s in SIGNS], [("az", 0, 0)], cost=0.15, sends=[("xa",)]
    )
    for dz in range(-3, 5):
        task(("by", dz, 2), after=[("m2", dz)], cost=0.1, sends=[("by", dz, s, 2) for s in SIGNS])
        for s in SIGNS:
            task(
                ("by", dz, s, 1),
                [("by", dz, s, 2)],
                [("m2", dz)],
                cost=0.15,
                sends=[("by", dz, s, 1)],
            )
        task(("by", dz, 0), [("by", dz, s, 1) for s in SIGNS], [("m2", dz)], cost=0.2)
    task(("bz", 4), after=[("by", 4, 0)], cost=0.1, sends=[("bz", s, 4) for s in SIGNS])
    for s in SIGNS:
        for d in (3, 2, 1):
            task(
                ("bz", s, d),
                [("bz", s, d + 1)],
                [("by", s * d, 0)],
                cost=0.15,
                sends=[("bz", s, d)],
            )
    task(("xb",), [("bz", s, 1) for s in SIGNS], [("by", 0, 0)], cost=0.2, sends=[("xb",)])
    for k in range(4):
        needs, after = [], [("m2", ORDER[-1])]
        if k == 0:
            needs += [("RZ", s, 4) for s in SIGNS] + [("RY", s, 2) for s in SIGNS]
            needs += [("hc",), ("vx",)]
            after += [("RZ", s, h) for s in SIGNS for h in (1, 2, 3)] + [("RY", s) for s in SIGNS]
            after += [("RZ0",), ("RY0",), ("hc",), ("vx",), ("gram",)]
        else:
            after += [("p8", k - 1)]
        task(("p8", k), needs, after, cost=1.3)
    task(("g1",), after=[("p8", 3)], cost=0.1, sends=[("g1z", k) for k in range(1, NZ)])
    task(
        ("g2",), [("g1z", k) for k in range(1, NZ)], [("g1",)], 0.1, [("g1y", k) for k in range(1, NY)]
    )
    task(
        ("g3",), [("g1y", k) for k in range(1, NY)], [("g2",)], 0.1, [("g1x", k) for k in range(1, 8)]
    )
    return tasks


PLANES = ((0,), (1, -1), (2, -2), (3, -3), (4,))
ORDER = (4, 3, -3, 2, -2, 1, -1, 0)


def schedule(tasks):
    rate = {"z": 46.0, "y": 46.0, "x": 45.0, "c": 400.0}
    delay = {"z": 1.5, "y": 1.5, "x": 2.0, "c": 0.8}
    waits = {}
    followers = {name: [] for name in tasks}
    for name, (needs, after, _, _) in tasks.items():
        for msg in needs:
            waits.setdefault(msg, []).append(name)
        for other in after:
            followers[other].append(name)

    def cost_of(msg):
        axis = link_of(msg)[0]
        return kilobytes(msg) / rate.get(axis, 40.0) + delay.get(axis, 3.0)

    @functools.cache
    def rank(name):
        _, _, cost, sends = tasks[name]
        rest = [rank(f) for f in followers[name]]
        rest += [cost_of(m) + max([rank(w) for w in waits.get(m, ())], default=0) for m in sends]
        return cost + max(rest, default=0)

    now, free, arrives, done, order = 0.0, {}, {}, {}, []
    left = dict(tasks)
    while left:
        ready, soonest = [], None
        for name, (needs, after, _, _) in left.items():
            if any(a not in done for a in after) or any(m not in arrives for m in needs):
                continue
            at = max([arrives[m] for m in needs], default=0.0)
            if at <= now:
                ready.append((-rank(name), at, name))
            else:
                soonest = at if soonest is None else min(soonest, at)
        if not ready:
            now = soonest
            continue
        name = min(ready, key=lambda r: (r[0], r[1]))[2]
        _, _, cost, sends = left.pop(name)
        now += cost
        done[name] = now
        order.append(name)
        for msg in sends:
            link = link_of(msg)
            axis = link[0]
            begin = max(now, free.get(link, 0.0))
            free[link] = begin + kilobytes(msg) / rate.get(axis, 40.0)
            arrives[msg] = free[link] + delay.get(axis, 3.0)
    return order, done, arrives


def product(a, b, ca, cb):
    return lax.dot_general(a, b, (((ca,), (cb,)), ((), ())), preferred_element_type=F32)


def kernel(
    order, tasks, index,
    x_hbm, hid_ref, res_ref, basis_ref,
    new_ref, hess_ref, proj_ref,
    xv, q, p, send_a, send_b, recv_a, recv_b, acc, img, r, v16, ht, hs, cur,
    early, late, gz, gy, gx, square, load_sem, send_sem, recv_sem,
):
    dp, fs = lax.axis_index("dp"), lax.axis_index("fsdp")
    z, y, xh = fs // 8, lax.rem(fs // 2, 4), lax.rem(fs, 2)
    xl, core = dp // 2, lax.rem(dp, 2)
    other = 1 - xh

    zi = {d: lax.rem(z + (d + NZ), NZ) for d in range(-3, 8)}
    zi[-4] = zi[4]
    yi = {d: lax.rem(y + (d + NY), NY) for d in range(-1, 4)}
    yi[-2] = yi[2]

    def fsdp(za, ya, xa):
        return (za * NY + ya) * 2 + xa

    def along_z(d):
        return (dp, fsdp(zi[d], y, xh))

    def along_y(d):
        return (dp, fsdp(z, yi[d], xh))

    def along_x(k):
        xa = 1 - xh if k & 4 else xh
        la = 1 - xl if k & 2 else xl
        ca = 1 - core if k & 1 else core
        return (la * 2 + ca, fsdp(z, y, xa))

    partners = [along_z(d) for d in range(1, NZ)] + [along_y(d) for d in range(1, NY)]
    partners += [along_x(k) for k in range(1, 8)]

    loading = pltpu.make_async_copy(x_hbm, xv, load_sem)
    loading.start()
    barrier = pltpu.get_barrier_semaphore()
    for device in partners:
        pl.semaphore_signal(barrier, inc=1, device_id=device, device_id_type=MESH)

    def q_part(rows, part, oz, oy):
        at = q.at[zi[oz], yi[oy]]
        which = {"f": slice(None), "o": xh, "t": other}.get(part, part)
        return at.at[which, rows]

    a_rows, b_rows = pl.ds(0, ROWS_A), pl.ds(ROWS_A, ROWS_B)

    def slot_a(msg):
        if msg[0] == "az":
            _, dy, s, d = msg
            base = {0: 0, 1: 7, -1: 14, 2: 21}[dy]
            return base + (6 if d == 4 else (d - 1) * 2 + half_of(s)), d == 4, s
        if msg[0] == "ay":
            _, s, d = msg
            return 28 + (2 if d == 2 else half_of(s)), d == 2, s
        return 31, False, 1

    def slot_b(msg):
        if msg[0] == "by":
            _, dz, s, d = msg
            return (dz + 3) * 3 + (2 if d == 2 else half_of(s)), d == 2, s
        if msg[0] == "bz":
            _, s, d = msg
            return 24 + (6 if d == 4 else (d - 1) * 2 + half_of(s)), d == 4, s
        return 31, False, 1

    def piece(buf, slot):
        n, halved, s = slot
        return buf.at[n, half_of(s)] if halved else buf.at[n]

    def place(msg):
        kind = msg[0]
        if kind == "qx":
            here = q.at[z, y, xh]
            return here, here, q.at[z, y, other], along_x(4)
        if kind in ("Ay", "Az", "Bz", "By"):
            rows = a_rows if kind[0] == "A" else b_rows
            if kind in ("Ay", "Bz"):
                _, s, h, part = msg
            else:
                _, off, s, h, part = msg
            size = NZ if kind[1] == "z" else NY
            if h == size // 2:
                part = half_of(s)
            if kind[1] == "y":
                oz = off if kind == "By" else 0
                here = q_part(rows, part, oz, wrap(-s * (h - 1), NY))
                there = q_part(rows, part, oz, wrap(-s * h, NY))
                return here, here, there, along_y(s)
            oy = off if kind == "Az" else 0
            here = q_part(rows, part, wrap(-s * (h - 1), NZ), oy)
            there = q_part(rows, part, wrap(-s * h, NZ), oy)
            return here, here, there, along_z(s)
        if kind in ("Ry", "RZ", "Rz", "RY"):
            _, s, h = msg
            last = h == (NY if kind[1] in "yY" else NZ) // 2
            low = 0 if kind in ("Ry", "RZ") else 32
            rows = pl.ds(low + 16 * half_of(s), 16) if last else pl.ds(low, 32)
            n = NY if kind[1] in "yY" else NZ
            a, b = wrap(-s * (h - 1), n), wrap(-s * h, n)
            if kind == "Ry":
                here, there = r.at[z, yi[a], rows], r.at[z, yi[b], rows]
            elif kind == "Rz":
                here, there = r.at[zi[a], y, rows], r.at[zi[b], y, rows]
            elif kind == "RZ":
                here, there = r.at[zi[a], :, rows], r.at[zi[b], :, rows]
            else:
                here, there = r.at[:, yi[a], rows], r.at[:, yi[b], rows]
            return here, here, there, along_y(s) if n == NY else along_z(s)
        if kind == "vx":
            here = v16.at[pl.ds(0, K - 1), xh]
            return here, here, v16.at[pl.ds(0, K - 1), other], along_x(4)
        if kind == "hx":
            return hs, ht.at[xl, core, xh], ht.at[xl, core, other], along_x(4)
        if kind == "hl":
            here = ht.at[xl, core]
            return here, here, ht.at[1 - xl, core], along_x(2)
        if kind == "hc":
            here = ht.at[:, core]
            return here, here, ht.at[:, 1 - core], along_x(1)
        if kind in ("az", "ay", "xa"):
            slot = slot_a(msg)
            target = piece(recv_a, slot)
            src = piece(send_a, slot)
        elif kind in ("by", "bz", "xb"):
            slot = slot_b(msg)
            target = piece(recv_b, slot)
            src = piece(send_b, slot)
        if kind in ("xa", "xb"):
            return src, target, target, along_x(4)
        if kind in ("az", "by"):
            return src, target, target, along_z(msg[2]) if kind == "az" else along_y(msg[2])
        if kind in ("ay", "bz"):
            return src, target, target, along_y(msg[1]) if kind == "ay" else along_z(msg[1])
        lane, k = int(kind[1]) - 1, msg[1]
        if kind[2] == "z":
            return gz.at[lane, z], gz.at[lane, z], gz.at[lane, zi[-k + NZ if k > 3 else -k]], along_z(k)
        if kind[2] == "y":
            return gy.at[lane, y], gy.at[lane, y], gy.at[lane, yi[-k + NY if k > 1 else -k]], along_y(k)
        mine = xh * 4 + xl * 2 + core
        xa = 1 - xh if k & 4 else xh
        la = 1 - xl if k & 2 else xl
        ca = 1 - core if k & 1 else core
        return gx.at[lane, mine], gx.at[lane, mine], gx.at[lane, xa * 4 + la * 2 + ca], along_x(k)

    started = []

    def send(msg):
        src, target, _, device = place(msg)
        n = index[msg]
        copy = pltpu.make_async_remote_copy(
            src_ref=src, dst_ref=target, send_sem=send_sem.at[n], recv_sem=recv_sem.at[n],
            device_id=device, device_id_type=MESH,
        )
        copy.start()
        started.append(copy)

    def receive(msg):
        _, _, lands, device = place(msg)
        n = index[msg]
        pltpu.make_async_remote_copy(
            src_ref=lands, dst_ref=lands, send_sem=send_sem.at[n], recv_sem=recv_sem.at[n],
            device_id=device, device_id_type=MESH,
        ).wait_recv()

    def fold(rows, buf, where, slots, out):
        for k in (0, 1):
            total = p[where[0], where[1], k, rows]
            for n, halved, s in slots:
                if not halved or half_of(s) == k:
                    total = total + buf[n, k].astype(F32)
            if out is None:
                p[where[0], where[1], k, rows] = total
            else:
                out[0][out[1], k] = total.astype(BF)

    def fold_a(where, msgs, out=None):
        fold(a_rows, recv_a, where, [slot_a(m) for m in msgs], out and (send_a, slot_a(out)[0]))

    def fold_b(where, msgs, out=None):
        fold(b_rows, recv_b, where, [slot_b(m) for m in msgs], out and (send_b, slot_b(out)[0]))

    def lanes_of(plane):
        return pl.ds(pl.multiple_of(plane * (NY * 2 * BLK), 128), NY * 2 * BLK)

    def per_token(rows, k):
        errors = r[2 * k : 2 * k + 2].reshape(512, WID)
        hidden = ht[k // 2, k % 2].reshape(2 * BLK, 512).astype(F32)
        mapped = product(rows, errors, 1, 1)
        n = rows.shape[0] // (2 * BLK)
        return jnp.sum(mapped.reshape(n, 2 * BLK, 512) * hidden[None], axis=1)

    def per_example(tokens, k):
        t = lax.broadcasted_iota(jnp.int32, (512, 128), 0)
        e = lax.broadcasted_iota(jnp.int32, (512, 128), 1)
        owner = 32 * k + (t // 64) * 4 + 2 * xh + lax.rem(t, 64) // EX_TOK
        marks = jnp.where(owner == e, 1.0, 0.0).astype(F32)
        return jnp.dot(tokens, marks, precision=lax.Precision.HIGHEST, preferred_element_type=F32)

    def work(name):
        kind = name[0]
        if kind == "start":
            narrow = basis_ref[K - 1].astype(BF)
            q[z, y, xh] = narrow
            v16[K - 1, xh] = narrow
            r[z, y] = res_ref[...]
            pl.semaphore_wait(barrier, len(partners))
        elif kind == "vx":
            for n in range(K - 1):
                v16[n, xh] = basis_ref[n].astype(BF)
            v16[K - 1, other] = q[z, y, other]
        elif kind == "hx":
            eye_a = lax.broadcasted_iota(jnp.int32, (BLK, BLK), 0)
            eye_b = lax.broadcasted_iota(jnp.int32, (BLK, BLK), 1)
            eye = jnp.where(eye_a == eye_b, 1.0, 0.0).astype(BF)

            def turned(which):
                rows = [hid_ref[pl.ds(pl.multiple_of((2 * n + which) * 64, 64), 64), :] for n in range(8)]
                return product(eye, jnp.concatenate(rows, axis=0), 1, 1).astype(BF)

            ht[xl, core, xh] = turned(xh)
            hs[...] = turned(other)
        elif kind == "gram":
            lane = lax.broadcasted_iota(jnp.int32, (8, 128), 1)
            table = jnp.zeros((8, 128), F32)
            for i in range(K):
                rows = [jnp.sum(basis_ref[j] * basis_ref[i], axis=0, keepdims=True) for j in range(K)]
                column = jnp.sum(jnp.concatenate(rows, axis=0), axis=1, keepdims=True)
                table = table + jnp.where(lane == i, column, 0.0)
            early[8:16] = table
            early[0:8] = jnp.zeros((8, 128), F32)
        elif kind == "load":
            loading.wait()
        elif kind == "m1":
            total = None
            for dz in PLANES[name[1]]:
                term = product(xv[:, lanes_of(zi[dz])], q[zi[dz]].reshape(NY * 2 * BLK, WID), 1, 0)
                total = term if total is None else total + term
            acc[...] = total if name[1] == 0 else acc[...] + total
        elif kind == "img":
            img[...] = acc[...].astype(BF)
        elif kind == "m2":
            plane = zi[name[1]]
            p[plane] = product(xv[:, lanes_of(plane)], img[...], 0, 0).reshape(NY, 2, BLK, WID)
        elif kind == "az":
            dy = name[1]
            if name[2] == 4:
                fold_a((zi[4], yi[dy]), [], ("az", dy, 1, 4))
            elif name[2] == 0:
                fold_a((z, yi[dy]), [("az", dy, s, 1) for s in SIGNS])
            else:
                s, d = name[2:]
                fold_a((zi[s * d], yi[dy]), [("az", dy, s, d + 1)], ("az", dy, s, d))
        elif kind == "ay":
            if name[1] == 2 and len(name) == 2:
                fold_a((z, yi[2]), [], ("ay", 1, 2))
            else:
                s = name[1]
                fold_a((z, yi[s]), [("ay", s, 2)], ("ay", s, 1))
        elif kind == "xa":
            fold_a((z, y), [("ay", s, 1) for s in SIGNS])
            fold_a((z, y), [], ("xa",))
        elif kind == "by":
            dz = name[1]
            if len(name) == 4:
                s = name[2]
                fold_b((zi[dz], yi[s]), [("by", dz, s, 2)], ("by", dz, s, 1))
            elif name[2] == 2:
                fold_b((zi[dz], yi[2]), [], ("by", dz, 1, 2))
            else:
                fold_b((zi[dz], y), [("by", dz, s, 1) for s in SIGNS])
        elif kind == "bz":
            if len(name) == 2:
                fold_b((zi[4], y), [], ("bz", 1, 4))
            else:
                s, d = name[1:]
                fold_b((zi[s * d], y), [("bz", s, d + 1)], ("bz", s, d))
        elif kind == "xb":
            fold_b((z, y), [("bz", s, 1) for s in SIGNS])
            fold_b((z, y), [], ("xb",))
        elif kind == "p8":
            k = name[1]
            early[0:8] = early[0:8] + per_example(per_token(v16[...].reshape(K * 2 * BLK, WID), k), k)
        elif kind == "g1":
            gz[0, z] = early[...]
        elif kind == "g2":
            gy[0, y] = ring_sum(gz, 0, NZ)
        elif kind == "g3":
            gx[0, xh * 4 + xl * 2 + core] = ring_sum(gy, 0, NY)

    def ring_sum(buf, lane, n):
        total = buf[lane, 0]
        for k in range(1, n):
            total = total + buf[lane, k]
        return total

    for name in order:
        needs, _, _, sends = tasks[name]
        if name[0] != "start":
            for msg in needs:
                receive(msg)
        work(name)
        for msg in sends:
            send(msg)

    receive(("xa",))
    receive(("xb",))
    mean = 1.0 / (FF * D)
    for k in (0, 1):
        cur[k, a_rows] = (p[z, y, k, a_rows] + recv_a[31, k].astype(F32)) * (1.0 / TOKENS)
        cur[k, b_rows] = (p[z, y, k, b_rows] + recv_b[31, k].astype(F32)) * (1.0 / TOKENS)
    mine = cur[xh]
    rows = [jnp.sum(basis_ref[n] * mine, axis=0, keepdims=True) for n in range(K)]
    rows.append(jnp.sum(mine * mine, axis=0, keepdims=True))
    rows.append(jnp.zeros((7, WID), F32))
    sums = jnp.sum(jnp.concatenate(rows, axis=0), axis=1, keepdims=True)
    late[...] = jnp.broadcast_to(sums, (16, 128))
    both = cur[...].reshape(2 * BLK, WID)
    high = both.astype(BF)
    low = (both - high.astype(F32)).astype(BF)
    pair = jnp.concatenate([high, low], axis=0)
    shown = jnp.zeros((1, 128), F32)
    for k in range(4):
        tokens = per_token(pair, k)
        tokens = tokens[0:1] + tokens[1:2]
        shown = shown + per_example(jnp.broadcast_to(tokens, (8, 512)), k)[0:1]
    late[9:10] = shown

    gz[1, z] = late[...]
    for k in range(1, NZ):
        send(("g2z", k))
    for k in range(1, 8):
        receive(("g1x", k))
    first = ring_sum(gx, 0, 8)
    for k in range(1, NZ):
        receive(("g2z", k))
    gy[1, y] = ring_sum(gz, 1, NZ)
    for k in range(1, NY):
        send(("g2y", k))
    for k in range(1, NY):
        receive(("g2y", k))
    gx[1, xh * 4 + xl * 2 + core] = ring_sum(gy, 1, NY)
    for k in range(1, 8):
        send(("g2x", k))
    for k in range(1, 8):
        receive(("g2x", k))
    second = ring_sum(gx, 1, 8)

    coeff = second[0:8] * mean
    squared = second[8:9] * mean
    sub = lax.broadcasted_iota(jnp.int32, (8, 128), 0)
    lane = lax.broadcasted_iota(jnp.int32, (8, 128), 1)
    row = jnp.sum(jnp.where(sub == lane, coeff, 0.0), axis=0, keepdims=True)
    cross = jnp.sum(coeff * first[8:16], axis=0, keepdims=True) * row
    cross = jnp.sum(cross, axis=1, keepdims=True) * mean
    twice = 2.0 * jnp.sum(coeff * coeff, axis=0, keepdims=True)
    beta = jnp.sqrt(jnp.maximum(squared - twice + cross, squared * 1e-12))
    inverse = 1.0 / beta
    lane1 = lax.broadcasted_iota(jnp.int32, (1, 128), 1)
    hess_ref[...] = jnp.where(lane1 == K, beta, row)[:, 0 : K + 1]
    left = mine
    for n in range(K):
        left = left - coeff[n : n + 1, 0:1] * basis_ref[n]
    new_ref[0] = left * inverse[:, 0:1]
    last = (second[9:10] - jnp.sum(coeff * first[0:8], axis=0, keepdims=True)) * inverse
    scale = (FF * D) ** (-0.5)
    square[...] = jnp.zeros((128, 128), F32)
    square[0:8] = first[0:8] * scale
    square[8:9] = last * scale
    square[...] = square[...].T
    proj_ref[...] = square[pl.ds(pl.multiple_of(dp * 32, 32), 32), 0 : K + 1]
    for copy in started:
        copy.wait_send()


def local(train_hidden, index_hidden, index_resid, basis):
    tasks = build()
    order, _, _ = schedule(tasks)
    messages = [m for name in tasks for m in tasks[name][3]]
    messages += [("g2z", k) for k in range(1, NZ)] + [("g2y", k) for k in range(1, NY)]
    messages += [("g2x", k) for k in range(1, 8)]
    index = {m: n for n, m in enumerate(messages)}
    vmem = pltpu.VMEM
    whole = pl.BlockSpec(memory_space=pltpu.VMEM)
    call = pl.pallas_call(
        functools.partial(kernel, order, tasks, index),
        out_shape=(
            jax.ShapeDtypeStruct((1, BLK, WID), F32),
            jax.ShapeDtypeStruct((1, K + 1), F32),
            jax.ShapeDtypeStruct((32, K + 1), F32),
        ),
        in_specs=[pl.BlockSpec(memory_space=pl.ANY), whole, whole, whole],
        out_specs=(whole, whole, whole),
        scratch_shapes=[
            vmem((1024, FF), BF),
            vmem((NZ, NY, 2, BLK, WID), BF),
            vmem((NZ, NY, 2, BLK, WID), F32),
            vmem((32, 2, ROWS_A, WID), BF),
            vmem((32, 2, ROWS_B, WID), BF),
            vmem((32, 2, ROWS_A, WID), BF),
            vmem((32, 2, ROWS_B, WID), BF),
            vmem((1024, WID), F32),
            vmem((1024, WID), BF),
            vmem((NZ, NY, 64, WID), BF),
            vmem((K, 2, BLK, WID), BF),
            vmem((2, 2, 2, BLK, WID), BF),
            vmem((BLK, WID), BF),
            vmem((2, BLK, WID), F32),
            vmem((16, 128), F32),
            vmem((16, 128), F32),
            vmem((2, NZ, 16, 128), F32),
            vmem((2, NY, 16, 128), F32),
            vmem((2, 8, 16, 128), F32),
            vmem((128, 128), F32),
            pltpu.SemaphoreType.DMA,
            pltpu.SemaphoreType.DMA((len(messages),)),
            pltpu.SemaphoreType.DMA((len(messages),)),
        ],
        compiler_params=pltpu.CompilerParams(
            collective_id=0, has_side_effects=True, vmem_limit_bytes=60 * 2**20
        ),
        cost_estimate=pl.CostEstimate(
            flops=14 * 10**9, bytes_accessed=13 * 10**6, transcendentals=0
        ),
        name="arnoldi",
    )
    return call(train_hidden, index_hidden, index_resid, basis)


def solution(mesh):
    in_specs = (P("fsdp", None), P("dp", "fsdp"), P("fsdp", "dp"), P(None, "fsdp", "dp"))
    out_specs = (P(None, "fsdp", "dp"), P(), P("dp", None))
    return jax.shard_map(local, mesh=mesh, in_specs=in_specs, out_specs=out_specs, check_vma=False)
```

```python
import functools

import jax
import jax.numpy as jnp
from jax import lax
from jax.experimental import pallas as pl
from jax.experimental.pallas import tpu as pltpu
from jax.sharding import PartitionSpec as P

D = 2048
FF = 5120
TOKENS = 65536
EX_TOK = 32
K = 8
NZ, NY = 8, 4
BLK = 80
WID = 512
ROWS_A, ROWS_B, ROWS_C = 32, 32, 16
MESH = pl.DeviceIdType.MESH
BF = jnp.bfloat16
F32 = jnp.float32
SIGNS = (1, -1)
FAR = (4, 3, 5, 2, 6, 1, 7)
WIDE = sorted(
    range(1, 32), key=lambda k: -(min(k // 8, 4 - k // 8) + (0, 1, 2, 1)[(k >> 1) & 3]) * 2 - (k & 1)
)


def half_of(sign):
    return 0 if sign > 0 else 1


def wrap(delta, size):
    delta %= size
    return delta - size if delta > size // 2 else delta


def parts_of(kind, hop, own):
    if hop == 1 and own:
        return ("o", "t")
    return ("f",)


def link_of(msg):
    kind = msg[0]
    if kind in ("Az", "az"):
        return ("z", msg[2])
    if kind in ("Ay", "ay", "Ry", "RY", "Cy"):
        return ("y", msg[1])
    if kind in ("Bz", "bz", "Rz", "RZ", "Cz", "cz"):
        return ("z", msg[1])
    if kind in ("By", "by", "cy"):
        return ("y", msg[2])
    if kind in ("qx", "vx", "hx", "xa", "xb", "xc", "hl", "Cx", "cx"):
        return ("x", 0)
    return ("c", 0) if kind == "hc" else (kind, msg[1])


def kilobytes(msg):
    kind = msg[0]
    a, b = 2 * ROWS_A, 2 * ROWS_B
    if kind == "Ay":
        return a / 2 if msg[3] in ("o", "t") or msg[2] == 2 else a
    if kind == "Az":
        return a / 2 if msg[4] in ("o", "t") or msg[3] == 4 else a
    if kind == "Bz":
        return b / 2 if msg[3] in ("o", "t") or msg[2] == 4 else b
    if kind == "By":
        return b / 2 if msg[4] in ("o", "t") or msg[3] == 2 else b
    if kind == "az":
        return a / 2 if msg[3] == 4 else a
    if kind == "ay":
        return a / 2 if msg[2] == 2 else a
    if kind == "bz":
        return b / 2 if msg[2] == 4 else b
    if kind == "by":
        return b / 2 if msg[3] == 2 else b
    if kind in ("Ry", "Rz", "RZ", "RY", "Cz", "Cy"):
        full = {"Ry": 16, "Rz": 48, "RZ": 64, "RY": 384, "Cz": ROWS_C, "Cy": 8 * ROWS_C}[kind]
        return full / 2 if msg[2] == (4 if kind[1] in "zZ" else 2) else full
    if kind == "cz":
        return ROWS_C / 2 if msg[2] == 4 else ROWS_C
    if kind == "cy":
        return 2 * ROWS_C if msg[3] == 2 else 4 * ROWS_C
    if kind in ("Cx", "cx"):
        return (8 if kind == "Cx" else 4) * ROWS_C
    return {"qx": 64, "xc": ROWS_C, "vx": 560, "hx": 80, "hl": 160, "hc": 320, "xa": a, "xb": b}.get(kind, 8)


def build():
    tasks = {}

    def task(name, needs=(), after=(), cost=0.0, sends=()):
        needs, sends = list(needs), list(sends)
        tasks[name] = (needs, list(after), cost + 0.01 * (len(needs) + len(sends)), sends)

    first = []
    for s in SIGNS:
        first += [("Bz", s, 1), ("Ay", s, 1)]
    for s in SIGNS:
        first += [("Az", 0, s, 1), ("By", 0, s, 1)]
    task(
        ("start",),
        cost=0.5,
        sends=[("qx",)] + [("Cz", s, 1) for s in SIGNS] + [m + ("o",) for m in first]
        + [("Rz", s, 1) for s in SIGNS] + [("Ry", s, 1) for s in SIGNS],
    )
    task(("qx",), [("qx",)], [("start",)], sends=[m + ("t",) for m in first])
    for s in SIGNS:
        task(
            ("Ay", s),
            [("Ay", s, 1, "o"), ("Ay", s, 1, "t")],
            [("qx",)],
            sends=[("Ay", s, 2, "f")] + [("Az", wrap(-s, NY), u, 1, "f") for u in SIGNS],
        )
    task(
        ("Ay2",),
        [("Ay", s, 2, "f") for s in SIGNS],
        [("Ay", s) for s in SIGNS],
        sends=[("Az", 2, u, 1, "f") for u in SIGNS],
    )
    for dy in (0, 1, -1, 2):
        for s in SIGNS:
            for h in (1, 2, 3):
                task(
                    ("Az", dy, s, h),
                    [("Az", dy, s, h, p) for p in parts_of("Az", h, dy == 0)],
                    sends=[("Az", dy, s, h + 1, "f")],
                )
    for s in SIGNS:
        for h in (1, 2, 3):
            task(
                ("Bz", s, h),
                [("Bz", s, h, p) for p in parts_of("Bz", h, True)],
                sends=[("Bz", s, h + 1, "f")] + [("By", wrap(-s * h, NZ), u, 1, "f") for u in SIGNS],
            )
    task(
        ("Bz4",), [("Bz", s, 4, "f") for s in SIGNS], sends=[("By", 4, u, 1, "f") for u in SIGNS]
    )
    for dz in range(-3, 5):
        for s in SIGNS:
            task(
                ("By", dz, s),
                [("By", dz, s, 1, p) for p in parts_of("By", 1, dz == 0)],
                sends=[("By", dz, s, 2, "f")],
            )
    for s in SIGNS:
        for h in (1, 2, 3):
            task(("Cz", s, h), [("Cz", s, h)], sends=[("Cz", s, h + 1)])
        task(("Cy", s), [("Cy", s, 1)], sends=[("Cx", wrap(-s, NY)), ("Cy", s, 2)])
    task(
        ("CY0",),
        [("Cz", s, 4) for s in SIGNS],
        [("Cz", s, h) for s in SIGNS for h in (1, 2, 3)],
        sends=[("Cx", 0)] + [("Cy", s, 1) for s in SIGNS],
    )
    task(("Cy2",), [("Cy", s, 2) for s in SIGNS], [("Cy", s) for s in SIGNS], sends=[("Cx", 2)])
    late = [("Az", dy, s, 3) for dy in (0, 1, -1, 2) for s in SIGNS]
    late += [("By", dz, s) for dz in range(-3, 5) for s in SIGNS]
    for s in SIGNS:
        task(("Ry", s), [("Ry", s, 1)], sends=[("Ry", s, 2)])
        for h in (1, 2, 3):
            task(("Rz", s, h), [("Rz", s, h)], sends=[("Rz", s, h + 1)])
            task(("RZ", s, h), [("RZ", s, h)], sends=[("RZ", s, h + 1)])
        task(("RY", s), [("RY", s, 1)], sends=[("RY", s, 2)])
    task(
        ("RZ0",),
        [("Ry", s, 2) for s in SIGNS],
        [("Ry", s) for s in SIGNS] + late,
        sends=[("RZ", s, 1) for s in SIGNS],
    )
    task(
        ("RY0",),
        [("Rz", s, 4) for s in SIGNS],
        [("Rz", s, h) for s in SIGNS for h in (1, 2, 3)] + late,
        sends=[("RY", s, 1) for s in SIGNS],
    )
    task(("vx",), after=[("qx",), ("Cy2",)], cost=0.1, sends=[("vx",)])
    task(("hx",), after=[("vx",)], sends=[("hx",)])
    task(("hl",), [("hx",)], [("hx",)], sends=[("hl",)])
    task(("hc",), [("hl",)], [("hl",)], sends=[("hc",)])
    task(("gram",), after=[("qx",)], cost=2.0)
    for g, planes in enumerate(PLANES):
        needs, after = [], [("m1", g - 1)] if g else [("load",), ("CY0",), ("Cy2",)]
        for dz in planes:
            for s in SIGNS:
                needs.append(("By", dz, s, 2, "f"))
                after.append(("By", dz, s))
            if dz == 0:
                after += [("Ay", s) for s in SIGNS] + [("Ay2",)]
            elif dz == 4:
                needs += [("Az", dy, s, 4, "f") for dy in (0, 1, -1, 2) for s in SIGNS]
                after.append(("Bz4",))
            else:
                s = -1 if dz > 0 else 1
                after += [("Az", dy, s, abs(dz)) for dy in (0, 1, -1, 2)] + [("Bz", s, abs(dz))]
        task(("m1", g), needs, after, cost=1.1 * len(planes))
    task(("load",), after=[("start",)], cost=0.1)
    for k in range(4):
        task(("xs", k), after=[("load",)] + ([("xs", k - 1)] if k else []), cost=0.7)
    task(
        ("m1c",),
        [("Cx", dy) for dy in (0, 1, -1, 2)],
        [("CY0",), ("Cy2",), ("m1", 0), ("xs", 3)],
        cost=0.9,
    )
    task(("img",), after=[("m1", len(PLANES) - 1), ("m1c",)], cost=0.5)
    for n, dz in enumerate(ORDER):
        task(("m2", dz), after=[("img",)] + ([("m2", ORDER[n - 1])] if n else []), cost=0.95)
    for dy in (0, 1, -1, 2):
        task(("az", dy, 4), after=[("m2", 4)], cost=0.04, sends=[("az", dy, s, 4) for s in SIGNS])
        for s in SIGNS:
            for d in (3, 2, 1):
                task(
                    ("az", dy, s, d),
                    [("az", dy, s, d + 1)],
                    [("m2", s * d)],
                    cost=0.04,
                    sends=[("az", dy, s, d)],
                )
        task(("az", dy, 0), [("az", dy, s, 1) for s in SIGNS], [("m2", 0)], cost=0.04)
    task(("ay", 2), after=[("az", 2, 0)], cost=0.04, sends=[("ay", s, 2) for s in SIGNS])
    for s in SIGNS:
        task(("ay", s, 1), [("ay", s, 2)], [("az", s, 0)], cost=0.04, sends=[("ay", s, 1)])
    task(
        ("xa",), [("ay", s, 1) for s in SIGNS], [("az", 0, 0)], cost=0.04, sends=[("xa",)]
    )
    for dz in range(-3, 5):
        task(("by", dz, 2), after=[("m2", dz)], cost=0.04, sends=[("by", dz, s, 2) for s in SIGNS])
        for s in SIGNS:
            task(
                ("by", dz, s, 1),
                [("by", dz, s, 2)],
                [("m2", dz)],
                cost=0.04,
                sends=[("by", dz, s, 1)],
            )
        task(("by", dz, 0), [("by", dz, s, 1) for s in SIGNS], [("m2", dz)], cost=0.06)
    task(("bz", 4), after=[("by", 4, 0)], cost=0.04, sends=[("bz", s, 4) for s in SIGNS])
    for s in SIGNS:
        for d in (3, 2, 1):
            task(
                ("bz", s, d),
                [("bz", s, d + 1)],
                [("by", s * d, 0)],
                cost=0.04,
                sends=[("bz", s, d)],
            )
    task(("xb",), [("bz", s, 1) for s in SIGNS], [("by", 0, 0)], cost=0.06, sends=[("xb",)])
    for n, dz in enumerate(ORDER):
        task(("cx", dz), after=[("m2", dz)], cost=0.04, sends=[("cx", dz)])
        task(("cs", dz), [("cx", dz)], [("m2", dz)], cost=0.04)
    for g in (0, 1):
        done = [("cs", dz) for dz in GROUPS[g]]
        task(("cy", g, 2), after=done, cost=0.04, sends=[("cy", g, s, 2) for s in SIGNS])
        for s in SIGNS:
            task(("cy", g, s, 1), [("cy", g, s, 2)], done, cost=0.04, sends=[("cy", g, s, 1)])
        task(("cy", g, 0), [("cy", g, s, 1) for s in SIGNS], done, cost=0.04)
    task(("cz", 4), after=[("cy", 0, 0)], cost=0.03, sends=[("cz", s, 4) for s in SIGNS])
    for s in SIGNS:
        for d in (3, 2, 1):
            task(
                ("cz", s, d),
                [("cz", s, d + 1)],
                [("cy", 0 if s * d in GROUPS[0] else 1, 0)],
                cost=0.03,
                sends=[("cz", s, d)],
            )
    task(("xc",), [("cz", s, 1) for s in SIGNS], [("cy", 1, 0)], cost=0.03, sends=[("xc",)])
    for k in range(4):
        needs, after = [], [("m2", ORDER[-1])]
        if k == 0:
            needs += [("RZ", s, 4) for s in SIGNS] + [("RY", s, 2) for s in SIGNS]
            needs += [("hc",), ("vx",)]
            after += [("RZ", s, h) for s in SIGNS for h in (1, 2, 3)] + [("RY", s) for s in SIGNS]
            after += [("RZ0",), ("RY0",), ("hc",), ("vx",), ("gram",)]
        else:
            after += [("p8", k - 1)]
        task(("p8", k), needs, after, cost=1.3)
    task(("g1",), after=[("p8", 3)], cost=0.1, sends=[("g1z", k) for k in FAR])
    task(
        ("g2",), [("g1z", k) for k in range(1, NZ)], [("g1",)], 0.1, [("g1y", k) for k in range(1, NY)]
    )
    task(
        ("g3",), [("g1y", k) for k in range(1, NY)], [("g2",)], 0.1, [("g1x", k) for k in range(1, 8)]
    )
    return tasks


PLANES = ((0,), (1, -1), (2, -2), (3, -3), (4,))
ORDER = (4, 3, -3, 2, -2, 1, -1, 0)
GROUPS = (ORDER[:4], ORDER[4:])


def schedule(tasks):
    rate = {"z": 46.0, "y": 46.0, "x": 45.0, "c": 400.0}
    delay = {"z": 1.5, "y": 1.5, "x": 2.0, "c": 0.8}
    waits = {}
    followers = {name: [] for name in tasks}
    for name, (needs, after, _, _) in tasks.items():
        for msg in needs:
            waits.setdefault(msg, []).append(name)
        for other in after:
            followers[other].append(name)

    def cost_of(msg):
        axis = link_of(msg)[0]
        return kilobytes(msg) / rate.get(axis, 40.0) + delay.get(axis, 3.0)

    @functools.cache
    def rank(name):
        _, _, cost, sends = tasks[name]
        rest = [rank(f) for f in followers[name]]
        rest += [cost_of(m) + max([rank(w) for w in waits.get(m, ())], default=0) for m in sends]
        return cost + max(rest, default=0)

    now, free, arrives, done, order = 0.0, {}, {}, {}, []
    left = dict(tasks)
    while left:
        ready, soonest = [], None
        for name, (needs, after, cost, sends) in left.items():
            if any(a not in done for a in after) or any(m not in arrives for m in needs):
                continue
            at = max([arrives[m] for m in needs], default=0.0)
            if at <= now:
                heavy = cost >= 0.3 and not sends
                ready.append((heavy, -rank(name), at, name))
            else:
                soonest = at if soonest is None else min(soonest, at)
        if not ready:
            now = soonest
            continue
        name = min(ready, key=lambda r: r[:3])[3]
        _, _, cost, sends = left.pop(name)
        now += cost
        done[name] = now
        order.append(name)
        for msg in sends:
            link = link_of(msg)
            axis = link[0]
            begin = max(now, free.get(link, 0.0))
            free[link] = begin + kilobytes(msg) / rate.get(axis, 40.0)
            arrives[msg] = free[link] + delay.get(axis, 3.0)
    return order, done, arrives


def product(a, b, ca, cb):
    return lax.dot_general(a, b, (((ca,), (cb,)), ((), ())), preferred_element_type=F32)


def kernel(
    order, tasks, index,
    x_hbm, hid_ref, res_ref, basis_ref,
    own_ref, first_ref, second_ref,
    xv, q, qc, xc, select, p, send_a, send_b, recv_a, recv_b,
    send_cx, recv_cx, send_cy, recv_cy, send_cz, recv_cz, acc, img, r, v16, ht, hs, cur,
    early, gz, gy, gx, hz, hw, load_sem, send_sem, recv_sem,
):
    dp, fs = lax.axis_index("dp"), lax.axis_index("fsdp")
    z, y, xh = fs // 8, lax.rem(fs // 2, 4), lax.rem(fs, 2)
    xl, core = dp // 2, lax.rem(dp, 2)
    other = 1 - xh

    zi = {d: lax.rem(z + (d + NZ), NZ) for d in range(-3, 8)}
    zi[-4] = zi[4]
    yi = {d: lax.rem(y + (d + NY), NY) for d in range(-1, 4)}
    yi[-2] = yi[2]

    def fsdp(za, ya, xa):
        return (za * NY + ya) * 2 + xa

    def along_z(d):
        return (dp, fsdp(zi[d], y, xh))

    def along_y(d):
        return (dp, fsdp(z, yi[d], xh))

    def along_x(k):
        xa = 1 - xh if k & 4 else xh
        la = 1 - xl if k & 2 else xl
        ca = 1 - core if k & 1 else core
        return (la * 2 + ca, fsdp(z, y, xa))

    def along_w(k):
        bits = k & 7
        xa = 1 - xh if bits & 4 else xh
        la = 1 - xl if bits & 2 else xl
        ca = 1 - core if bits & 1 else core
        return (la * 2 + ca, fsdp(z, yi[k // 8], xa))

    partners = [along_z(d) for d in FAR] + [along_w(k) for k in WIDE]

    loading = pltpu.make_async_copy(x_hbm, xv, load_sem)
    loading.start()
    barrier = pltpu.get_barrier_semaphore()
    for device in partners:
        pl.semaphore_signal(barrier, inc=1, device_id=device, device_id_type=MESH)
    q[:, :, other, pl.ds(ROWS_A + ROWS_B, ROWS_C)] = jnp.zeros((NZ, NY, ROWS_C, WID), BF)
    narrow = basis_ref[K - 1].astype(BF)
    q[z, y, xh] = narrow
    v16[K - 1, xh] = narrow
    r[z, y] = res_ref[...]
    for n in range(K - 1):
        v16[n, xh] = basis_ref[n].astype(BF)
    turned = []
    for which in (0, 1):
        pieces = [hid_ref[:, (2 * n + which) * 64 : (2 * n + which + 1) * 64] for n in range(8)]
        turned.append(jnp.concatenate(pieces, axis=1))
    hs[0] = turned[0]
    hs[1] = turned[1]
    ht[xl, core, xh] = hs[xh]

    def q_part(rows, part, oz, oy):
        at = q.at[zi[oz], yi[oy]]
        which = {"f": slice(None), "o": xh, "t": other}.get(part, part)
        return at.at[which, rows]

    a_rows, b_rows = pl.ds(0, ROWS_A), pl.ds(ROWS_A, ROWS_B)
    c_rows = pl.ds(ROWS_A + ROWS_B, ROWS_C)

    def lane_half(sign):
        return pl.ds(half_of(sign) * (WID // 2), WID // 2)

    def slot_a(msg):
        if msg[0] == "az":
            _, dy, s, d = msg
            base = {0: 0, 1: 7, -1: 14, 2: 21}[dy]
            return base + (6 if d == 4 else (d - 1) * 2 + half_of(s)), d == 4, s
        if msg[0] == "ay":
            _, s, d = msg
            return 28 + (2 if d == 2 else half_of(s)), d == 2, s
        return 31, False, 1

    def slot_b(msg):
        if msg[0] == "by":
            _, dz, s, d = msg
            return (dz + 3) * 3 + (2 if d == 2 else half_of(s)), d == 2, s
        if msg[0] == "bz":
            _, s, d = msg
            return 24 + (6 if d == 4 else (d - 1) * 2 + half_of(s)), d == 4, s
        return 31, False, 1

    def piece(buf, slot):
        n, halved, s = slot
        return buf.at[n, half_of(s)] if halved else buf.at[n]

    def place(msg):
        kind = msg[0]
        if kind == "qx":
            rows = pl.ds(0, ROWS_A + ROWS_B)
            here = q.at[z, y, xh, rows]
            return here, here, q.at[z, y, other, rows], along_x(4)
        if kind == "Cz":
            _, s, h = msg
            lanes = lane_half(s) if h == 4 else slice(None)
            here = q.at[zi[wrap(-s * (h - 1), NZ)], y, xh, c_rows, lanes]
            return here, here, q.at[zi[wrap(-s * h, NZ)], y, xh, c_rows, lanes], along_z(s)
        if kind == "Cy":
            _, s, h = msg
            lanes = lane_half(s) if h == 2 else slice(None)
            here = q.at[:, yi[wrap(-s * (h - 1), NY)], xh, c_rows, lanes]
            return here, here, q.at[:, yi[wrap(-s * h, NY)], xh, c_rows, lanes], along_y(s)
        if kind == "Cx":
            lands = qc.at[:, yi[msg[1]]]
            return q.at[:, yi[msg[1]], xh, c_rows], lands, lands, along_x(4)
        if kind == "cx":
            n = ORDER.index(msg[1])
            return send_cx.at[n], recv_cx.at[n], recv_cx.at[n], along_x(4)
        if kind == "cy":
            _, g, s, d = msg
            n, lanes = (2, lane_half(s)) if d == 2 else (half_of(s), slice(None))
            target = recv_cy.at[g, n, :, :, lanes]
            return send_cy.at[g, n, :, :, lanes], target, target, along_y(s)
        if kind == "cz":
            _, s, d = msg
            n, lanes = (6, lane_half(s)) if d == 4 else ((d - 1) * 2 + half_of(s), slice(None))
            target = recv_cz.at[n, :, lanes]
            return send_cz.at[n, :, lanes], target, target, along_z(s)
        if kind == "xc":
            return send_cz.at[7], recv_cz.at[7], recv_cz.at[7], along_x(4)
        if kind in ("Ay", "Az", "Bz", "By"):
            rows = a_rows if kind[0] == "A" else b_rows
            if kind in ("Ay", "Bz"):
                _, s, h, part = msg
            else:
                _, off, s, h, part = msg
            size = NZ if kind[1] == "z" else NY
            if h == size // 2:
                part = half_of(s)
            if kind[1] == "y":
                oz = off if kind == "By" else 0
                here = q_part(rows, part, oz, wrap(-s * (h - 1), NY))
                there = q_part(rows, part, oz, wrap(-s * h, NY))
                return here, here, there, along_y(s)
            oy = off if kind == "Az" else 0
            here = q_part(rows, part, wrap(-s * (h - 1), NZ), oy)
            there = q_part(rows, part, wrap(-s * h, NZ), oy)
            return here, here, there, along_z(s)
        if kind in ("Ry", "RZ", "Rz", "RY"):
            _, s, h = msg
            last = h == (NY if kind[1] in "yY" else NZ) // 2
            rows = pl.ds(0, 16) if kind in ("Ry", "RZ") else pl.ds(16, 48)
            lanes = lane_half(s) if last else slice(None)
            n = NY if kind[1] in "yY" else NZ
            a, b = wrap(-s * (h - 1), n), wrap(-s * h, n)
            if kind == "Ry":
                here, there = r.at[z, yi[a], rows, lanes], r.at[z, yi[b], rows, lanes]
            elif kind == "Rz":
                here, there = r.at[zi[a], y, rows, lanes], r.at[zi[b], y, rows, lanes]
            elif kind == "RZ":
                here, there = r.at[zi[a], :, rows, lanes], r.at[zi[b], :, rows, lanes]
            else:
                here, there = r.at[:, yi[a], rows, lanes], r.at[:, yi[b], rows, lanes]
            return here, here, there, along_y(s) if n == NY else along_z(s)
        if kind == "vx":
            here = v16.at[pl.ds(0, K - 1), xh]
            return here, here, v16.at[pl.ds(0, K - 1), other], along_x(4)
        if kind == "hx":
            return hs.at[other], ht.at[xl, core, xh], ht.at[xl, core, other], along_x(4)
        if kind == "hl":
            here = ht.at[xl, core]
            return here, here, ht.at[1 - xl, core], along_x(2)
        if kind == "hc":
            here = ht.at[:, core]
            return here, here, ht.at[:, 1 - core], along_x(1)
        if kind in ("az", "ay", "xa"):
            slot = slot_a(msg)
            target = piece(recv_a, slot)
            src = piece(send_a, slot)
        elif kind in ("by", "bz", "xb"):
            slot = slot_b(msg)
            target = piece(recv_b, slot)
            src = piece(send_b, slot)
        if kind in ("xa", "xb"):
            return src, target, target, along_x(4)
        if kind in ("az", "by"):
            return src, target, target, along_z(msg[2]) if kind == "az" else along_y(msg[2])
        if kind in ("ay", "bz"):
            return src, target, target, along_y(msg[1]) if kind == "ay" else along_z(msg[1])
        k = msg[1]
        if kind == "g1z":
            here = gz.at[z]
            return here, here, gz.at[zi[-k + NZ if k > 3 else -k]], along_z(k)
        if kind == "g1y":
            here = gy.at[y]
            return here, here, gy.at[yi[-k + NY if k > 1 else -k]], along_y(k)
        if kind == "g2z":
            here = hz.at[z, pl.ds(0, 2)]
            return here, here, hz.at[zi[-k + NZ if k > 3 else -k], pl.ds(0, 2)], along_z(k)
        xa = 1 - xh if k & 4 else xh
        la = 1 - xl if k & 2 else xl
        ca = 1 - core if k & 1 else core
        mine, theirs = xh * 4 + xl * 2 + core, xa * 4 + la * 2 + ca
        if kind == "g1x":
            return gx.at[mine], gx.at[mine], gx.at[theirs], along_x(k)
        d = k // 8
        here = hw.at[y * 8 + mine, pl.ds(0, 2)]
        lands = hw.at[yi[-d + NY if d > 1 else -d] * 8 + theirs, pl.ds(0, 2)]
        return here, here, lands, along_w(k)

    started = []

    def send(msg):
        src, target, _, device = place(msg)
        n = index[msg]
        copy = pltpu.make_async_remote_copy(
            src_ref=src, dst_ref=target, send_sem=send_sem.at[n], recv_sem=recv_sem.at[n],
            device_id=device, device_id_type=MESH,
        )
        copy.start()
        started.append(copy)

    def receive(msg):
        _, _, lands, device = place(msg)
        n = index[msg]
        pltpu.make_async_remote_copy(
            src_ref=lands, dst_ref=lands, send_sem=send_sem.at[n], recv_sem=recv_sem.at[n],
            device_id=device, device_id_type=MESH,
        ).wait_recv()

    def fold(rows, buf, where, slots, out):
        for k in (0, 1):
            total = p[where[0], where[1], k, rows]
            for n, halved, s in slots:
                if not halved or half_of(s) == k:
                    total = total + buf[n, k].astype(F32)
            if out is None:
                p[where[0], where[1], k, rows] = total
            else:
                out[0][out[1], k] = total.astype(BF)

    def fold_a(where, msgs, out=None):
        fold(a_rows, recv_a, where, [slot_a(m) for m in msgs], out and (send_a, slot_a(out)[0]))

    def fold_b(where, msgs, out=None):
        fold(b_rows, recv_b, where, [slot_b(m) for m in msgs], out and (send_b, slot_b(out)[0]))

    def fold_c(plane, row, arrived, out=None):
        for h in (0, 1):
            lanes = pl.ds(h * (WID // 2), WID // 2)
            total = p[plane, row, xh, c_rows, lanes]
            for ref, s in arrived:
                if s is None or half_of(s) == h:
                    total = total + ref[:, lanes].astype(F32)
            if out is None:
                p[plane, row, xh, c_rows, lanes] = total
            else:
                out[:, lanes] = total.astype(BF)

    def lanes_of(plane):
        return pl.ds(pl.multiple_of(plane * (NY * 2 * BLK), 128), NY * 2 * BLK)

    def per_token(rows, k):
        errors = r[2 * k : 2 * k + 2].reshape(512, WID)
        hidden = ht[k // 2, k % 2].reshape(2 * BLK, 512).astype(F32)
        mapped = product(rows, errors, 1, 1)
        n = rows.shape[0] // (2 * BLK)
        return jnp.sum(mapped.reshape(n, 2 * BLK, 512) * hidden[None], axis=1)

    def per_example(tokens):
        t = lax.broadcasted_iota(jnp.int32, (512, 128), 0)
        e = lax.broadcasted_iota(jnp.int32, (512, 128), 1)
        owner = (t // 64) * 4 + 2 * xh + lax.rem(t, 64) // EX_TOK
        marks = jnp.where(owner == lax.rem(e, 32), 1.0, 0.0).astype(BF)
        terms, rest = [], tokens
        for _ in range(3):
            terms.append(rest.astype(BF).astype(F32))
            rest = rest - terms[-1]
        sums = product(jnp.concatenate(terms, axis=0).astype(BF), marks, 1, 0)
        return sums[0:8] + sums[8:16] + sums[16:24]

    def work(name):
        kind = name[0]
        if kind == "start":
            pl.semaphore_wait(barrier, len(partners))
        elif kind == "vx":
            pass
        elif kind == "gram":
            lane = lax.broadcasted_iota(jnp.int32, (8, 128), 1)
            table = jnp.zeros((8, 128), F32)
            for i in range(K):
                rows = [jnp.sum(basis_ref[j] * basis_ref[i], axis=0, keepdims=True) for j in range(K)]
                column = jnp.sum(jnp.concatenate(rows, axis=0), axis=1, keepdims=True)
                table = table + jnp.where(lane == i, column, 0.0)
            early[8:16] = table
            early[0:8] = jnp.zeros((8, 128), F32)
        elif kind == "load":
            loading.wait()
        elif kind == "m1":
            total = None
            for dz in PLANES[name[1]]:
                term = product(xv[:, lanes_of(zi[dz])], q[zi[dz]].reshape(NY * 2 * BLK, WID), 1, 0)
                total = term if total is None else total + term
            acc[...] = total if name[1] == 0 else acc[...] + total
        elif kind == "xs":
            k = name[1]
            if k == 0:
                f = lax.broadcasted_iota(jnp.int32, (1280, 128), 0)
                at = lax.broadcasted_iota(jnp.int32, (1280, 128), 1)
                block = (f * 52429) >> 22
                inside = f - block * BLK - (ROWS_A + ROWS_B)
                hit = (inside >= 0) & ((block & 1) == other) & ((block >> 1) * ROWS_C + inside == at)
                select[...] = jnp.where(hit, 1.0, 0.0).astype(BF)
            columns = xv[:, 1280 * k : 1280 * (k + 1)]
            xc[:, 128 * k : 128 * (k + 1)] = product(columns, select[...], 1, 0).astype(BF)
        elif kind == "m1c":
            acc[...] = acc[...] + product(xc[...], qc[...].reshape(NZ * NY * ROWS_C, WID), 1, 0)
        elif kind == "img":
            img[...] = acc[...].astype(BF)
        elif kind == "m2":
            plane = zi[name[1]]
            p[plane] = product(xv[:, lanes_of(plane)], img[...], 0, 0).reshape(NY, 2, BLK, WID)
        elif kind == "az":
            dy = name[1]
            if name[2] == 4:
                fold_a((zi[4], yi[dy]), [], ("az", dy, 1, 4))
            elif name[2] == 0:
                fold_a((z, yi[dy]), [("az", dy, s, 1) for s in SIGNS])
            else:
                s, d = name[2:]
                fold_a((zi[s * d], yi[dy]), [("az", dy, s, d + 1)], ("az", dy, s, d))
        elif kind == "ay":
            if name[1] == 2 and len(name) == 2:
                fold_a((z, yi[2]), [], ("ay", 1, 2))
            else:
                s = name[1]
                fold_a((z, yi[s]), [("ay", s, 2)], ("ay", s, 1))
        elif kind == "xa":
            fold_a((z, y), [("ay", s, 1) for s in SIGNS])
            fold_a((z, y), [], ("xa",))
        elif kind == "by":
            dz = name[1]
            if len(name) == 4:
                s = name[2]
                fold_b((zi[dz], yi[s]), [("by", dz, s, 2)], ("by", dz, s, 1))
            elif name[2] == 2:
                fold_b((zi[dz], yi[2]), [], ("by", dz, 1, 2))
            else:
                fold_b((zi[dz], y), [("by", dz, s, 1) for s in SIGNS])
        elif kind == "bz":
            if len(name) == 2:
                fold_b((zi[4], y), [], ("bz", 1, 4))
            else:
                s, d = name[1:]
                fold_b((zi[s * d], y), [("bz", s, d + 1)], ("bz", s, d))
        elif kind == "xb":
            fold_b((z, y), [("bz", s, 1) for s in SIGNS])
            fold_b((z, y), [], ("xb",))
        elif kind == "cx":
            send_cx[ORDER.index(name[1])] = p[zi[name[1]], :, other, c_rows].astype(BF)
        elif kind == "cs":
            plane = zi[name[1]]
            arrived = recv_cx[ORDER.index(name[1])].astype(F32)
            p[plane, :, xh, c_rows] = p[plane, :, xh, c_rows] + arrived
        elif kind == "cy":
            g = name[1]
            for j, dz in enumerate(GROUPS[g]):
                if len(name) == 4:
                    s = name[2]
                    got = [(recv_cy.at[g, 2, j], s)]
                    fold_c(zi[dz], yi[s], got, send_cy.at[g, half_of(s), j])
                elif name[2] == 2:
                    fold_c(zi[dz], yi[2], [], send_cy.at[g, 2, j])
                else:
                    fold_c(zi[dz], y, [(recv_cy.at[g, n, j], None) for n in (0, 1)])
        elif kind == "cz":
            if len(name) == 2:
                fold_c(zi[4], y, [], send_cz.at[6])
            else:
                s, d = name[1:]
                n = 6 if d == 3 else d * 2 + half_of(s)
                got = [(recv_cz.at[n], s if d == 3 else None)]
                fold_c(zi[s * d], y, got, send_cz.at[(d - 1) * 2 + half_of(s)])
        elif kind == "xc":
            fold_c(z, y, [(recv_cz.at[n], None) for n in (0, 1)])
            fold_c(z, y, [], send_cz.at[7])
        elif kind == "p8":
            k = name[1]
            if k == 0:
                v16[K - 1, other, pl.ds(0, ROWS_A + ROWS_B)] = q[z, y, other, pl.ds(0, ROWS_A + ROWS_B)]
                v16[K - 1, other, c_rows] = qc[z, y]
            sums = per_example(per_token(v16[...].reshape(K * 2 * BLK, WID), k))
            lane = lax.broadcasted_iota(jnp.int32, (8, 128), 1)
            early[0:8] = early[0:8] + jnp.where(lane // 32 == k, sums, 0.0)
        elif kind == "g1":
            gz[z] = early[...]
        elif kind == "g2":
            gy[y] = ring_sum(gz, NZ)
        elif kind == "g3":
            gx[xh * 4 + xl * 2 + core] = ring_sum(gy, NY)

    def ring_sum(buf, n, rows=16):
        total = buf[0, 0:rows]
        for k in range(1, n):
            total = total + buf[k, 0:rows]
        return total

    for name in order:
        needs, _, _, sends = tasks[name]
        if name[0] != "start":
            for msg in needs:
                receive(msg)
        work(name)
        for msg in sends:
            send(msg)

    receive(("xa",))
    receive(("xb",))
    receive(("xc",))
    cur[xh, c_rows] = p[z, y, xh, c_rows] * (1.0 / TOKENS)
    cur[other, c_rows] = recv_cz[7].astype(F32) * (1.0 / TOKENS)
    for k in (0, 1):
        cur[k, a_rows] = (p[z, y, k, a_rows] + recv_a[31, k].astype(F32)) * (1.0 / TOKENS)
        cur[k, b_rows] = (p[z, y, k, b_rows] + recv_b[31, k].astype(F32)) * (1.0 / TOKENS)
    mine = cur[xh]
    rows = [jnp.sum(basis_ref[n] * mine, axis=0, keepdims=True) for n in range(K)]
    rows.append(jnp.sum(mine * mine, axis=0, keepdims=True))
    rows.append(jnp.zeros((7, WID), F32))
    sums = jnp.sum(jnp.concatenate(rows, axis=0), axis=1, keepdims=True)
    sub = lax.broadcasted_iota(jnp.int32, (16, 128), 0)
    lane = lax.broadcasted_iota(jnp.int32, (16, 128), 1)
    sums = jnp.sum(jnp.where(sub == lane, sums, 0.0), axis=0, keepdims=True)
    both = cur[...].reshape(2 * BLK, WID)
    high = both.astype(BF)
    pair = jnp.concatenate([high, (both - high.astype(F32)).astype(BF)], axis=0)
    tokens = [jnp.sum(per_token(pair, k), axis=0, keepdims=True) for k in range(4)]
    tokens = jnp.concatenate(tokens + [jnp.zeros((4, 512), F32)], axis=0)
    sub = lax.broadcasted_iota(jnp.int32, (8, 128), 0)
    lane = lax.broadcasted_iota(jnp.int32, (8, 128), 1)
    shown = jnp.where(lane // 32 == sub, per_example(tokens), 0.0)
    shown = jnp.sum(shown, axis=0, keepdims=True)
    hz[z, 0:1] = shown
    hz[z, 1:2] = sums
    for k in FAR:
        send(("g2z", k))
    own_ref[...] = mine
    for k in range(1, 8):
        receive(("g1x", k))
    first_ref[...] = ring_sum(gx, 8)
    drain = list(started)
    for copy in drain[:-40]:
        copy.wait_send()
    for k in range(1, NZ):
        receive(("g2z", k))
    hw[y * 8 + xh * 4 + xl * 2 + core, 0:2] = ring_sum(hz, NZ, 2)
    for k in WIDE:
        send(("g2w", k))
    for copy in drain[-40:]:
        copy.wait_send()
    for k in WIDE:
        receive(("g2w", k))
    second_ref[0:2] = ring_sum(hw, 32, 2)
    second_ref[2:8] = jnp.zeros((6, 128), F32)
    for copy in started[len(drain):]:
        copy.wait_send()


def finish(own_ref, first_ref, second_ref, basis_ref, new_ref, hess_ref, proj_ref):
    mean = 1.0 / (FF * D)
    first, second = first_ref[...], second_ref[...]
    sub = lax.broadcasted_iota(jnp.int32, (8, 128), 0)
    lane = lax.broadcasted_iota(jnp.int32, (8, 128), 1)
    row = second[1:2] * mean
    coeff = jnp.sum(jnp.where(sub == lane, row, 0.0), axis=1, keepdims=True)
    squared = jnp.sum(jnp.where(lane[0:1] == K, row, 0.0), axis=1, keepdims=True)
    row = jnp.where(lane[0:1] < K, row, 0.0)
    cross = jnp.sum(coeff * first[8:16], axis=0, keepdims=True) * row
    cross = jnp.sum(cross, axis=1, keepdims=True) * mean
    twice = 2.0 * jnp.sum(row * row, axis=1, keepdims=True)
    beta = jnp.sqrt(jnp.maximum(squared - twice + cross, squared * 1e-12))
    inverse = 1.0 / beta
    hess_ref[...] = jnp.where(lane[0:1] == K, beta, row)[:, 0 : K + 1]
    left = own_ref[...]
    for n in range(K):
        left = left - coeff[n : n + 1] * basis_ref[n]
    new_ref[0] = left * inverse
    last = (second[0:1] - jnp.sum(coeff * first[0:8], axis=0, keepdims=True)) * inverse
    scale = (FF * D) ** (-0.5)
    shown = jnp.concatenate([first[0:8], jnp.broadcast_to(last, (8, 128))], axis=0) * scale
    dp = lax.axis_index("dp")
    for n in range(4):
        @pl.when(dp == n)
        def _():
            proj_ref[...] = shown[0 : K + 1, n * 32 : (n + 1) * 32]


def local(train_hidden, index_hidden, index_resid, basis):
    tasks = build()
    order, _, _ = schedule(tasks)
    messages = [m for name in tasks for m in tasks[name][3]]
    messages += [("g2z", k) for k in FAR] + [("g2w", k) for k in WIDE]
    index = {m: n for n, m in enumerate(messages)}
    vmem = pltpu.VMEM
    whole = pl.BlockSpec(memory_space=pltpu.VMEM)
    call = pl.pallas_call(
        functools.partial(kernel, order, tasks, index),
        out_shape=(
            jax.ShapeDtypeStruct((BLK, WID), F32),
            jax.ShapeDtypeStruct((16, 128), F32),
            jax.ShapeDtypeStruct((8, 128), F32),
        ),
        in_specs=[pl.BlockSpec(memory_space=pl.ANY), whole, whole, whole],
        out_specs=(whole, whole, whole),
        scratch_shapes=[
            vmem((1024, FF), BF),
            vmem((NZ, NY, 2, BLK, WID), BF),
            vmem((NZ, NY, ROWS_C, WID), BF),
            vmem((1024, NZ * NY * ROWS_C), BF),
            vmem((1280, 128), BF),
            vmem((NZ, NY, 2, BLK, WID), F32),
            vmem((32, 2, ROWS_A, WID), BF),
            vmem((32, 2, ROWS_B, WID), BF),
            vmem((32, 2, ROWS_A, WID), BF),
            vmem((32, 2, ROWS_B, WID), BF),
            vmem((NZ, NY, ROWS_C, WID), BF),
            vmem((NZ, NY, ROWS_C, WID), BF),
            vmem((2, 3, 4, ROWS_C, WID), BF),
            vmem((2, 3, 4, ROWS_C, WID), BF),
            vmem((8, ROWS_C, WID), BF),
            vmem((8, ROWS_C, WID), BF),
            vmem((1024, WID), F32),
            vmem((1024, WID), BF),
            vmem((NZ, NY, 64, WID), BF),
            vmem((K, 2, BLK, WID), BF),
            vmem((2, 2, 2, BLK, WID), BF),
            vmem((2, BLK, WID), BF),
            vmem((2, BLK, WID), F32),
            vmem((16, 128), F32),
            vmem((NZ, 16, 128), F32),
            vmem((NY, 16, 128), F32),
            vmem((8, 16, 128), F32),
            vmem((NZ, 8, 128), F32),
            vmem((32, 8, 128), F32),
            pltpu.SemaphoreType.DMA,
            pltpu.SemaphoreType.DMA((len(messages),)),
            pltpu.SemaphoreType.DMA((len(messages),)),
        ],
        compiler_params=pltpu.CompilerParams(
            collective_id=0, has_side_effects=True, vmem_limit_bytes=60 * 2**20
        ),
        cost_estimate=pl.CostEstimate(
            flops=14 * 10**9, bytes_accessed=13 * 10**6, transcendentals=0
        ),
        name="arnoldi",
    )
    own, first, second = call(train_hidden, index_hidden.T, index_resid, basis)
    new, hess, proj = pl.pallas_call(
        finish,
        out_shape=(
            jax.ShapeDtypeStruct((1, BLK, WID), F32),
            jax.ShapeDtypeStruct((1, K + 1), F32),
            jax.ShapeDtypeStruct((K + 1, 32), F32),
        ),
        in_specs=[whole] * 4,
        out_specs=(whole, whole, whole),
        name="finish",
    )(own, first, second, basis)
    return new, hess, proj.T


def solution(mesh):
    in_specs = (P("fsdp", None), P("dp", "fsdp"), P("fsdp", "dp"), P(None, "fsdp", "dp"))
    out_specs = (P(None, "fsdp", "dp"), P(), P("dp", None))
    return jax.shard_map(local, mesh=mesh, in_specs=in_specs, out_specs=out_specs, check_vma=False)
```

```python
import functools

import jax
import jax.numpy as jnp
from jax import lax
from jax.experimental import pallas as pl
from jax.experimental.pallas import tpu as pltpu
from jax.sharding import PartitionSpec as P

D = 2048
FF = 5120
TOKENS = 65536
EX_TOK = 32
K = 8
NZ, NY = 8, 4
BLK = 80
WID = 512
ROWS_A, ROWS_B, ROWS_C = 32, 32, 16
MESH = pl.DeviceIdType.MESH
BF = jnp.bfloat16
F32 = jnp.float32
SIGNS = (1, -1)
FAR = (4, 3, 5, 2, 6, 1, 7)
WIDE = sorted(
    range(1, 32), key=lambda k: -(min(k // 8, 4 - k // 8) + (0, 1, 2, 1)[(k >> 1) & 3]) * 2 - (k & 1)
)


def half_of(sign):
    return 0 if sign > 0 else 1


def wrap(delta, size):
    delta %= size
    return delta - size if delta > size // 2 else delta


def parts_of(kind, hop, own):
    if hop == 1 and own:
        return ("o", "t")
    return ("f",)


def link_of(msg):
    kind = msg[0]
    if kind in ("Az", "az"):
        return ("z", msg[2])
    if kind in ("Ay", "ay", "Ry", "RY", "Cy"):
        return ("y", msg[1])
    if kind in ("Bz", "bz", "Rz", "RZ", "Cz", "cz"):
        return ("z", msg[1])
    if kind in ("By", "by", "cy"):
        return ("y", msg[2])
    if kind in ("qx", "vx", "hx", "xa", "xb", "xc", "hl", "Cx", "cx"):
        return ("x", 0)
    return ("c", 0) if kind == "hc" else (kind, msg[1])


def kilobytes(msg):
    kind = msg[0]
    a, b = 2 * ROWS_A, 2 * ROWS_B
    if kind == "Ay":
        return a / 2 if msg[3] in ("o", "t") or msg[2] == 2 else a
    if kind == "Az":
        return a / 2 if msg[4] in ("o", "t") or msg[3] == 4 else a
    if kind == "Bz":
        return b / 2 if msg[3] in ("o", "t") or msg[2] == 4 else b
    if kind == "By":
        return b / 2 if msg[4] in ("o", "t") or msg[3] == 2 else b
    if kind == "az":
        return a / 2 if msg[3] == 4 else a
    if kind == "ay":
        return a / 2 if msg[2] == 2 else a
    if kind == "bz":
        return b / 2 if msg[2] == 4 else b
    if kind == "by":
        return b / 2 if msg[3] == 2 else b
    if kind in ("Ry", "Rz", "RZ", "RY", "Cz", "Cy"):
        full = {"Ry": 16, "Rz": 48, "RZ": 64, "RY": 384, "Cz": ROWS_C, "Cy": 8 * ROWS_C}[kind]
        return full / 2 if msg[2] == (4 if kind[1] in "zZ" else 2) else full
    if kind == "cz":
        return ROWS_C / 2 if msg[2] == 4 else ROWS_C
    if kind == "cy":
        return 2 * ROWS_C if msg[3] == 2 else 4 * ROWS_C
    if kind in ("Cx", "cx"):
        return (8 if kind == "Cx" else 4) * ROWS_C
    return {"qx": 64, "xc": ROWS_C, "vx": 560, "hx": 80, "hl": 160, "hc": 320, "xa": a, "xb": b}.get(kind, 8)


def build():
    tasks = {}

    def task(name, needs=(), after=(), cost=0.0, sends=()):
        needs, sends = list(needs), list(sends)
        tasks[name] = (needs, list(after), cost + 0.01 * (len(needs) + len(sends)), sends)

    first = []
    for s in SIGNS:
        first += [("Bz", s, 1), ("Ay", s, 1)]
    for s in SIGNS:
        first += [("Az", 0, s, 1), ("By", 0, s, 1)]
    task(
        ("start",),
        cost=0.5,
        sends=[("qx",)] + [("Cz", s, 1) for s in SIGNS] + [m + ("o",) for m in first]
        + [("Rz", s, 1) for s in SIGNS] + [("Ry", s, 1) for s in SIGNS],
    )
    task(("qx",), [("qx",)], [("start",)], sends=[m + ("t",) for m in first])
    for s in SIGNS:
        task(
            ("Ay", s),
            [("Ay", s, 1, "o"), ("Ay", s, 1, "t")],
            [("qx",)],
            sends=[("Ay", s, 2, "f")] + [("Az", wrap(-s, NY), u, 1, "f") for u in SIGNS],
        )
    task(
        ("Ay2",),
        [("Ay", s, 2, "f") for s in SIGNS],
        [("Ay", s) for s in SIGNS],
        sends=[("Az", 2, u, 1, "f") for u in SIGNS],
    )
    for dy in (0, 1, -1, 2):
        for s in SIGNS:
            for h in (1, 2, 3):
                task(
                    ("Az", dy, s, h),
                    [("Az", dy, s, h, p) for p in parts_of("Az", h, dy == 0)],
                    sends=[("Az", dy, s, h + 1, "f")],
                )
    for s in SIGNS:
        for h in (1, 2, 3):
            task(
                ("Bz", s, h),
                [("Bz", s, h, p) for p in parts_of("Bz", h, True)],
                sends=[("Bz", s, h + 1, "f")] + [("By", wrap(-s * h, NZ), u, 1, "f") for u in SIGNS],
            )
    task(
        ("Bz4",), [("Bz", s, 4, "f") for s in SIGNS], sends=[("By", 4, u, 1, "f") for u in SIGNS]
    )
    for dz in range(-3, 5):
        for s in SIGNS:
            task(
                ("By", dz, s),
                [("By", dz, s, 1, p) for p in parts_of("By", 1, dz == 0)],
                sends=[("By", dz, s, 2, "f")],
            )
    for s in SIGNS:
        for h in (1, 2, 3):
            task(("Cz", s, h), [("Cz", s, h)], sends=[("Cz", s, h + 1)])
        task(("Cy", s), [("Cy", s, 1)], sends=[("Cx", wrap(-s, NY)), ("Cy", s, 2)])
    task(
        ("CY0",),
        [("Cz", s, 4) for s in SIGNS],
        [("Cz", s, h) for s in SIGNS for h in (1, 2, 3)],
        sends=[("Cx", 0)] + [("Cy", s, 1) for s in SIGNS],
    )
    task(("Cy2",), [("Cy", s, 2) for s in SIGNS], [("Cy", s) for s in SIGNS], sends=[("Cx", 2)])
    late = {
        0: [],
        1: [("Bz4",)],
        2: [("Az", dy, s, 2) for dy in (0, 1, -1, 2) for s in SIGNS],
        3: [("Az", dy, s, 3) for dy in (0, 1, -1, 2) for s in SIGNS]
        + [("By", dz, s) for dz in range(-3, 5) for s in SIGNS],
    }[LATE]
    for s in SIGNS:
        task(("Ry", s), [("Ry", s, 1)], sends=[("Ry", s, 2)])
        for h in (1, 2, 3):
            task(("Rz", s, h), [("Rz", s, h)], sends=[("Rz", s, h + 1)])
            task(("RZ", s, h), [("RZ", s, h)], sends=[("RZ", s, h + 1)])
        task(("RY", s), [("RY", s, 1)], sends=[("RY", s, 2)])
    task(
        ("RZ0",),
        [("Ry", s, 2) for s in SIGNS],
        [("Ry", s) for s in SIGNS] + late,
        sends=[("RZ", s, 1) for s in SIGNS],
    )
    task(
        ("RY0",),
        [("Rz", s, 4) for s in SIGNS],
        [("Rz", s, h) for s in SIGNS for h in (1, 2, 3)] + late,
        sends=[("RY", s, 1) for s in SIGNS],
    )
    task(("vx",), after=[("start",)], cost=0.25, sends=[("vx",)])
    task(("hx",), after=[("vx",)], cost=0.25, sends=[("hx",)])
    task(("hl",), [("hx",)], [("hx",), ("Cy2",)], sends=[("hl",)])
    task(("hc",), [("hl",)], [("hl",)], sends=[("hc",)])
    task(("gram",), after=[("vx",)], cost=0.8)
    for g, planes in enumerate(PLANES):
        needs, after = [], [("m1", g - 1)] if g else [("load",), ("CY0",), ("Cy2",)]
        if g == len(PLANES) - 1:
            after.append(("m1c",))
        for dz in planes:
            for s in SIGNS:
                needs.append(("By", dz, s, 2, "f"))
                after.append(("By", dz, s))
            if dz == 0:
                after += [("Ay", s) for s in SIGNS] + [("Ay2",)]
            elif dz == 4:
                needs += [("Az", dy, s, 4, "f") for dy in (0, 1, -1, 2) for s in SIGNS]
                after.append(("Bz4",))
            else:
                s = -1 if dz > 0 else 1
                after += [("Az", dy, s, abs(dz)) for dy in (0, 1, -1, 2)] + [("Bz", s, abs(dz))]
        task(("m1", g), needs, after, cost=1.1 * len(planes))
    task(("load",), after=[("start",)], cost=0.1)
    for k in range(4):
        task(("xs", k), after=[("load",)] + ([("xs", k - 1)] if k else []), cost=0.7)
    task(
        ("m1c",),
        [("Cx", dy) for dy in (0, 1, -1, 2)],
        [("CY0",), ("Cy2",), ("m1", 0), ("xs", 3)],
        cost=0.9,
    )
    task(("img",), after=[("m1", len(PLANES) - 1)], cost=0.0)
    for n, dz in enumerate(ORDER):
        task(("m2", dz), after=[("img",)] + ([("m2", ORDER[n - 1])] if n else []), cost=0.95)
    for dy in (0, 1, -1, 2):
        task(("az", dy, 4), after=[("m2", 4)], cost=0.04, sends=[("az", dy, s, 4) for s in SIGNS])
        for s in SIGNS:
            for d in (3, 2, 1):
                task(
                    ("az", dy, s, d),
                    [("az", dy, s, d + 1)],
                    [("m2", s * d)],
                    cost=0.04,
                    sends=[("az", dy, s, d)],
                )
        task(("az", dy, 0), [("az", dy, s, 1) for s in SIGNS], [("m2", 0)], cost=0.04)
    task(("ay", 2), after=[("az", 2, 0)], cost=0.04, sends=[("ay", s, 2) for s in SIGNS])
    for s in SIGNS:
        task(("ay", s, 1), [("ay", s, 2)], [("az", s, 0)], cost=0.04, sends=[("ay", s, 1)])
    task(
        ("xa",), [("ay", s, 1) for s in SIGNS], [("az", 0, 0)], cost=0.04, sends=[("xa",)]
    )
    for dz in range(-3, 5):
        task(("by", dz, 2), after=[("m2", dz)], cost=0.04, sends=[("by", dz, s, 2) for s in SIGNS])
        for s in SIGNS:
            task(
                ("by", dz, s, 1),
                [("by", dz, s, 2)],
                [("m2", dz)],
                cost=0.04,
                sends=[("by", dz, s, 1)],
            )
        task(("by", dz, 0), [("by", dz, s, 1) for s in SIGNS], [("m2", dz)], cost=0.06)
    task(("bz", 4), after=[("by", 4, 0)], cost=0.04, sends=[("bz", s, 4) for s in SIGNS])
    for s in SIGNS:
        for d in (3, 2, 1):
            task(
                ("bz", s, d),
                [("bz", s, d + 1)],
                [("by", s * d, 0)],
                cost=0.04,
                sends=[("bz", s, d)],
            )
    task(("xb",), [("bz", s, 1) for s in SIGNS], [("by", 0, 0)], cost=0.06, sends=[("xb",)])
    for n, dz in enumerate(ORDER):
        task(("cx", dz), after=[("m2", dz)], cost=0.04, sends=[("cx", dz)])
        task(("cs", dz), [("cx", dz)], [("m2", dz)], cost=0.04)
    for g in (0, 1):
        done = [("cs", dz) for dz in GROUPS[g]]
        task(("cy", g, 2), after=done, cost=0.04, sends=[("cy", g, s, 2) for s in SIGNS])
        for s in SIGNS:
            task(("cy", g, s, 1), [("cy", g, s, 2)], done, cost=0.04, sends=[("cy", g, s, 1)])
        task(("cy", g, 0), [("cy", g, s, 1) for s in SIGNS], done, cost=0.04)
    task(("cz", 4), after=[("cy", 0, 0)], cost=0.03, sends=[("cz", s, 4) for s in SIGNS])
    for s in SIGNS:
        for d in (3, 2, 1):
            task(
                ("cz", s, d),
                [("cz", s, d + 1)],
                [("cy", 0 if s * d in GROUPS[0] else 1, 0)],
                cost=0.03,
                sends=[("cz", s, d)],
            )
    task(("xc",), [("cz", s, 1) for s in SIGNS], [("cy", 1, 0)], cost=0.03, sends=[("xc",)])
    for k in range(8):
        needs, after = [], [("m2", ORDER[-1])]
        if k == 0:
            needs += [("RZ", s, 4) for s in SIGNS] + [("RY", s, 2) for s in SIGNS]
            needs += [("hc",), ("vx",)]
            after += [("RZ", s, h) for s in SIGNS for h in (1, 2, 3)] + [("RY", s) for s in SIGNS]
            after += [("RZ0",), ("RY0",), ("hc",), ("vx",), ("gram",)]
        else:
            after += [("p8", k - 1)]
        task(("p8", k), needs, after, cost=0.65)
    task(("g1",), after=[("p8", 7)], cost=0.1, sends=[("g1z", k) for k in FAR])
    return tasks


PLANES = ((0,), (1, -1), (2, -2), (3, -3), (4,))
ORDER = (4, 3, -3, 2, -2, 1, -1, 0)
LATE, RATE, DELAY, CLS = 1, 46.0, 1.4, True
SLACK = {"Ry": 1.0, "Rz": 1.0, "RZ": 1.5, "RY": 1.5, "vx": 2.0, "hx": 2.0, "hl": 2.0, "hc": 2.0}
GROUPS = (ORDER[:4], ORDER[4:])


def schedule(tasks):
    rate = {"z": RATE, "y": RATE, "x": RATE - 1, "c": 400.0}
    delay = {"z": DELAY, "y": DELAY, "x": DELAY + 0.5, "c": 0.8}
    waits = {}
    followers = {name: [] for name in tasks}
    for name, (needs, after, _, _) in tasks.items():
        for msg in needs:
            waits.setdefault(msg, []).append(name)
        for other in after:
            followers[other].append(name)

    def cost_of(msg):
        axis = link_of(msg)[0]
        return kilobytes(msg) / rate.get(axis, 40.0) + delay.get(axis, 3.0)

    @functools.cache
    def rank(name):
        _, _, cost, sends = tasks[name]
        rest = [rank(f) for f in followers[name]]
        rest += [cost_of(m) + max([rank(w) for w in waits.get(m, ())], default=0) for m in sends]
        return cost + max(rest, default=0)

    now, free, arrives, done, order = 0.0, {}, {}, {}, []
    left = dict(tasks)
    while left:
        ready, soonest = [], None
        for name, (needs, after, cost, sends) in left.items():
            if any(a not in done for a in after) or any(m not in arrives for m in needs):
                continue
            at = max([arrives[m] for m in needs], default=0.0)
            if at <= now:
                heavy = CLS and cost >= 0.3 and not sends
                ready.append((heavy, -rank(name), at, name))
            else:
                soonest = at if soonest is None else min(soonest, at)
        if not ready:
            now = soonest
            continue
        name = min(ready, key=lambda r: r[:3])[3]
        _, _, cost, sends = left.pop(name)
        now += cost
        done[name] = now
        order.append(name)
        for msg in sends:
            link = link_of(msg)
            axis = link[0]
            begin = max(now, free.get(link, 0.0))
            free[link] = begin + kilobytes(msg) / rate.get(axis, 40.0)
            arrives[msg] = free[link] + delay.get(axis, 3.0) + SLACK.get(msg[0], 0.0)
    return order, done, arrives


def product(a, b, ca, cb):
    return lax.dot_general(a, b, (((ca,), (cb,)), ((), ())), preferred_element_type=F32)


def kernel(
    order, tasks, index,
    x_hbm, hid_hbm, res_hbm, basis_hbm,
    own_ref, first_ref, second_ref,
    xv, q, qc, xc, select, p, send_a, send_b, recv_a, recv_b,
    send_cx, recv_cx, send_cy, recv_cy, send_cz, recv_cz, acc, img, r, v16, ht, hs, cur,
    early, tokens8, basis_ref, hid_ref, res_ref, gz, gy, gx, hz, hw, load_sem, send_sem, recv_sem,
):
    dp, fs = lax.axis_index("dp"), lax.axis_index("fsdp")
    z, y, xh = fs // 8, lax.rem(fs // 2, 4), lax.rem(fs, 2)
    xl, core = dp // 2, lax.rem(dp, 2)
    other = 1 - xh

    zi = {d: lax.rem(z + (d + NZ), NZ) for d in range(-3, 8)}
    zi[-4] = zi[4]
    yi = {d: lax.rem(y + (d + NY), NY) for d in range(-1, 4)}
    yi[-2] = yi[2]

    def fsdp(za, ya, xa):
        return (za * NY + ya) * 2 + xa

    def along_z(d):
        return (dp, fsdp(zi[d], y, xh))

    def along_y(d):
        return (dp, fsdp(z, yi[d], xh))

    def along_x(k):
        xa = 1 - xh if k & 4 else xh
        la = 1 - xl if k & 2 else xl
        ca = 1 - core if k & 1 else core
        return (la * 2 + ca, fsdp(z, y, xa))

    def along_w(k):
        bits = k & 7
        xa = 1 - xh if bits & 4 else xh
        la = 1 - xl if bits & 2 else xl
        ca = 1 - core if bits & 1 else core
        return (la * 2 + ca, fsdp(z, yi[k // 8], xa))

    partners = [along_z(d) for d in FAR] + [along_w(k) for k in WIDE]

    barrier = pltpu.get_barrier_semaphore()
    loads = [
        pltpu.make_async_copy(basis_hbm.at[K - 1], basis_ref.at[K - 1], load_sem.at[0]),
        pltpu.make_async_copy(res_hbm, res_ref, load_sem.at[1]),
        pltpu.make_async_copy(hid_hbm, hid_ref, load_sem.at[2]),
        pltpu.make_async_copy(
            basis_hbm.at[pl.ds(0, K - 1)], basis_ref.at[pl.ds(0, K - 1)], load_sem.at[3]
        ),
        pltpu.make_async_copy(x_hbm, xv, load_sem.at[4]),
    ]
    for load in loads:
        load.start()
    for device in partners:
        pl.semaphore_signal(barrier, inc=1, device_id=device, device_id_type=MESH)
    loads[0].wait()
    loads[1].wait()
    q[:, :, other, pl.ds(ROWS_A + ROWS_B, ROWS_C)] = jnp.zeros((NZ, NY, ROWS_C, WID), BF)
    narrow = basis_ref[K - 1].astype(BF)
    q[z, y, xh] = narrow
    v16[K - 1, xh] = narrow
    r[z, y] = res_ref[...]

    def q_part(rows, part, oz, oy):
        at = q.at[zi[oz], yi[oy]]
        which = {"f": slice(None), "o": xh, "t": other}.get(part, part)
        return at.at[which, rows]

    a_rows, b_rows = pl.ds(0, ROWS_A), pl.ds(ROWS_A, ROWS_B)
    c_rows = pl.ds(ROWS_A + ROWS_B, ROWS_C)

    def lane_half(sign):
        return pl.ds(half_of(sign) * (WID // 2), WID // 2)

    def slot_a(msg):
        if msg[0] == "az":
            _, dy, s, d = msg
            base = {0: 0, 1: 7, -1: 14, 2: 21}[dy]
            return base + (6 if d == 4 else (d - 1) * 2 + half_of(s)), d == 4, s
        if msg[0] == "ay":
            _, s, d = msg
            return 28 + (2 if d == 2 else half_of(s)), d == 2, s
        return 31, False, 1

    def slot_b(msg):
        if msg[0] == "by":
            _, dz, s, d = msg
            return (dz + 3) * 3 + (2 if d == 2 else half_of(s)), d == 2, s
        if msg[0] == "bz":
            _, s, d = msg
            return 24 + (6 if d == 4 else (d - 1) * 2 + half_of(s)), d == 4, s
        return 31, False, 1

    def piece(buf, slot):
        n, halved, s = slot
        return buf.at[n, half_of(s)] if halved else buf.at[n]

    def place(msg):
        kind = msg[0]
        if kind == "qx":
            rows = pl.ds(0, ROWS_A + ROWS_B)
            here = q.at[z, y, xh, rows]
            return here, here, q.at[z, y, other, rows], along_x(4)
        if kind == "Cz":
            _, s, h = msg
            lanes = lane_half(s) if h == 4 else slice(None)
            here = q.at[zi[wrap(-s * (h - 1), NZ)], y, xh, c_rows, lanes]
            return here, here, q.at[zi[wrap(-s * h, NZ)], y, xh, c_rows, lanes], along_z(s)
        if kind == "Cy":
            _, s, h = msg
            lanes = lane_half(s) if h == 2 else slice(None)
            here = q.at[:, yi[wrap(-s * (h - 1), NY)], xh, c_rows, lanes]
            return here, here, q.at[:, yi[wrap(-s * h, NY)], xh, c_rows, lanes], along_y(s)
        if kind == "Cx":
            lands = qc.at[:, yi[msg[1]]]
            return q.at[:, yi[msg[1]], xh, c_rows], lands, lands, along_x(4)
        if kind == "cx":
            n = ORDER.index(msg[1])
            return send_cx.at[n], recv_cx.at[n], recv_cx.at[n], along_x(4)
        if kind == "cy":
            _, g, s, d = msg
            n, lanes = (2, lane_half(s)) if d == 2 else (half_of(s), slice(None))
            target = recv_cy.at[g, n, :, :, lanes]
            return send_cy.at[g, n, :, :, lanes], target, target, along_y(s)
        if kind == "cz":
            _, s, d = msg
            n, lanes = (6, lane_half(s)) if d == 4 else ((d - 1) * 2 + half_of(s), slice(None))
            target = recv_cz.at[n, :, lanes]
            return send_cz.at[n, :, lanes], target, target, along_z(s)
        if kind == "xc":
            return send_cz.at[7], recv_cz.at[7], recv_cz.at[7], along_x(4)
        if kind in ("Ay", "Az", "Bz", "By"):
            rows = a_rows if kind[0] == "A" else b_rows
            if kind in ("Ay", "Bz"):
                _, s, h, part = msg
            else:
                _, off, s, h, part = msg
            size = NZ if kind[1] == "z" else NY
            if h == size // 2:
                part = half_of(s)
            if kind[1] == "y":
                oz = off if kind == "By" else 0
                here = q_part(rows, part, oz, wrap(-s * (h - 1), NY))
                there = q_part(rows, part, oz, wrap(-s * h, NY))
                return here, here, there, along_y(s)
            oy = off if kind == "Az" else 0
            here = q_part(rows, part, wrap(-s * (h - 1), NZ), oy)
            there = q_part(rows, part, wrap(-s * h, NZ), oy)
            return here, here, there, along_z(s)
        if kind in ("Ry", "RZ", "Rz", "RY"):
            _, s, h = msg
            last = h == (NY if kind[1] in "yY" else NZ) // 2
            rows = pl.ds(0, 16) if kind in ("Ry", "RZ") else pl.ds(16, 48)
            lanes = lane_half(s) if last else slice(None)
            n = NY if kind[1] in "yY" else NZ
            a, b = wrap(-s * (h - 1), n), wrap(-s * h, n)
            if kind == "Ry":
                here, there = r.at[z, yi[a], rows, lanes], r.at[z, yi[b], rows, lanes]
            elif kind == "Rz":
                here, there = r.at[zi[a], y, rows, lanes], r.at[zi[b], y, rows, lanes]
            elif kind == "RZ":
                here, there = r.at[zi[a], :, rows, lanes], r.at[zi[b], :, rows, lanes]
            else:
                here, there = r.at[:, yi[a], rows, lanes], r.at[:, yi[b], rows, lanes]
            return here, here, there, along_y(s) if n == NY else along_z(s)
        if kind == "vx":
            here = v16.at[pl.ds(0, K - 1), xh]
            return here, here, v16.at[pl.ds(0, K - 1), other], along_x(4)
        if kind == "hx":
            return hs.at[other], ht.at[xl, core, xh], ht.at[xl, core, other], along_x(4)
        if kind == "hl":
            here = ht.at[xl, core]
            return here, here, ht.at[1 - xl, core], along_x(2)
        if kind == "hc":
            here = ht.at[:, core]
            return here, here, ht.at[:, 1 - core], along_x(1)
        if kind in ("az", "ay", "xa"):
            slot = slot_a(msg)
            target = piece(recv_a, slot)
            src = piece(send_a, slot)
        elif kind in ("by", "bz", "xb"):
            slot = slot_b(msg)
            target = piece(recv_b, slot)
            src = piece(send_b, slot)
        if kind in ("xa", "xb"):
            return src, target, target, along_x(4)
        if kind in ("az", "by"):
            return src, target, target, along_z(msg[2]) if kind == "az" else along_y(msg[2])
        if kind in ("ay", "bz"):
            return src, target, target, along_y(msg[1]) if kind == "ay" else along_z(msg[1])
        k = msg[1]
        if kind == "g1z":
            here = gz.at[z]
            return here, here, gz.at[zi[-k + NZ if k > 3 else -k]], along_z(k)
        if kind == "g1y":
            here = gy.at[y]
            return here, here, gy.at[yi[-k + NY if k > 1 else -k]], along_y(k)
        if kind == "g2z":
            here = hz.at[z, pl.ds(0, 2)]
            return here, here, hz.at[zi[-k + NZ if k > 3 else -k], pl.ds(0, 2)], along_z(k)
        xa = 1 - xh if k & 4 else xh
        la = 1 - xl if k & 2 else xl
        ca = 1 - core if k & 1 else core
        mine, theirs = xh * 4 + xl * 2 + core, xa * 4 + la * 2 + ca
        if kind == "g1x":
            return gx.at[mine], gx.at[mine], gx.at[theirs], along_x(k)
        d = k // 8
        here = hw.at[y * 8 + mine, pl.ds(0, 2)]
        lands = hw.at[yi[-d + NY if d > 1 else -d] * 8 + theirs, pl.ds(0, 2)]
        return here, here, lands, along_w(k)

    started = []

    def send(msg):
        src, target, _, device = place(msg)
        n = index[msg]
        copy = pltpu.make_async_remote_copy(
            src_ref=src, dst_ref=target, send_sem=send_sem.at[n], recv_sem=recv_sem.at[n],
            device_id=device, device_id_type=MESH,
        )
        copy.start()
        started.append(copy)

    def receive(msg):
        _, _, lands, device = place(msg)
        n = index[msg]
        pltpu.make_async_remote_copy(
            src_ref=lands, dst_ref=lands, send_sem=send_sem.at[n], recv_sem=recv_sem.at[n],
            device_id=device, device_id_type=MESH,
        ).wait_recv()

    def fold(rows, buf, where, slots, out):
        for k in (0, 1):
            total = p[where[0], where[1], k, rows]
            for n, halved, s in slots:
                if not halved or half_of(s) == k:
                    total = total + buf[n, k].astype(F32)
            if out is None:
                p[where[0], where[1], k, rows] = total
            else:
                out[0][out[1], k] = total.astype(BF)

    def fold_a(where, msgs, out=None):
        fold(a_rows, recv_a, where, [slot_a(m) for m in msgs], out and (send_a, slot_a(out)[0]))

    def fold_b(where, msgs, out=None):
        fold(b_rows, recv_b, where, [slot_b(m) for m in msgs], out and (send_b, slot_b(out)[0]))

    def fold_c(plane, row, arrived, out=None):
        for h in (0, 1):
            lanes = pl.ds(h * (WID // 2), WID // 2)
            total = p[plane, row, xh, c_rows, lanes]
            for ref, s in arrived:
                if s is None or half_of(s) == h:
                    total = total + ref[:, lanes].astype(F32)
            if out is None:
                p[plane, row, xh, c_rows, lanes] = total
            else:
                out[:, lanes] = total.astype(BF)

    def lanes_of(plane):
        return pl.ds(pl.multiple_of(plane * (NY * 2 * BLK), 128), NY * 2 * BLK)

    def per_token(rows, k, part=None):
        if part is None:
            many, errors, hidden = 512, r[2 * k : 2 * k + 2], ht[k // 2, k % 2]
        else:
            many, errors = 256, r[2 * k + part]
            hidden = ht[k // 2, k % 2, :, :, 256 * part : 256 * (part + 1)]
        mapped = product(rows, errors.reshape(many, WID), 1, 1)
        n = rows.shape[0] // (2 * BLK)
        hidden = hidden.reshape(2 * BLK, many).astype(F32)
        return jnp.sum(mapped.reshape(n, 2 * BLK, many) * hidden[None], axis=1)

    def per_example(tokens):
        t = lax.broadcasted_iota(jnp.int32, (512, 128), 0)
        e = lax.broadcasted_iota(jnp.int32, (512, 128), 1)
        owner = (t // 64) * 4 + 2 * xh + lax.rem(t, 64) // EX_TOK
        marks = jnp.where(owner == lax.rem(e, 32), 1.0, 0.0).astype(BF)
        terms, rest = [], tokens
        for _ in range(3):
            terms.append(rest.astype(BF).astype(F32))
            rest = rest - terms[-1]
        sums = product(jnp.concatenate(terms, axis=0).astype(BF), marks, 1, 0)
        return sums[0:8] + sums[8:16] + sums[16:24]

    def work(name):
        kind = name[0]
        if kind == "start":
            pl.semaphore_wait(barrier, len(partners))
        elif kind == "vx":
            loads[3].wait()
            for n in range(K - 1):
                v16[n, xh] = basis_ref[n].astype(BF)
        elif kind == "hx":
            loads[2].wait()
            for which in (0, 1):
                cuts = [(2 * n + which) * 64 for n in range(8)]
                pieces = [hid_ref[:, at : at + 64] for at in cuts]
                hs[which] = jnp.concatenate(pieces, axis=1)
            ht[xl, core, xh] = hs[xh]
        elif kind == "gram":
            lane = lax.broadcasted_iota(jnp.int32, (8, 128), 1)
            table = jnp.zeros((8, 128), F32)
            for i in range(K):
                rows = [jnp.sum(basis_ref[j] * basis_ref[i], axis=0, keepdims=True) for j in range(K)]
                column = jnp.sum(jnp.concatenate(rows, axis=0), axis=1, keepdims=True)
                table = table + jnp.where(lane == i, column, 0.0)
            early[8:16] = table
            early[0:8] = jnp.zeros((8, 128), F32)
        elif kind == "load":
            loads[4].wait()
        elif kind == "m1":
            total = None
            for dz in PLANES[name[1]]:
                term = product(xv[:, lanes_of(zi[dz])], q[zi[dz]].reshape(NY * 2 * BLK, WID), 1, 0)
                total = term if total is None else total + term
            if name[1] == len(PLANES) - 1:
                img[...] = (acc[...] + total).astype(BF)
            else:
                acc[...] = total if name[1] == 0 else acc[...] + total
        elif kind == "xs":
            k = name[1]
            if k == 0:
                f = lax.broadcasted_iota(jnp.int32, (1280, 128), 0)
                at = lax.broadcasted_iota(jnp.int32, (1280, 128), 1)
                block = (f * 52429) >> 22
                inside = f - block * BLK - (ROWS_A + ROWS_B)
                hit = (inside >= 0) & ((block & 1) == other) & ((block >> 1) * ROWS_C + inside == at)
                select[...] = jnp.where(hit, 1.0, 0.0).astype(BF)
            columns = xv[:, 1280 * k : 1280 * (k + 1)]
            xc[:, 128 * k : 128 * (k + 1)] = product(columns, select[...], 1, 0).astype(BF)
        elif kind == "m1c":
            acc[...] = acc[...] + product(xc[...], qc[...].reshape(NZ * NY * ROWS_C, WID), 1, 0)
        elif kind == "img":
            pass
        elif kind == "m2":
            plane = zi[name[1]]
            p[plane] = product(xv[:, lanes_of(plane)], img[...], 0, 0).reshape(NY, 2, BLK, WID)
        elif kind == "az":
            dy = name[1]
            if name[2] == 4:
                fold_a((zi[4], yi[dy]), [], ("az", dy, 1, 4))
            elif name[2] == 0:
                fold_a((z, yi[dy]), [("az", dy, s, 1) for s in SIGNS])
            else:
                s, d = name[2:]
                fold_a((zi[s * d], yi[dy]), [("az", dy, s, d + 1)], ("az", dy, s, d))
        elif kind == "ay":
            if name[1] == 2 and len(name) == 2:
                fold_a((z, yi[2]), [], ("ay", 1, 2))
            else:
                s = name[1]
                fold_a((z, yi[s]), [("ay", s, 2)], ("ay", s, 1))
        elif kind == "xa":
            fold_a((z, y), [("ay", s, 1) for s in SIGNS])
            fold_a((z, y), [], ("xa",))
        elif kind == "by":
            dz = name[1]
            if len(name) == 4:
                s = name[2]
                fold_b((zi[dz], yi[s]), [("by", dz, s, 2)], ("by", dz, s, 1))
            elif name[2] == 2:
                fold_b((zi[dz], yi[2]), [], ("by", dz, 1, 2))
            else:
                fold_b((zi[dz], y), [("by", dz, s, 1) for s in SIGNS])
        elif kind == "bz":
            if len(name) == 2:
                fold_b((zi[4], y), [], ("bz", 1, 4))
            else:
                s, d = name[1:]
                fold_b((zi[s * d], y), [("bz", s, d + 1)], ("bz", s, d))
        elif kind == "xb":
            fold_b((z, y), [("bz", s, 1) for s in SIGNS])
            fold_b((z, y), [], ("xb",))
        elif kind == "cx":
            send_cx[ORDER.index(name[1])] = p[zi[name[1]], :, other, c_rows].astype(BF)
        elif kind == "cs":
            plane = zi[name[1]]
            arrived = recv_cx[ORDER.index(name[1])].astype(F32)
            p[plane, :, xh, c_rows] = p[plane, :, xh, c_rows] + arrived
        elif kind == "cy":
            g = name[1]
            for j, dz in enumerate(GROUPS[g]):
                if len(name) == 4:
                    s = name[2]
                    got = [(recv_cy.at[g, 2, j], s)]
                    fold_c(zi[dz], yi[s], got, send_cy.at[g, half_of(s), j])
                elif name[2] == 2:
                    fold_c(zi[dz], yi[2], [], send_cy.at[g, 2, j])
                else:
                    fold_c(zi[dz], y, [(recv_cy.at[g, n, j], None) for n in (0, 1)])
        elif kind == "cz":
            if len(name) == 2:
                fold_c(zi[4], y, [], send_cz.at[6])
            else:
                s, d = name[1:]
                n = 6 if d == 3 else d * 2 + half_of(s)
                got = [(recv_cz.at[n], s if d == 3 else None)]
                fold_c(zi[s * d], y, got, send_cz.at[(d - 1) * 2 + half_of(s)])
        elif kind == "xc":
            fold_c(z, y, [(recv_cz.at[n], None) for n in (0, 1)])
            fold_c(z, y, [], send_cz.at[7])
        elif kind == "p8":
            k = name[1]
            if k == 0:
                v16[K - 1, other, pl.ds(0, ROWS_A + ROWS_B)] = q[z, y, other, pl.ds(0, ROWS_A + ROWS_B)]
                v16[K - 1, other, c_rows] = qc[z, y]
            half = pl.ds(256 * (k % 2), 256)
            tokens8[:, half] = per_token(v16[...].reshape(K * 2 * BLK, WID), k // 2, k % 2)
            if k % 2:
                sums = per_example(tokens8[...])
                lane = lax.broadcasted_iota(jnp.int32, (8, 128), 1)
                early[0:8] = early[0:8] + jnp.where(lane // 32 == k // 2, sums, 0.0)
        elif kind == "g1":
            gz[z] = early[...]

    def ring_sum(buf, n, rows=16):
        total = buf[0, 0:rows]
        for k in range(1, n):
            total = total + buf[k, 0:rows]
        return total

    for name in order:
        needs, _, _, sends = tasks[name]
        if name[0] != "start":
            for msg in needs:
                receive(msg)
        work(name)
        for msg in sends:
            send(msg)

    receive(("xa",))
    receive(("xb",))
    receive(("xc",))
    cur[xh, c_rows] = p[z, y, xh, c_rows] * (1.0 / TOKENS)
    cur[other, c_rows] = recv_cz[7].astype(F32) * (1.0 / TOKENS)
    for k in (0, 1):
        cur[k, a_rows] = (p[z, y, k, a_rows] + recv_a[31, k].astype(F32)) * (1.0 / TOKENS)
        cur[k, b_rows] = (p[z, y, k, b_rows] + recv_b[31, k].astype(F32)) * (1.0 / TOKENS)
    mine = cur[xh]
    rows = [jnp.sum(basis_ref[n] * mine, axis=0, keepdims=True) for n in range(K)]
    rows.append(jnp.sum(mine * mine, axis=0, keepdims=True))
    rows.append(jnp.zeros((7, WID), F32))
    sums = jnp.sum(jnp.concatenate(rows, axis=0), axis=1, keepdims=True)
    sub = lax.broadcasted_iota(jnp.int32, (16, 128), 0)
    lane = lax.broadcasted_iota(jnp.int32, (16, 128), 1)
    sums = jnp.sum(jnp.where(sub == lane, sums, 0.0), axis=0, keepdims=True)
    both = cur[...].reshape(2 * BLK, WID)
    high = both.astype(BF)
    pair = jnp.concatenate([high, (both - high.astype(F32)).astype(BF)], axis=0)
    tokens = [jnp.sum(per_token(pair, k), axis=0, keepdims=True) for k in range(4)]
    tokens = jnp.concatenate(tokens + [jnp.zeros((4, 512), F32)], axis=0)
    sub = lax.broadcasted_iota(jnp.int32, (8, 128), 0)
    lane = lax.broadcasted_iota(jnp.int32, (8, 128), 1)
    shown = jnp.where(lane // 32 == sub, per_example(tokens), 0.0)
    shown = jnp.sum(shown, axis=0, keepdims=True)
    hz[z, 0:1] = shown
    hz[z, 1:2] = sums
    for k in FAR:
        send(("g2z", k))
    own_ref[...] = mine
    for k in FAR:
        receive(("g1z", k))
    gy[y] = ring_sum(gz, NZ)
    for k in range(1, NY):
        send(("g1y", k))
    drain = list(started)
    for copy in drain[:-40]:
        copy.wait_send()
    for k in range(1, NZ):
        receive(("g2z", k))
    hw[y * 8 + xh * 4 + xl * 2 + core, 0:2] = ring_sum(hz, NZ, 2)
    for k in WIDE:
        send(("g2w", k))
    for copy in drain[-40:]:
        copy.wait_send()
    for k in range(1, NY):
        receive(("g1y", k))
    gx[xh * 4 + xl * 2 + core] = ring_sum(gy, NY)
    for k in range(1, 8):
        send(("g1x", k))
    for k in range(1, 8):
        receive(("g1x", k))
    first_ref[...] = ring_sum(gx, 8)
    for k in WIDE:
        receive(("g2w", k))
    second_ref[0:2] = ring_sum(hw, 32, 2)
    second_ref[2:8] = jnp.zeros((6, 128), F32)
    for copy in started[len(drain):]:
        copy.wait_send()


def finish(own_ref, first_ref, second_ref, basis_ref, new_ref, hess_ref, proj_ref):
    mean = 1.0 / (FF * D)
    first, second = first_ref[...], second_ref[...]
    sub = lax.broadcasted_iota(jnp.int32, (8, 128), 0)
    lane = lax.broadcasted_iota(jnp.int32, (8, 128), 1)
    row = second[1:2] * mean
    coeff = jnp.sum(jnp.where(sub == lane, row, 0.0), axis=1, keepdims=True)
    squared = jnp.sum(jnp.where(lane[0:1] == K, row, 0.0), axis=1, keepdims=True)
    row = jnp.where(lane[0:1] < K, row, 0.0)
    cross = jnp.sum(coeff * first[8:16], axis=0, keepdims=True) * row
    cross = jnp.sum(cross, axis=1, keepdims=True) * mean
    twice = 2.0 * jnp.sum(row * row, axis=1, keepdims=True)
    beta = jnp.sqrt(jnp.maximum(squared - twice + cross, squared * 1e-12))
    inverse = 1.0 / beta
    hess_ref[...] = jnp.where(lane[0:1] == K, beta, row)[:, 0 : K + 1]
    left = own_ref[...]
    for n in range(K):
        left = left - coeff[n : n + 1] * basis_ref[n]
    new_ref[0] = left * inverse
    last = (second[0:1] - jnp.sum(coeff * first[0:8], axis=0, keepdims=True)) * inverse
    scale = (FF * D) ** (-0.5)
    shown = jnp.concatenate([first[0:8], jnp.broadcast_to(last, (8, 128))], axis=0) * scale
    dp = lax.axis_index("dp")
    for n in range(4):
        @pl.when(dp == n)
        def _():
            proj_ref[...] = shown[0 : K + 1, n * 32 : (n + 1) * 32]


def local(train_hidden, index_hidden, index_resid, basis):
    tasks = build()
    order, _, _ = schedule(tasks)
    messages = [m for name in tasks for m in tasks[name][3]]
    messages += [("g1y", k) for k in range(1, NY)] + [("g1x", k) for k in range(1, 8)]
    messages += [("g2z", k) for k in FAR] + [("g2w", k) for k in WIDE]
    index = {m: n for n, m in enumerate(messages)}
    vmem = pltpu.VMEM
    whole = pl.BlockSpec(memory_space=pltpu.VMEM)
    call = pl.pallas_call(
        functools.partial(kernel, order, tasks, index),
        out_shape=(
            jax.ShapeDtypeStruct((BLK, WID), F32),
            jax.ShapeDtypeStruct((16, 128), F32),
            jax.ShapeDtypeStruct((8, 128), F32),
        ),
        in_specs=[pl.BlockSpec(memory_space=pl.ANY)] * 4,
        out_specs=(whole, whole, whole),
        scratch_shapes=[
            vmem((1024, FF), BF),
            vmem((NZ, NY, 2, BLK, WID), BF),
            vmem((NZ, NY, ROWS_C, WID), BF),
            vmem((1024, NZ * NY * ROWS_C), BF),
            vmem((1280, 128), BF),
            vmem((NZ, NY, 2, BLK, WID), F32),
            vmem((32, 2, ROWS_A, WID), BF),
            vmem((32, 2, ROWS_B, WID), BF),
            vmem((32, 2, ROWS_A, WID), BF),
            vmem((32, 2, ROWS_B, WID), BF),
            vmem((NZ, NY, ROWS_C, WID), BF),
            vmem((NZ, NY, ROWS_C, WID), BF),
            vmem((2, 3, 4, ROWS_C, WID), BF),
            vmem((2, 3, 4, ROWS_C, WID), BF),
            vmem((8, ROWS_C, WID), BF),
            vmem((8, ROWS_C, WID), BF),
            vmem((1024, WID), F32),
            vmem((1024, WID), BF),
            vmem((NZ, NY, 64, WID), BF),
            vmem((K, 2, BLK, WID), BF),
            vmem((2, 2, 2, BLK, WID), BF),
            vmem((2, BLK, WID), BF),
            vmem((2, BLK, WID), F32),
            vmem((16, 128), F32),
            vmem((8, 512), F32),
            vmem((K, BLK, WID), F32),
            vmem((BLK, 1024), BF),
            vmem((64, WID), BF),
            vmem((NZ, 16, 128), F32),
            vmem((NY, 16, 128), F32),
            vmem((8, 16, 128), F32),
            vmem((NZ, 8, 128), F32),
            vmem((32, 8, 128), F32),
            pltpu.SemaphoreType.DMA((5,)),
            pltpu.SemaphoreType.DMA((len(messages),)),
            pltpu.SemaphoreType.DMA((len(messages),)),
        ],
        compiler_params=pltpu.CompilerParams(
            collective_id=0, has_side_effects=True, vmem_limit_bytes=60 * 2**20
        ),
        cost_estimate=pl.CostEstimate(
            flops=14 * 10**9, bytes_accessed=13 * 10**6, transcendentals=0
        ),
        name="arnoldi",
    )
    own, first, second = call(train_hidden, index_hidden.T, index_resid, basis)
    new, hess, proj = pl.pallas_call(
        finish,
        out_shape=(
            jax.ShapeDtypeStruct((1, BLK, WID), F32),
            jax.ShapeDtypeStruct((1, K + 1), F32),
            jax.ShapeDtypeStruct((K + 1, 32), F32),
        ),
        in_specs=[whole] * 4,
        out_specs=(whole, whole, whole),
        name="finish",
    )(own, first, second, basis)
    return new, hess, proj.T


def solution(mesh):
    in_specs = (P("fsdp", None), P("dp", "fsdp"), P("fsdp", "dp"), P(None, "fsdp", "dp"))
    out_specs = (P(None, "fsdp", "dp"), P(), P("dp", None))
    return jax.shard_map(local, mesh=mesh, in_specs=in_specs, out_specs=out_specs, check_vma=False)
```

```python
import functools

import jax
import jax.numpy as jnp
from jax import lax
from jax.experimental import pallas as pl
from jax.experimental.pallas import tpu as pltpu
from jax.sharding import PartitionSpec as P

D = 2048
FF = 5120
TOKENS = 65536
EX_TOK = 32
K = 8
NZ, NY = 8, 4
BLK = 80
WID = 512
ROWS_A, ROWS_B, ROWS_C = 32, 32, 16
MESH = pl.DeviceIdType.MESH
BF = jnp.bfloat16
F32 = jnp.float32
SIGNS = (1, -1)
FAR = (4, 3, 5, 2, 6, 1, 7)
WIDE = sorted(
    range(1, 32), key=lambda k: -(min(k // 8, 4 - k // 8) + (0, 1, 2, 1)[(k >> 1) & 3]) * 2 - (k & 1)
)


def half_of(sign):
    return 0 if sign > 0 else 1


def wrap(delta, size):
    delta %= size
    return delta - size if delta > size // 2 else delta


def parts_of(kind, hop, own):
    if hop == 1 and own:
        return ("o", "t")
    return ("f",)


def link_of(msg):
    kind = msg[0]
    if kind in ("Az", "az"):
        return ("z", msg[2])
    if kind in ("Ay", "ay", "Ry", "RY", "Cy"):
        return ("y", msg[1])
    if kind == "cz":
        return ("z", 1 if msg[1] < 4 else -1)
    if kind in ("Bz", "bz", "Rz", "RZ", "Cz"):
        return ("z", msg[1])
    if kind in ("By", "by", "cy"):
        return ("y", msg[2])
    if kind in ("qx", "vx", "hx", "xa", "xb", "xc", "hl", "Cx", "cx"):
        return ("x", 0)
    return ("c", 0) if kind == "hc" else (kind, msg[1])


def kilobytes(msg):
    kind = msg[0]
    a, b = 2 * ROWS_A, 2 * ROWS_B
    if kind == "Ay":
        return a / 2 if msg[3] in ("o", "t") or msg[2] == 2 else a
    if kind == "Az":
        return a / 2 if msg[4] in ("o", "t") or msg[3] == 4 else a
    if kind == "Bz":
        return b / 2 if msg[3] in ("o", "t") or msg[2] == 4 else b
    if kind == "By":
        return b / 2 if msg[4] in ("o", "t") or msg[3] == 2 else b
    if kind == "az":
        return a / 2 if msg[3] == 4 else a
    if kind == "ay":
        return a / 2 if msg[2] == 2 else a
    if kind == "bz":
        return b / 2 if msg[2] == 4 else b
    if kind == "by":
        return b / 2 if msg[3] == 2 else b
    if kind in ("Ry", "Rz", "RZ", "RY", "Cz", "Cy"):
        full = {"Ry": 16, "Rz": 48, "RZ": 64, "RY": 384, "Cz": ROWS_C, "Cy": 8 * ROWS_C}[kind]
        return full / 2 if msg[2] == (4 if kind[1] in "zZ" else 2) else full
    if kind == "cz":
        return 2 * ROWS_C
    if kind == "cy":
        return 2 * ROWS_C if msg[3] == 2 else 4 * ROWS_C
    if kind in ("Cx", "cx"):
        return (8 if kind == "Cx" else 4) * ROWS_C
    return {"qx": 64, "xc": ROWS_C, "vx": 560, "hx": 80, "hl": 160, "hc": 320, "xa": a, "xb": b}.get(kind, 8)


def build():
    tasks = {}

    def task(name, needs=(), after=(), cost=0.0, sends=()):
        needs, sends = list(needs), list(sends)
        tasks[name] = (needs, list(after), cost + 0.01 * (len(needs) + len(sends)), sends)

    first = []
    for s in SIGNS:
        first += [("Bz", s, 1), ("Ay", s, 1)]
    for s in SIGNS:
        first += [("Az", 0, s, 1), ("By", 0, s, 1)]
    task(
        ("start",),
        cost=0.5,
        sends=[("qx",)] + [("Cz", s, 1) for s in SIGNS] + [m + ("o",) for m in first]
        + [("Rz", s, 1) for s in SIGNS] + [("Ry", s, 1) for s in SIGNS],
    )
    task(("qx",), [("qx",)], [("start",)], sends=[m + ("t",) for m in first])
    for s in SIGNS:
        task(
            ("Ay", s),
            [("Ay", s, 1, "o"), ("Ay", s, 1, "t")],
            [("qx",)],
            sends=[("Ay", s, 2, "f")] + [("Az", wrap(-s, NY), u, 1, "f") for u in SIGNS],
        )
    task(
        ("Ay2",),
        [("Ay", s, 2, "f") for s in SIGNS],
        [("Ay", s) for s in SIGNS],
        sends=[("Az", 2, u, 1, "f") for u in SIGNS],
    )
    for dy in (0, 1, -1, 2):
        for s in SIGNS:
            for h in (1, 2, 3):
                task(
                    ("Az", dy, s, h),
                    [("Az", dy, s, h, p) for p in parts_of("Az", h, dy == 0)],
                    sends=[("Az", dy, s, h + 1, "f")],
                )
    for s in SIGNS:
        for h in (1, 2, 3):
            task(
                ("Bz", s, h),
                [("Bz", s, h, p) for p in parts_of("Bz", h, True)],
                sends=[("Bz", s, h + 1, "f")] + [("By", wrap(-s * h, NZ), u, 1, "f") for u in SIGNS],
            )
    task(
        ("Bz4",), [("Bz", s, 4, "f") for s in SIGNS], sends=[("By", 4, u, 1, "f") for u in SIGNS]
    )
    for dz in range(-3, 5):
        for s in SIGNS:
            task(
                ("By", dz, s),
                [("By", dz, s, 1, p) for p in parts_of("By", 1, dz == 0)],
                sends=[("By", dz, s, 2, "f")],
            )
    for s in SIGNS:
        for h in (1, 2, 3):
            task(("Cz", s, h), [("Cz", s, h)], sends=[("Cz", s, h + 1)])
        task(("Cy", s), [("Cy", s, 1)], sends=[("Cx", wrap(-s, NY)), ("Cy", s, 2)])
    task(
        ("CY0",),
        [("Cz", s, 4) for s in SIGNS],
        [("Cz", s, h) for s in SIGNS for h in (1, 2, 3)],
        sends=[("Cx", 0)] + [("Cy", s, 1) for s in SIGNS],
    )
    task(("Cy2",), [("Cy", s, 2) for s in SIGNS], [("Cy", s) for s in SIGNS], sends=[("Cx", 2)])
    late = {
        0: [],
        1: [("Bz4",)],
        2: [("Az", dy, s, 2) for dy in (0, 1, -1, 2) for s in SIGNS],
        3: [("Az", dy, s, 3) for dy in (0, 1, -1, 2) for s in SIGNS]
        + [("By", dz, s) for dz in range(-3, 5) for s in SIGNS],
    }[LATE]
    for s in SIGNS:
        task(("Ry", s), [("Ry", s, 1)], sends=[("Ry", s, 2)])
        for h in (1, 2, 3):
            task(("Rz", s, h), [("Rz", s, h)], sends=[("Rz", s, h + 1)])
            task(("RZ", s, h), [("RZ", s, h)], sends=[("RZ", s, h + 1)])
        task(("RY", s), [("RY", s, 1)], sends=[("RY", s, 2)])
    task(
        ("RZ0",),
        [("Ry", s, 2) for s in SIGNS],
        [("Ry", s) for s in SIGNS] + late,
        sends=[("RZ", s, 1) for s in SIGNS],
    )
    task(
        ("RY0",),
        [("Rz", s, 4) for s in SIGNS],
        [("Rz", s, h) for s in SIGNS for h in (1, 2, 3)] + late,
        sends=[("RY", s, 1) for s in SIGNS],
    )
    task(("vx",), after=[("start",)], cost=0.25, sends=[("vx",)])
    task(("hx",), after=[("vx",)], cost=0.25, sends=[("hx",)])
    task(("hl",), [("hx",)], [("hx",), ("Cy2",)], sends=[("hl",)])
    task(("hc",), [("hl",)], [("hl",)], sends=[("hc",)])
    task(("gram",), after=[("vx",)], cost=0.8)
    for g, planes in enumerate(PLANES):
        needs, after = [], [("m1", g - 1)] if g else [("load",), ("CY0",), ("Cy2",)]
        if g == len(PLANES) - 1:
            after.append(("m1c",))
        for dz in planes:
            for s in SIGNS:
                needs.append(("By", dz, s, 2, "f"))
                after.append(("By", dz, s))
            if dz == 0:
                after += [("Ay", s) for s in SIGNS] + [("Ay2",)]
            elif dz == 4:
                needs += [("Az", dy, s, 4, "f") for dy in (0, 1, -1, 2) for s in SIGNS]
                after.append(("Bz4",))
            else:
                s = -1 if dz > 0 else 1
                after += [("Az", dy, s, abs(dz)) for dy in (0, 1, -1, 2)] + [("Bz", s, abs(dz))]
        task(("m1", g), needs, after, cost=1.1 * len(planes))
    task(("load",), after=[("start",)], cost=0.1)
    for k in range(4):
        task(("xs", k), after=[("load",)] + ([("xs", k - 1)] if k else []), cost=0.7)
    task(
        ("m1c",),
        [("Cx", dy) for dy in (0, 1, -1, 2)],
        [("CY0",), ("Cy2",), ("m1", 0), ("xs", 3)],
        cost=0.9,
    )
    task(("img",), after=[("m1", len(PLANES) - 1)], cost=0.0)
    for n, dz in enumerate(ORDER):
        task(("m2", dz), after=[("img",)] + ([("m2", ORDER[n - 1])] if n else []), cost=0.95)
    for dy in (0, 1, -1, 2):
        task(("az", dy, 4), after=[("m2", 4)], cost=0.04, sends=[("az", dy, s, 4) for s in SIGNS])
        for s in SIGNS:
            for d in (3, 2, 1):
                task(
                    ("az", dy, s, d),
                    [("az", dy, s, d + 1)],
                    [("m2", s * d)],
                    cost=0.04,
                    sends=[("az", dy, s, d)],
                )
        task(("az", dy, 0), [("az", dy, s, 1) for s in SIGNS], [("m2", 0)], cost=0.04)
    task(("ay", 2), after=[("az", 2, 0)], cost=0.04, sends=[("ay", s, 2) for s in SIGNS])
    for s in SIGNS:
        task(("ay", s, 1), [("ay", s, 2)], [("az", s, 0)], cost=0.04, sends=[("ay", s, 1)])
    task(
        ("xa",), [("ay", s, 1) for s in SIGNS], [("az", 0, 0)], cost=0.04, sends=[("xa",)]
    )
    for dz in range(-3, 5):
        task(("by", dz, 2), after=[("m2", dz)], cost=0.04, sends=[("by", dz, s, 2) for s in SIGNS])
        for s in SIGNS:
            task(
                ("by", dz, s, 1),
                [("by", dz, s, 2)],
                [("m2", dz)],
                cost=0.04,
                sends=[("by", dz, s, 1)],
            )
        task(("by", dz, 0), [("by", dz, s, 1) for s in SIGNS], [("m2", dz)], cost=0.06)
    task(("bz", 4), after=[("by", 4, 0)], cost=0.04, sends=[("bz", s, 4) for s in SIGNS])
    for s in SIGNS:
        for d in (3, 2, 1):
            task(
                ("bz", s, d),
                [("bz", s, d + 1)],
                [("by", s * d, 0)],
                cost=0.04,
                sends=[("bz", s, d)],
            )
    task(("xb",), [("bz", s, 1) for s in SIGNS], [("by", 0, 0)], cost=0.06, sends=[("xb",)])
    for n, dz in enumerate(ORDER):
        task(("cx", dz), after=[("m2", dz)], cost=0.04, sends=[("cx", dz)])
        task(("cs", dz), [("cx", dz)], [("m2", dz)], cost=0.04)
    for g in (0, 1):
        done = [("cs", dz) for dz in GROUPS[g]]
        task(("cy", g, 2), after=done, cost=0.04, sends=[("cy", g, s, 2) for s in SIGNS])
        for s in SIGNS:
            task(("cy", g, s, 1), [("cy", g, s, 2)], done, cost=0.04, sends=[("cy", g, s, 1)])
        task(("cy", g, 0), [("cy", g, s, 1) for s in SIGNS], done, cost=0.04)
    for g in (0, 1):
        sends = [("cz", dz % NZ) for dz in GROUPS[g] if dz]
        task(("cz", g), after=[("cy", g, 0)], cost=0.05, sends=sends)
    task(("xc",), [("cz", k) for k in FAR], [("cy", 1, 0)], cost=0.05, sends=[("xc",)])
    for k in range(8):
        needs, after = [], [("m2", ORDER[-1])]
        if k == 0:
            needs += [("RZ", s, 4) for s in SIGNS] + [("RY", s, 2) for s in SIGNS]
            needs += [("hc",), ("vx",)]
            after += [("RZ", s, h) for s in SIGNS for h in (1, 2, 3)] + [("RY", s) for s in SIGNS]
            after += [("RZ0",), ("RY0",), ("hc",), ("vx",), ("gram",)]
        else:
            after += [("p8", k - 1)]
        task(("p8", k), needs, after, cost=0.65)
    task(("g1",), after=[("p8", 7)], cost=0.1, sends=[("g1z", k) for k in FAR])
    return tasks


PLANES = ((0,), (1, -1), (2, -2), (3, -3), (4,))
ORDER = (4, 3, -3, 2, -2, 1, -1, 0)
LATE, RATE, DELAY, CLS = 1, 46.0, 2.5, True
SLACK = {"Ry": 1.0, "Rz": 1.0, "RZ": 1.5, "RY": 1.5, "vx": 2.0, "hx": 2.0, "hl": 2.0, "hc": 2.0}
GROUPS = (ORDER[:4], ORDER[4:])


def schedule(tasks):
    rate = {"z": RATE, "y": RATE, "x": RATE - 1, "c": 400.0}
    delay = {"z": DELAY, "y": DELAY, "x": DELAY + 0.5, "c": 0.8}
    waits = {}
    followers = {name: [] for name in tasks}
    for name, (needs, after, _, _) in tasks.items():
        for msg in needs:
            waits.setdefault(msg, []).append(name)
        for other in after:
            followers[other].append(name)

    def cost_of(msg):
        axis = link_of(msg)[0]
        return kilobytes(msg) / rate.get(axis, 40.0) + delay.get(axis, 3.0)

    @functools.cache
    def rank(name):
        _, _, cost, sends = tasks[name]
        rest = [rank(f) for f in followers[name]]
        rest += [cost_of(m) + max([rank(w) for w in waits.get(m, ())], default=0) for m in sends]
        return cost + max(rest, default=0)

    now, free, arrives, done, order = 0.0, {}, {}, {}, []
    left = dict(tasks)
    while left:
        ready, soonest = [], None
        for name, (needs, after, cost, sends) in left.items():
            if any(a not in done for a in after) or any(m not in arrives for m in needs):
                continue
            at = max([arrives[m] for m in needs], default=0.0)
            if at <= now:
                heavy = CLS and cost >= 0.3 and not sends
                ready.append((heavy, -rank(name), at, name))
            else:
                soonest = at if soonest is None else min(soonest, at)
        if not ready:
            now = soonest
            continue
        name = min(ready, key=lambda r: r[:3])[3]
        _, _, cost, sends = left.pop(name)
        now += cost
        done[name] = now
        order.append(name)
        for msg in sends:
            link = link_of(msg)
            axis = link[0]
            begin = max(now, free.get(link, 0.0))
            free[link] = begin + kilobytes(msg) / rate.get(axis, 40.0)
            arrives[msg] = free[link] + delay.get(axis, 3.0) + SLACK.get(msg[0], 0.0)
    return order, done, arrives


def product(a, b, ca, cb):
    return lax.dot_general(a, b, (((ca,), (cb,)), ((), ())), preferred_element_type=F32)


def kernel(
    order, tasks, index,
    x_hbm, hid_hbm, res_hbm, basis_hbm,
    own_ref, first_ref, second_ref,
    xv, q, qc, xc, select, p, send_a, send_b, recv_a, recv_b,
    send_cx, recv_cx, send_cy, recv_cy, send_cz, recv_cz, acc, img, r, v16, ht, hs, cur,
    early, tokens8, basis_ref, hid_ref, res_ref, gz, gy, gx, hz, hw, load_sem, send_sem, recv_sem,
):
    dp, fs = lax.axis_index("dp"), lax.axis_index("fsdp")
    z, y, xh = fs // 8, lax.rem(fs // 2, 4), lax.rem(fs, 2)
    xl, core = dp // 2, lax.rem(dp, 2)
    other = 1 - xh

    zi = {d: lax.rem(z + (d + NZ), NZ) for d in range(-3, 8)}
    zi[-4] = zi[4]
    yi = {d: lax.rem(y + (d + NY), NY) for d in range(-1, 4)}
    yi[-2] = yi[2]

    def fsdp(za, ya, xa):
        return (za * NY + ya) * 2 + xa

    def along_z(d):
        return (dp, fsdp(zi[d], y, xh))

    def along_y(d):
        return (dp, fsdp(z, yi[d], xh))

    def along_x(k):
        xa = 1 - xh if k & 4 else xh
        la = 1 - xl if k & 2 else xl
        ca = 1 - core if k & 1 else core
        return (la * 2 + ca, fsdp(z, y, xa))

    def along_w(k):
        bits = k & 7
        xa = 1 - xh if bits & 4 else xh
        la = 1 - xl if bits & 2 else xl
        ca = 1 - core if bits & 1 else core
        return (la * 2 + ca, fsdp(z, yi[k // 8], xa))

    partners = [along_z(d) for d in FAR] + [along_w(k) for k in WIDE]

    barrier = pltpu.get_barrier_semaphore()
    loads = [
        pltpu.make_async_copy(basis_hbm.at[K - 1], basis_ref.at[K - 1], load_sem.at[0]),
        pltpu.make_async_copy(res_hbm, res_ref, load_sem.at[1]),
        pltpu.make_async_copy(hid_hbm, hid_ref, load_sem.at[2]),
        pltpu.make_async_copy(
            basis_hbm.at[pl.ds(0, K - 1)], basis_ref.at[pl.ds(0, K - 1)], load_sem.at[3]
        ),
        pltpu.make_async_copy(x_hbm, xv, load_sem.at[4]),
    ]
    for load in loads:
        load.start()
    for device in partners:
        pl.semaphore_signal(barrier, inc=1, device_id=device, device_id_type=MESH)
    loads[0].wait()
    loads[1].wait()
    q[:, :, other, pl.ds(ROWS_A + ROWS_B, ROWS_C)] = jnp.zeros((NZ, NY, ROWS_C, WID), BF)
    narrow = basis_ref[K - 1].astype(BF)
    q[z, y, xh] = narrow
    v16[K - 1, xh] = narrow
    r[z, y] = res_ref[...]

    def q_part(rows, part, oz, oy):
        at = q.at[zi[oz], yi[oy]]
        which = {"f": slice(None), "o": xh, "t": other}.get(part, part)
        return at.at[which, rows]

    a_rows, b_rows = pl.ds(0, ROWS_A), pl.ds(ROWS_A, ROWS_B)
    c_rows = pl.ds(ROWS_A + ROWS_B, ROWS_C)

    def lane_half(sign):
        return pl.ds(half_of(sign) * (WID // 2), WID // 2)

    def slot_a(msg):
        if msg[0] == "az":
            _, dy, s, d = msg
            base = {0: 0, 1: 7, -1: 14, 2: 21}[dy]
            return base + (6 if d == 4 else (d - 1) * 2 + half_of(s)), d == 4, s
        if msg[0] == "ay":
            _, s, d = msg
            return 28 + (2 if d == 2 else half_of(s)), d == 2, s
        return 31, False, 1

    def slot_b(msg):
        if msg[0] == "by":
            _, dz, s, d = msg
            return (dz + 3) * 3 + (2 if d == 2 else half_of(s)), d == 2, s
        if msg[0] == "bz":
            _, s, d = msg
            return 24 + (6 if d == 4 else (d - 1) * 2 + half_of(s)), d == 4, s
        return 31, False, 1

    def piece(buf, slot):
        n, halved, s = slot
        return buf.at[n, half_of(s)] if halved else buf.at[n]

    def place(msg):
        kind = msg[0]
        if kind == "qx":
            rows = pl.ds(0, ROWS_A + ROWS_B)
            here = q.at[z, y, xh, rows]
            return here, here, q.at[z, y, other, rows], along_x(4)
        if kind == "Cz":
            _, s, h = msg
            lanes = lane_half(s) if h == 4 else slice(None)
            here = q.at[zi[wrap(-s * (h - 1), NZ)], y, xh, c_rows, lanes]
            return here, here, q.at[zi[wrap(-s * h, NZ)], y, xh, c_rows, lanes], along_z(s)
        if kind == "Cy":
            _, s, h = msg
            lanes = lane_half(s) if h == 2 else slice(None)
            here = q.at[:, yi[wrap(-s * (h - 1), NY)], xh, c_rows, lanes]
            return here, here, q.at[:, yi[wrap(-s * h, NY)], xh, c_rows, lanes], along_y(s)
        if kind == "Cx":
            lands = qc.at[:, yi[msg[1]]]
            return q.at[:, yi[msg[1]], xh, c_rows], lands, lands, along_x(4)
        if kind == "cx":
            n = ORDER.index(msg[1])
            return send_cx.at[n], recv_cx.at[n], recv_cx.at[n], along_x(4)
        if kind == "cy":
            _, g, s, d = msg
            n, lanes = (2, lane_half(s)) if d == 2 else (half_of(s), slice(None))
            target = recv_cy.at[g, n, :, :, lanes]
            return send_cy.at[g, n, :, :, lanes], target, target, along_y(s)
        if kind == "cz":
            n = msg[1]
            return send_cz.at[n], recv_cz.at[n], recv_cz.at[n], along_z(n)
        if kind == "xc":
            return send_cz.at[0], recv_cz.at[0], recv_cz.at[0], along_x(4)
        if kind in ("Ay", "Az", "Bz", "By"):
            rows = a_rows if kind[0] == "A" else b_rows
            if kind in ("Ay", "Bz"):
                _, s, h, part = msg
            else:
                _, off, s, h, part = msg
            size = NZ if kind[1] == "z" else NY
            if h == size // 2:
                part = half_of(s)
            if kind[1] == "y":
                oz = off if kind == "By" else 0
                here = q_part(rows, part, oz, wrap(-s * (h - 1), NY))
                there = q_part(rows, part, oz, wrap(-s * h, NY))
                return here, here, there, along_y(s)
            oy = off if kind == "Az" else 0
            here = q_part(rows, part, wrap(-s * (h - 1), NZ), oy)
            there = q_part(rows, part, wrap(-s * h, NZ), oy)
            return here, here, there, along_z(s)
        if kind in ("Ry", "RZ", "Rz", "RY"):
            _, s, h = msg
            last = h == (NY if kind[1] in "yY" else NZ) // 2
            rows = pl.ds(0, 16) if kind in ("Ry", "RZ") else pl.ds(16, 48)
            lanes = lane_half(s) if last else slice(None)
            n = NY if kind[1] in "yY" else NZ
            a, b = wrap(-s * (h - 1), n), wrap(-s * h, n)
            if kind == "Ry":
                here, there = r.at[z, yi[a], rows, lanes], r.at[z, yi[b], rows, lanes]
            elif kind == "Rz":
                here, there = r.at[zi[a], y, rows, lanes], r.at[zi[b], y, rows, lanes]
            elif kind == "RZ":
                here, there = r.at[zi[a], :, rows, lanes], r.at[zi[b], :, rows, lanes]
            else:
                here, there = r.at[:, yi[a], rows, lanes], r.at[:, yi[b], rows, lanes]
            return here, here, there, along_y(s) if n == NY else along_z(s)
        if kind == "vx":
            here = v16.at[pl.ds(0, K - 1), xh]
            return here, here, v16.at[pl.ds(0, K - 1), other], along_x(4)
        if kind == "hx":
            return hs.at[other], ht.at[xl, core, xh], ht.at[xl, core, other], along_x(4)
        if kind == "hl":
            here = ht.at[xl, core]
            return here, here, ht.at[1 - xl, core], along_x(2)
        if kind == "hc":
            here = ht.at[:, core]
            return here, here, ht.at[:, 1 - core], along_x(1)
        if kind in ("az", "ay", "xa"):
            slot = slot_a(msg)
            target = piece(recv_a, slot)
            src = piece(send_a, slot)
        elif kind in ("by", "bz", "xb"):
            slot = slot_b(msg)
            target = piece(recv_b, slot)
            src = piece(send_b, slot)
        if kind in ("xa", "xb"):
            return src, target, target, along_x(4)
        if kind in ("az", "by"):
            return src, target, target, along_z(msg[2]) if kind == "az" else along_y(msg[2])
        if kind in ("ay", "bz"):
            return src, target, target, along_y(msg[1]) if kind == "ay" else along_z(msg[1])
        k = msg[1]
        if kind == "g1z":
            here = gz.at[z]
            return here, here, gz.at[zi[-k + NZ if k > 3 else -k]], along_z(k)
        if kind == "g1y":
            here = gy.at[y]
            return here, here, gy.at[yi[-k + NY if k > 1 else -k]], along_y(k)
        if kind == "g2z":
            here = hz.at[z, pl.ds(0, 2)]
            return here, here, hz.at[zi[-k + NZ if k > 3 else -k], pl.ds(0, 2)], along_z(k)
        xa = 1 - xh if k & 4 else xh
        la = 1 - xl if k & 2 else xl
        ca = 1 - core if k & 1 else core
        mine, theirs = xh * 4 + xl * 2 + core, xa * 4 + la * 2 + ca
        if kind == "g1x":
            return gx.at[mine], gx.at[mine], gx.at[theirs], along_x(k)
        d = k // 8
        here = hw.at[y * 8 + mine, pl.ds(0, 2)]
        lands = hw.at[yi[-d + NY if d > 1 else -d] * 8 + theirs, pl.ds(0, 2)]
        return here, here, lands, along_w(k)

    started = []

    def send(msg):
        src, target, _, device = place(msg)
        n = index[msg]
        copy = pltpu.make_async_remote_copy(
            src_ref=src, dst_ref=target, send_sem=send_sem.at[n], recv_sem=recv_sem.at[n],
            device_id=device, device_id_type=MESH,
        )
        copy.start()
        started.append(copy)

    def receive(msg):
        _, _, lands, device = place(msg)
        n = index[msg]
        pltpu.make_async_remote_copy(
            src_ref=lands, dst_ref=lands, send_sem=send_sem.at[n], recv_sem=recv_sem.at[n],
            device_id=device, device_id_type=MESH,
        ).wait_recv()

    def fold(rows, buf, where, slots, out):
        for k in (0, 1):
            total = p[where[0], where[1], k, rows]
            for n, halved, s in slots:
                if not halved or half_of(s) == k:
                    total = total + buf[n, k].astype(F32)
            if out is None:
                p[where[0], where[1], k, rows] = total
            else:
                out[0][out[1], k] = total.astype(BF)

    def fold_a(where, msgs, out=None):
        fold(a_rows, recv_a, where, [slot_a(m) for m in msgs], out and (send_a, slot_a(out)[0]))

    def fold_b(where, msgs, out=None):
        fold(b_rows, recv_b, where, [slot_b(m) for m in msgs], out and (send_b, slot_b(out)[0]))

    def fold_c(plane, row, arrived, out=None):
        for h in (0, 1):
            lanes = pl.ds(h * (WID // 2), WID // 2)
            total = p[plane, row, xh, c_rows, lanes]
            for ref, s in arrived:
                if s is None or half_of(s) == h:
                    total = total + ref[:, lanes].astype(F32)
            if out is None:
                p[plane, row, xh, c_rows, lanes] = total
            else:
                out[:, lanes] = total.astype(BF)

    def lanes_of(plane):
        return pl.ds(pl.multiple_of(plane * (NY * 2 * BLK), 128), NY * 2 * BLK)

    def per_token(rows, k, part=None):
        if part is None:
            many, errors, hidden = 512, r[2 * k : 2 * k + 2], ht[k // 2, k % 2]
        else:
            many, errors = 256, r[2 * k + part]
            hidden = ht[k // 2, k % 2, :, :, 256 * part : 256 * (part + 1)]
        mapped = product(rows, errors.reshape(many, WID), 1, 1)
        n = rows.shape[0] // (2 * BLK)
        hidden = hidden.reshape(2 * BLK, many).astype(F32)
        return jnp.sum(mapped.reshape(n, 2 * BLK, many) * hidden[None], axis=1)

    def per_example(tokens):
        t = lax.broadcasted_iota(jnp.int32, (512, 128), 0)
        e = lax.broadcasted_iota(jnp.int32, (512, 128), 1)
        owner = (t // 64) * 4 + 2 * xh + lax.rem(t, 64) // EX_TOK
        marks = jnp.where(owner == lax.rem(e, 32), 1.0, 0.0).astype(BF)
        terms, rest = [], tokens
        for _ in range(3):
            terms.append(rest.astype(BF).astype(F32))
            rest = rest - terms[-1]
        sums = product(jnp.concatenate(terms, axis=0).astype(BF), marks, 1, 0)
        return sums[0:8] + sums[8:16] + sums[16:24]

    def work(name):
        kind = name[0]
        if kind == "start":
            pl.semaphore_wait(barrier, len(partners))
        elif kind == "vx":
            loads[3].wait()
            for n in range(K - 1):
                v16[n, xh] = basis_ref[n].astype(BF)
        elif kind == "hx":
            loads[2].wait()
            for which in (0, 1):
                cuts = [(2 * n + which) * 64 for n in range(8)]
                pieces = [hid_ref[:, at : at + 64] for at in cuts]
                hs[which] = jnp.concatenate(pieces, axis=1)
            ht[xl, core, xh] = hs[xh]
        elif kind == "gram":
            lane = lax.broadcasted_iota(jnp.int32, (8, 128), 1)
            table = jnp.zeros((8, 128), F32)
            for i in range(K):
                rows = [jnp.sum(basis_ref[j] * basis_ref[i], axis=0, keepdims=True) for j in range(K)]
                column = jnp.sum(jnp.concatenate(rows, axis=0), axis=1, keepdims=True)
                table = table + jnp.where(lane == i, column, 0.0)
            early[8:16] = table
            early[0:8] = jnp.zeros((8, 128), F32)
        elif kind == "load":
            loads[4].wait()
        elif kind == "m1":
            total = None
            for dz in PLANES[name[1]]:
                term = product(xv[:, lanes_of(zi[dz])], q[zi[dz]].reshape(NY * 2 * BLK, WID), 1, 0)
                total = term if total is None else total + term
            if name[1] == len(PLANES) - 1:
                img[...] = (acc[...] + total).astype(BF)
            else:
                acc[...] = total if name[1] == 0 else acc[...] + total
        elif kind == "xs":
            k = name[1]
            if k == 0:
                f = lax.broadcasted_iota(jnp.int32, (1280, 128), 0)
                at = lax.broadcasted_iota(jnp.int32, (1280, 128), 1)
                block = (f * 52429) >> 22
                inside = f - block * BLK - (ROWS_A + ROWS_B)
                hit = (inside >= 0) & ((block & 1) == other) & ((block >> 1) * ROWS_C + inside == at)
                select[...] = jnp.where(hit, 1.0, 0.0).astype(BF)
            columns = xv[:, 1280 * k : 1280 * (k + 1)]
            xc[:, 128 * k : 128 * (k + 1)] = product(columns, select[...], 1, 0).astype(BF)
        elif kind == "m1c":
            acc[...] = acc[...] + product(xc[...], qc[...].reshape(NZ * NY * ROWS_C, WID), 1, 0)
        elif kind == "img":
            pass
        elif kind == "m2":
            plane = zi[name[1]]
            p[plane] = product(xv[:, lanes_of(plane)], img[...], 0, 0).reshape(NY, 2, BLK, WID)
        elif kind == "az":
            dy = name[1]
            if name[2] == 4:
                fold_a((zi[4], yi[dy]), [], ("az", dy, 1, 4))
            elif name[2] == 0:
                fold_a((z, yi[dy]), [("az", dy, s, 1) for s in SIGNS])
            else:
                s, d = name[2:]
                fold_a((zi[s * d], yi[dy]), [("az", dy, s, d + 1)], ("az", dy, s, d))
        elif kind == "ay":
            if name[1] == 2 and len(name) == 2:
                fold_a((z, yi[2]), [], ("ay", 1, 2))
            else:
                s = name[1]
                fold_a((z, yi[s]), [("ay", s, 2)], ("ay", s, 1))
        elif kind == "xa":
            fold_a((z, y), [("ay", s, 1) for s in SIGNS])
            fold_a((z, y), [], ("xa",))
        elif kind == "by":
            dz = name[1]
            if len(name) == 4:
                s = name[2]
                fold_b((zi[dz], yi[s]), [("by", dz, s, 2)], ("by", dz, s, 1))
            elif name[2] == 2:
                fold_b((zi[dz], yi[2]), [], ("by", dz, 1, 2))
            else:
                fold_b((zi[dz], y), [("by", dz, s, 1) for s in SIGNS])
        elif kind == "bz":
            if len(name) == 2:
                fold_b((zi[4], y), [], ("bz", 1, 4))
            else:
                s, d = name[1:]
                fold_b((zi[s * d], y), [("bz", s, d + 1)], ("bz", s, d))
        elif kind == "xb":
            fold_b((z, y), [("bz", s, 1) for s in SIGNS])
            fold_b((z, y), [], ("xb",))
        elif kind == "cx":
            send_cx[ORDER.index(name[1])] = p[zi[name[1]], :, other, c_rows].astype(BF)
        elif kind == "cs":
            plane = zi[name[1]]
            arrived = recv_cx[ORDER.index(name[1])].astype(F32)
            p[plane, :, xh, c_rows] = p[plane, :, xh, c_rows] + arrived
        elif kind == "cy":
            g = name[1]
            for j, dz in enumerate(GROUPS[g]):
                if len(name) == 4:
                    s = name[2]
                    got = [(recv_cy.at[g, 2, j], s)]
                    fold_c(zi[dz], yi[s], got, send_cy.at[g, half_of(s), j])
                elif name[2] == 2:
                    fold_c(zi[dz], yi[2], [], send_cy.at[g, 2, j])
                else:
                    fold_c(zi[dz], y, [(recv_cy.at[g, n, j], None) for n in (0, 1)])
        elif kind == "cz":
            for dz in GROUPS[name[1]]:
                if dz:
                    fold_c(zi[dz], y, [], send_cz.at[dz % NZ])
        elif kind == "xc":
            fold_c(z, y, [(recv_cz.at[n], None) for n in range(1, NZ)])
            fold_c(z, y, [], send_cz.at[0])
        elif kind == "p8":
            k = name[1]
            if k == 0:
                v16[K - 1, other, pl.ds(0, ROWS_A + ROWS_B)] = q[z, y, other, pl.ds(0, ROWS_A + ROWS_B)]
                v16[K - 1, other, c_rows] = qc[z, y]
            half = pl.ds(256 * (k % 2), 256)
            tokens8[:, half] = per_token(v16[...].reshape(K * 2 * BLK, WID), k // 2, k % 2)
            if k % 2:
                sums = per_example(tokens8[...])
                lane = lax.broadcasted_iota(jnp.int32, (8, 128), 1)
                early[0:8] = early[0:8] + jnp.where(lane // 32 == k // 2, sums, 0.0)
        elif kind == "g1":
            gz[z] = early[...]

    def ring_sum(buf, n, rows=16):
        total = buf[0, 0:rows]
        for k in range(1, n):
            total = total + buf[k, 0:rows]
        return total

    for name in order:
        needs, _, _, sends = tasks[name]
        if name[0] != "start":
            for msg in needs:
                receive(msg)
        work(name)
        for msg in sends:
            send(msg)

    receive(("xa",))
    receive(("xb",))
    receive(("xc",))
    cur[xh, c_rows] = p[z, y, xh, c_rows] * (1.0 / TOKENS)
    cur[other, c_rows] = recv_cz[0].astype(F32) * (1.0 / TOKENS)
    for k in (0, 1):
        cur[k, a_rows] = (p[z, y, k, a_rows] + recv_a[31, k].astype(F32)) * (1.0 / TOKENS)
        cur[k, b_rows] = (p[z, y, k, b_rows] + recv_b[31, k].astype(F32)) * (1.0 / TOKENS)
    mine = cur[xh]
    rows = [jnp.sum(basis_ref[n] * mine, axis=0, keepdims=True) for n in range(K)]
    rows.append(jnp.sum(mine * mine, axis=0, keepdims=True))
    rows.append(jnp.zeros((7, WID), F32))
    sums = jnp.sum(jnp.concatenate(rows, axis=0), axis=1, keepdims=True)
    sub = lax.broadcasted_iota(jnp.int32, (16, 128), 0)
    lane = lax.broadcasted_iota(jnp.int32, (16, 128), 1)
    sums = jnp.sum(jnp.where(sub == lane, sums, 0.0), axis=0, keepdims=True)
    both = cur[...].reshape(2 * BLK, WID)
    high = both.astype(BF)
    pair = jnp.concatenate([high, (both - high.astype(F32)).astype(BF)], axis=0)
    tokens = [jnp.sum(per_token(pair, k), axis=0, keepdims=True) for k in range(4)]
    tokens = jnp.concatenate(tokens + [jnp.zeros((4, 512), F32)], axis=0)
    sub = lax.broadcasted_iota(jnp.int32, (8, 128), 0)
    lane = lax.broadcasted_iota(jnp.int32, (8, 128), 1)
    shown = jnp.where(lane // 32 == sub, per_example(tokens), 0.0)
    shown = jnp.sum(shown, axis=0, keepdims=True)
    hz[z, 0:1] = shown
    hz[z, 1:2] = sums
    for k in FAR:
        send(("g2z", k))
    own_ref[...] = mine
    for k in FAR:
        receive(("g1z", k))
    gy[y] = ring_sum(gz, NZ)
    for k in range(1, NY):
        send(("g1y", k))
    drain = list(started)
    for copy in drain[:-40]:
        copy.wait_send()
    for k in range(1, NZ):
        receive(("g2z", k))
    hw[y * 8 + xh * 4 + xl * 2 + core, 0:2] = ring_sum(hz, NZ, 2)
    for k in WIDE:
        send(("g2w", k))
    for copy in drain[-40:]:
        copy.wait_send()
    for k in range(1, NY):
        receive(("g1y", k))
    gx[xh * 4 + xl * 2 + core] = ring_sum(gy, NY)
    for k in range(1, 8):
        send(("g1x", k))
    for k in range(1, 8):
        receive(("g1x", k))
    first_ref[...] = ring_sum(gx, 8)
    for k in WIDE:
        receive(("g2w", k))
    second_ref[0:2] = ring_sum(hw, 32, 2)
    second_ref[2:8] = jnp.zeros((6, 128), F32)
    for copy in started[len(drain):]:
        copy.wait_send()


def finish(own_ref, first_ref, second_ref, basis_ref, new_ref, hess_ref, proj_ref):
    mean = 1.0 / (FF * D)
    first, second = first_ref[...], second_ref[...]
    sub = lax.broadcasted_iota(jnp.int32, (8, 128), 0)
    lane = lax.broadcasted_iota(jnp.int32, (8, 128), 1)
    row = second[1:2] * mean
    coeff = jnp.sum(jnp.where(sub == lane, row, 0.0), axis=1, keepdims=True)
    squared = jnp.sum(jnp.where(lane[0:1] == K, row, 0.0), axis=1, keepdims=True)
    row = jnp.where(lane[0:1] < K, row, 0.0)
    cross = jnp.sum(coeff * first[8:16], axis=0, keepdims=True) * row
    cross = jnp.sum(cross, axis=1, keepdims=True) * mean
    twice = 2.0 * jnp.sum(row * row, axis=1, keepdims=True)
    beta = jnp.sqrt(jnp.maximum(squared - twice + cross, squared * 1e-12))
    inverse = 1.0 / beta
    hess_ref[...] = jnp.where(lane[0:1] == K, beta, row)[:, 0 : K + 1]
    left = own_ref[...]
    for n in range(K):
        left = left - coeff[n : n + 1] * basis_ref[n]
    new_ref[0] = left * inverse
    last = (second[0:1] - jnp.sum(coeff * first[0:8], axis=0, keepdims=True)) * inverse
    scale = (FF * D) ** (-0.5)
    shown = jnp.concatenate([first[0:8], jnp.broadcast_to(last, (8, 128))], axis=0) * scale
    dp = lax.axis_index("dp")
    for n in range(4):
        @pl.when(dp == n)
        def _():
            proj_ref[...] = shown[0 : K + 1, n * 32 : (n + 1) * 32]


def local(train_hidden, index_hidden, index_resid, basis):
    tasks = build()
    order, _, _ = schedule(tasks)
    messages = [m for name in tasks for m in tasks[name][3]]
    messages += [("g1y", k) for k in range(1, NY)] + [("g1x", k) for k in range(1, 8)]
    messages += [("g2z", k) for k in FAR] + [("g2w", k) for k in WIDE]
    index = {m: n for n, m in enumerate(messages)}
    vmem = pltpu.VMEM
    whole = pl.BlockSpec(memory_space=pltpu.VMEM)
    call = pl.pallas_call(
        functools.partial(kernel, order, tasks, index),
        out_shape=(
            jax.ShapeDtypeStruct((BLK, WID), F32),
            jax.ShapeDtypeStruct((16, 128), F32),
            jax.ShapeDtypeStruct((8, 128), F32),
        ),
        in_specs=[pl.BlockSpec(memory_space=pl.ANY)] * 4,
        out_specs=(whole, whole, whole),
        scratch_shapes=[
            vmem((1024, FF), BF),
            vmem((NZ, NY, 2, BLK, WID), BF),
            vmem((NZ, NY, ROWS_C, WID), BF),
            vmem((1024, NZ * NY * ROWS_C), BF),
            vmem((1280, 128), BF),
            vmem((NZ, NY, 2, BLK, WID), F32),
            vmem((32, 2, ROWS_A, WID), BF),
            vmem((32, 2, ROWS_B, WID), BF),
            vmem((32, 2, ROWS_A, WID), BF),
            vmem((32, 2, ROWS_B, WID), BF),
            vmem((NZ, NY, ROWS_C, WID), BF),
            vmem((NZ, NY, ROWS_C, WID), BF),
            vmem((2, 3, 4, ROWS_C, WID), BF),
            vmem((2, 3, 4, ROWS_C, WID), BF),
            vmem((8, ROWS_C, WID), BF),
            vmem((8, ROWS_C, WID), BF),
            vmem((1024, WID), F32),
            vmem((1024, WID), BF),
            vmem((NZ, NY, 64, WID), BF),
            vmem((K, 2, BLK, WID), BF),
            vmem((2, 2, 2, BLK, WID), BF),
            vmem((2, BLK, WID), BF),
            vmem((2, BLK, WID), F32),
            vmem((16, 128), F32),
            vmem((8, 512), F32),
            vmem((K, BLK, WID), F32),
            vmem((BLK, 1024), BF),
            vmem((64, WID), BF),
            vmem((NZ, 16, 128), F32),
            vmem((NY, 16, 128), F32),
            vmem((8, 16, 128), F32),
            vmem((NZ, 8, 128), F32),
            vmem((32, 8, 128), F32),
            pltpu.SemaphoreType.DMA((5,)),
            pltpu.SemaphoreType.DMA((len(messages),)),
            pltpu.SemaphoreType.DMA((len(messages),)),
        ],
        compiler_params=pltpu.CompilerParams(
            collective_id=0, has_side_effects=True, vmem_limit_bytes=60 * 2**20
        ),
        cost_estimate=pl.CostEstimate(
            flops=14 * 10**9, bytes_accessed=13 * 10**6, transcendentals=0
        ),
        name="arnoldi",
    )
    own, first, second = call(train_hidden, index_hidden.T, index_resid, basis)
    new, hess, proj = pl.pallas_call(
        finish,
        out_shape=(
            jax.ShapeDtypeStruct((1, BLK, WID), F32),
            jax.ShapeDtypeStruct((1, K + 1), F32),
            jax.ShapeDtypeStruct((K + 1, 32), F32),
        ),
        in_specs=[whole] * 4,
        out_specs=(whole, whole, whole),
        name="finish",
    )(own, first, second, basis)
    return new, hess, proj.T


def solution(mesh):
    in_specs = (P("fsdp", None), P("dp", "fsdp"), P("fsdp", "dp"), P(None, "fsdp", "dp"))
    out_specs = (P(None, "fsdp", "dp"), P(), P("dp", None))
    return jax.shard_map(local, mesh=mesh, in_specs=in_specs, out_specs=out_specs, check_vma=False)
```

```python
import functools

import jax
import jax.numpy as jnp
from jax import lax
from jax.experimental import pallas as pl
from jax.experimental.pallas import tpu as pltpu
from jax.sharding import PartitionSpec as P

D = 2048
FF = 5120
TOKENS = 65536
EX_TOK = 32
K = 8
NZ, NY = 8, 4
BLK = 80
WID = 512
ROWS_A, ROWS_B, ROWS_C = 32, 32, 16
MESH = pl.DeviceIdType.MESH
BF = jnp.bfloat16
F32 = jnp.float32
SIGNS = (1, -1)
FAR = (4, 3, 5, 2, 6, 1, 7)
WIDE = sorted(
    range(1, 32), key=lambda k: -(min(k // 8, 4 - k // 8) + (0, 1, 2, 1)[(k >> 1) & 3]) * 2 - (k & 1)
)


def half_of(sign):
    return 0 if sign > 0 else 1


def wrap(delta, size):
    delta %= size
    return delta - size if delta > size // 2 else delta


def parts_of(kind, hop, own):
    if hop == 1 and own:
        return ("o", "t")
    return ("f",)


def link_of(msg):
    kind = msg[0]
    if kind in ("Az", "az"):
        return ("z", msg[2])
    if kind in ("Ay", "ay", "Ry", "RY", "Cy"):
        return ("y", msg[1])
    if kind == "cz":
        return ("z", 1 if msg[1] < 4 else -1)
    if kind in ("Bz", "bz", "Rz", "RZ", "Cz"):
        return ("z", msg[1])
    if kind in ("By", "by", "cy"):
        return ("y", msg[2])
    if kind in ("qx", "vx", "hx", "xa", "xb", "xc", "hl", "Cx", "cx"):
        return ("x", 0)
    return ("c", 0) if kind == "hc" else (kind, msg[1])


def kilobytes(msg):
    kind = msg[0]
    a, b = 2 * ROWS_A, 2 * ROWS_B
    if kind == "Ay":
        return a / 2 if msg[3] in ("o", "t") or msg[2] == 2 else a
    if kind == "Az":
        return a / 2 if msg[4] in ("o", "t") or msg[3] == 4 else a
    if kind == "Bz":
        return b / 2 if msg[3] in ("o", "t") or msg[2] == 4 else b
    if kind == "By":
        return b / 2 if msg[4] in ("o", "t") or msg[3] == 2 else b
    if kind == "az":
        return a / 2 if msg[3] == 4 else a
    if kind == "ay":
        return a / 2 if msg[2] == 2 else a
    if kind == "bz":
        return b / 2 if msg[2] == 4 else b
    if kind == "by":
        return b / 2 if msg[3] == 2 else b
    if kind in ("Ry", "Rz", "RZ", "RY", "Cz", "Cy"):
        full = {"Ry": 16, "Rz": 48, "RZ": 64, "RY": 384, "Cz": ROWS_C, "Cy": 8 * ROWS_C}[kind]
        return full / 2 if msg[2] == (4 if kind[1] in "zZ" else 2) else full
    if kind == "cz":
        return 2 * ROWS_C
    if kind == "cy":
        return 2 * ROWS_C if msg[3] == 2 else 4 * ROWS_C
    if kind in ("Cx", "cx"):
        return (8 if kind == "Cx" else 4) * ROWS_C
    return {"qx": 64, "xc": ROWS_C, "vx": 560, "hx": 80, "hl": 160, "hc": 320, "xa": a, "xb": b}.get(kind, 8)


def build():
    tasks = {}

    def task(name, needs=(), after=(), cost=0.0, sends=()):
        needs, sends = list(needs), list(sends)
        tasks[name] = (needs, list(after), cost + 0.01 * (len(needs) + len(sends)), sends)

    first = []
    for s in SIGNS:
        first += [("Bz", s, 1), ("Ay", s, 1)]
    for s in SIGNS:
        first += [("Az", 0, s, 1), ("By", 0, s, 1)]
    task(
        ("start",),
        cost=0.5,
        sends=[("qx",)] + [("Cz", s, 1) for s in SIGNS] + [m + ("o",) for m in first]
        + [("Rz", s, 1) for s in SIGNS] + [("Ry", s, 1) for s in SIGNS],
    )
    task(("qx",), [("qx",)], [("start",)], sends=[m + ("t",) for m in first])
    for s in SIGNS:
        task(
            ("Ay", s),
            [("Ay", s, 1, "o"), ("Ay", s, 1, "t")],
            [("qx",)],
            sends=[("Ay", s, 2, "f")] + [("Az", wrap(-s, NY), u, 1, "f") for u in SIGNS],
        )
    task(
        ("Ay2",),
        [("Ay", s, 2, "f") for s in SIGNS],
        [("Ay", s) for s in SIGNS],
        sends=[("Az", 2, u, 1, "f") for u in SIGNS],
    )
    for dy in (0, 1, -1, 2):
        for s in SIGNS:
            for h in (1, 2, 3):
                task(
                    ("Az", dy, s, h),
                    [("Az", dy, s, h, p) for p in parts_of("Az", h, dy == 0)],
                    sends=[("Az", dy, s, h + 1, "f")],
                )
    for s in SIGNS:
        for h in (1, 2, 3):
            task(
                ("Bz", s, h),
                [("Bz", s, h, p) for p in parts_of("Bz", h, True)],
                sends=[("Bz", s, h + 1, "f")] + [("By", wrap(-s * h, NZ), u, 1, "f") for u in SIGNS],
            )
    task(
        ("Bz4",), [("Bz", s, 4, "f") for s in SIGNS], sends=[("By", 4, u, 1, "f") for u in SIGNS]
    )
    for dz in range(-3, 5):
        for s in SIGNS:
            task(
                ("By", dz, s),
                [("By", dz, s, 1, p) for p in parts_of("By", 1, dz == 0)],
                sends=[("By", dz, s, 2, "f")],
            )
    for s in SIGNS:
        for h in (1, 2, 3):
            task(("Cz", s, h), [("Cz", s, h)], sends=[("Cz", s, h + 1)])
        task(("Cy", s), [("Cy", s, 1)], sends=[("Cx", wrap(-s, NY)), ("Cy", s, 2)])
    task(
        ("CY0",),
        [("Cz", s, 4) for s in SIGNS],
        [("Cz", s, h) for s in SIGNS for h in (1, 2, 3)],
        sends=[("Cx", 0)] + [("Cy", s, 1) for s in SIGNS],
    )
    task(("Cy2",), [("Cy", s, 2) for s in SIGNS], [("Cy", s) for s in SIGNS], sends=[("Cx", 2)])
    late = {
        0: [],
        1: [("Bz4",)],
        2: [("Az", dy, s, 2) for dy in (0, 1, -1, 2) for s in SIGNS],
        3: [("Az", dy, s, 3) for dy in (0, 1, -1, 2) for s in SIGNS]
        + [("By", dz, s) for dz in range(-3, 5) for s in SIGNS],
    }[LATE]
    for s in SIGNS:
        task(("Ry", s), [("Ry", s, 1)], sends=[("Ry", s, 2)])
        for h in (1, 2, 3):
            task(("Rz", s, h), [("Rz", s, h)], sends=[("Rz", s, h + 1)])
            task(("RZ", s, h), [("RZ", s, h)], sends=[("RZ", s, h + 1)])
        task(("RY", s), [("RY", s, 1)], sends=[("RY", s, 2)])
    task(
        ("RZ0",),
        [("Ry", s, 2) for s in SIGNS],
        [("Ry", s) for s in SIGNS] + late,
        sends=[("RZ", s, 1) for s in SIGNS],
    )
    task(
        ("RY0",),
        [("Rz", s, 4) for s in SIGNS],
        [("Rz", s, h) for s in SIGNS for h in (1, 2, 3)] + late,
        sends=[("RY", s, 1) for s in SIGNS],
    )
    task(("vx",), after=[("start",)], cost=0.25, sends=[("vx",)])
    task(("hx",), after=[("vx",)], cost=0.25, sends=[("hx",)])
    task(("hl",), [("hx",)], [("hx",), ("Cy2",)], sends=[("hl",)])
    task(("hc",), [("hl",)], [("hl",)], sends=[("hc",)])
    task(("gram",), after=[("vx",)], cost=0.8)
    for g, planes in enumerate(PLANES):
        needs, after = [], [("m1", g - 1)] if g else [("load",), ("CY0",), ("Cy2",)]
        if g == len(PLANES) - 1:
            after.append(("m1c",))
        for dz in planes:
            for s in SIGNS:
                needs.append(("By", dz, s, 2, "f"))
                after.append(("By", dz, s))
            if dz == 0:
                after += [("Ay", s) for s in SIGNS] + [("Ay2",)]
            elif dz == 4:
                needs += [("Az", dy, s, 4, "f") for dy in (0, 1, -1, 2) for s in SIGNS]
                after.append(("Bz4",))
            else:
                s = -1 if dz > 0 else 1
                after += [("Az", dy, s, abs(dz)) for dy in (0, 1, -1, 2)] + [("Bz", s, abs(dz))]
        task(("m1", g), needs, after, cost=1.1 * len(planes))
    task(("load",), after=[("start",)], cost=0.1)
    for k in range(4):
        task(("xs", k), after=[("load",)] + ([("xs", k - 1)] if k else []), cost=0.7)
    task(
        ("m1c",),
        [("Cx", dy) for dy in (0, 1, -1, 2)],
        [("CY0",), ("Cy2",), ("m1", 0), ("xs", 3)],
        cost=0.9,
    )
    task(("img",), after=[("m1", len(PLANES) - 1)], cost=0.0)
    for n, dz in enumerate(ORDER):
        task(("m2", dz), after=[("img",)] + ([("m2", ORDER[n - 1])] if n else []), cost=0.95)
    for dy in (0, 1, -1, 2):
        task(("az", dy, 4), after=[("m2", 4)], cost=0.04, sends=[("az", dy, s, 4) for s in SIGNS])
        for s in SIGNS:
            for d in (3, 2, 1):
                task(
                    ("az", dy, s, d),
                    [("az", dy, s, d + 1)],
                    [("m2", s * d)],
                    cost=0.04,
                    sends=[("az", dy, s, d)],
                )
        task(("az", dy, 0), [("az", dy, s, 1) for s in SIGNS], [("m2", 0)], cost=0.04)
    task(("ay", 2), after=[("az", 2, 0)], cost=0.04, sends=[("ay", s, 2) for s in SIGNS])
    for s in SIGNS:
        task(("ay", s, 1), [("ay", s, 2)], [("az", s, 0)], cost=0.04, sends=[("ay", s, 1)])
    task(
        ("xa",), [("ay", s, 1) for s in SIGNS], [("az", 0, 0)], cost=0.04, sends=[("xa",)]
    )
    for dz in range(-3, 5):
        task(("by", dz, 2), after=[("m2", dz)], cost=0.04, sends=[("by", dz, s, 2) for s in SIGNS])
        for s in SIGNS:
            task(
                ("by", dz, s, 1),
                [("by", dz, s, 2)],
                [("m2", dz)],
                cost=0.04,
                sends=[("by", dz, s, 1)],
            )
        task(("by", dz, 0), [("by", dz, s, 1) for s in SIGNS], [("m2", dz)], cost=0.06)
    task(("bz", 4), after=[("by", 4, 0)], cost=0.04, sends=[("bz", s, 4) for s in SIGNS])
    for s in SIGNS:
        for d in (3, 2, 1):
            task(
                ("bz", s, d),
                [("bz", s, d + 1)],
                [("by", s * d, 0)],
                cost=0.04,
                sends=[("bz", s, d)],
            )
    task(("xb",), [("bz", s, 1) for s in SIGNS], [("by", 0, 0)], cost=0.06, sends=[("xb",)])
    for n, dz in enumerate(ORDER):
        task(("cx", dz), after=[("m2", dz)], cost=0.04, sends=[("cx", dz)])
        task(("cs", dz), [("cx", dz)], [("m2", dz)], cost=0.04)
    for g in (0, 1):
        done = [("cs", dz) for dz in GROUPS[g]]
        task(("cy", g, 2), after=done, cost=0.04, sends=[("cy", g, s, 2) for s in SIGNS])
        for s in SIGNS:
            task(("cy", g, s, 1), [("cy", g, s, 2)], done, cost=0.04, sends=[("cy", g, s, 1)])
        task(("cy", g, 0), [("cy", g, s, 1) for s in SIGNS], done, cost=0.04)
    for g in (0, 1):
        sends = [("cz", dz % NZ) for dz in GROUPS[g] if dz]
        task(("cz", g), after=[("cy", g, 0)], cost=0.05, sends=sends)
    task(("xc",), [("cz", k) for k in FAR], [("cy", 1, 0)], cost=0.05, sends=[("xc",)])
    for k in range(8):
        needs, after = [], [("m2", ORDER[-1])]
        if k == 0:
            needs += [("RZ", s, 4) for s in SIGNS] + [("RY", s, 2) for s in SIGNS]
            needs += [("hc",), ("vx",)]
            after += [("RZ", s, h) for s in SIGNS for h in (1, 2, 3)] + [("RY", s) for s in SIGNS]
            after += [("RZ0",), ("RY0",), ("hc",), ("vx",), ("gram",)]
        else:
            after += [("p8", k - 1)]
        task(("p8", k), needs, after, cost=0.65)
    task(("g1",), after=[("p8", 7)], cost=0.1, sends=[("g1z", k) for k in FAR])
    return tasks


PLANES = ((0,), (1, -1), (2, -2), (3, -3), (4,))
ORDER = (4, 3, -3, 2, -2, 1, -1, 0)
BIAS = {
    "By": 10, "Bz": 10, "RZ": -10, "RZ0": -20, "Ry": 10, "Rz": -10, "ay": 2, "az": -5,
    "bz": -10, "cz": 5, "g1": -10, "hc": 2, "m1": -20, "m2": -5, "vx": -2, "xs": -20,
}
LATE, RATE, DELAY, CLS = 2, 46.0, 2.2, True
SLACK = {
    "Ry": 1, "Rz": 2, "RZ": 1.5, "RY": 3, "vx": 3, "hx": 1, "hl": 5, "hc": 0,
}
GROUPS = (ORDER[:4], ORDER[4:])


def schedule(tasks):
    rate = {"z": RATE, "y": RATE, "x": RATE - 1, "c": 400.0}
    delay = {"z": DELAY, "y": DELAY, "x": DELAY + 0.5, "c": 0.8}
    waits = {}
    followers = {name: [] for name in tasks}
    for name, (needs, after, _, _) in tasks.items():
        for msg in needs:
            waits.setdefault(msg, []).append(name)
        for other in after:
            followers[other].append(name)

    def cost_of(msg):
        axis = link_of(msg)[0]
        return kilobytes(msg) / rate.get(axis, 40.0) + delay.get(axis, 3.0)

    @functools.cache
    def rank(name):
        _, _, cost, sends = tasks[name]
        rest = [rank(f) for f in followers[name]]
        rest += [cost_of(m) + max([rank(w) for w in waits.get(m, ())], default=0) for m in sends]
        return cost + max(rest, default=0)

    now, free, arrives, done, order = 0.0, {}, {}, {}, []
    left = dict(tasks)
    while left:
        ready, soonest = [], None
        for name, (needs, after, cost, sends) in left.items():
            if any(a not in done for a in after) or any(m not in arrives for m in needs):
                continue
            at = max([arrives[m] for m in needs], default=0.0)
            if at <= now:
                heavy = CLS and cost >= 0.3 and not sends
                ready.append((heavy, -rank(name) - BIAS.get(name[0], 0.0), at, name))
            else:
                soonest = at if soonest is None else min(soonest, at)
        if not ready:
            now = soonest
            continue
        name = min(ready, key=lambda r: r[:3])[3]
        _, _, cost, sends = left.pop(name)
        now += cost
        done[name] = now
        order.append(name)
        for msg in sends:
            link = link_of(msg)
            axis = link[0]
            begin = max(now, free.get(link, 0.0))
            free[link] = begin + kilobytes(msg) / rate.get(axis, 40.0)
            arrives[msg] = free[link] + delay.get(axis, 3.0) + SLACK.get(msg[0], 0.0)
    return order, done, arrives


def product(a, b, ca, cb):
    return lax.dot_general(a, b, (((ca,), (cb,)), ((), ())), preferred_element_type=F32)


def kernel(
    order, tasks, index,
    x_hbm, hid_hbm, res_hbm, basis_hbm,
    own_ref, first_ref, second_ref,
    xv, q, qc, xc, select, p, send_a, send_b, recv_a, recv_b,
    send_cx, recv_cx, send_cy, recv_cy, send_cz, recv_cz, acc, img, r, v16, ht, hs, cur,
    early, tokens8, basis_ref, hid_ref, res_ref, gz, gy, gx, hz, hw, load_sem, send_sem, recv_sem,
):
    dp, fs = lax.axis_index("dp"), lax.axis_index("fsdp")
    z, y, xh = fs // 8, lax.rem(fs // 2, 4), lax.rem(fs, 2)
    xl, core = dp // 2, lax.rem(dp, 2)
    other = 1 - xh

    zi = {d: lax.rem(z + (d + NZ), NZ) for d in range(-3, 8)}
    zi[-4] = zi[4]
    yi = {d: lax.rem(y + (d + NY), NY) for d in range(-1, 4)}
    yi[-2] = yi[2]

    def fsdp(za, ya, xa):
        return (za * NY + ya) * 2 + xa

    def along_z(d):
        return (dp, fsdp(zi[d], y, xh))

    def along_y(d):
        return (dp, fsdp(z, yi[d], xh))

    def along_x(k):
        xa = 1 - xh if k & 4 else xh
        la = 1 - xl if k & 2 else xl
        ca = 1 - core if k & 1 else core
        return (la * 2 + ca, fsdp(z, y, xa))

    def along_w(k):
        bits = k & 7
        xa = 1 - xh if bits & 4 else xh
        la = 1 - xl if bits & 2 else xl
        ca = 1 - core if bits & 1 else core
        return (la * 2 + ca, fsdp(z, yi[k // 8], xa))

    partners = [along_z(d) for d in FAR] + [along_w(k) for k in WIDE]

    barrier = pltpu.get_barrier_semaphore()
    loads = [
        pltpu.make_async_copy(basis_hbm.at[K - 1], basis_ref.at[K - 1], load_sem.at[0]),
        pltpu.make_async_copy(res_hbm, res_ref, load_sem.at[1]),
        pltpu.make_async_copy(hid_hbm, hid_ref, load_sem.at[2]),
        pltpu.make_async_copy(
            basis_hbm.at[pl.ds(0, K - 1)], basis_ref.at[pl.ds(0, K - 1)], load_sem.at[3]
        ),
        pltpu.make_async_copy(x_hbm, xv, load_sem.at[4]),
    ]
    for load in loads:
        load.start()
    for device in partners:
        pl.semaphore_signal(barrier, inc=1, device_id=device, device_id_type=MESH)
    loads[0].wait()
    loads[1].wait()
    q[:, :, other, pl.ds(ROWS_A + ROWS_B, ROWS_C)] = jnp.zeros((NZ, NY, ROWS_C, WID), BF)
    narrow = basis_ref[K - 1].astype(BF)
    q[z, y, xh] = narrow
    v16[K - 1, xh] = narrow
    r[z, y] = res_ref[...]

    def q_part(rows, part, oz, oy):
        at = q.at[zi[oz], yi[oy]]
        which = {"f": slice(None), "o": xh, "t": other}.get(part, part)
        return at.at[which, rows]

    a_rows, b_rows = pl.ds(0, ROWS_A), pl.ds(ROWS_A, ROWS_B)
    c_rows = pl.ds(ROWS_A + ROWS_B, ROWS_C)

    def lane_half(sign):
        return pl.ds(half_of(sign) * (WID // 2), WID // 2)

    def slot_a(msg):
        if msg[0] == "az":
            _, dy, s, d = msg
            base = {0: 0, 1: 7, -1: 14, 2: 21}[dy]
            return base + (6 if d == 4 else (d - 1) * 2 + half_of(s)), d == 4, s
        if msg[0] == "ay":
            _, s, d = msg
            return 28 + (2 if d == 2 else half_of(s)), d == 2, s
        return 31, False, 1

    def slot_b(msg):
        if msg[0] == "by":
            _, dz, s, d = msg
            return (dz + 3) * 3 + (2 if d == 2 else half_of(s)), d == 2, s
        if msg[0] == "bz":
            _, s, d = msg
            return 24 + (6 if d == 4 else (d - 1) * 2 + half_of(s)), d == 4, s
        return 31, False, 1

    def piece(buf, slot):
        n, halved, s = slot
        return buf.at[n, half_of(s)] if halved else buf.at[n]

    def place(msg):
        kind = msg[0]
        if kind == "qx":
            rows = pl.ds(0, ROWS_A + ROWS_B)
            here = q.at[z, y, xh, rows]
            return here, here, q.at[z, y, other, rows], along_x(4)
        if kind == "Cz":
            _, s, h = msg
            lanes = lane_half(s) if h == 4 else slice(None)
            here = q.at[zi[wrap(-s * (h - 1), NZ)], y, xh, c_rows, lanes]
            return here, here, q.at[zi[wrap(-s * h, NZ)], y, xh, c_rows, lanes], along_z(s)
        if kind == "Cy":
            _, s, h = msg
            lanes = lane_half(s) if h == 2 else slice(None)
            here = q.at[:, yi[wrap(-s * (h - 1), NY)], xh, c_rows, lanes]
            return here, here, q.at[:, yi[wrap(-s * h, NY)], xh, c_rows, lanes], along_y(s)
        if kind == "Cx":
            lands = qc.at[:, yi[msg[1]]]
            return q.at[:, yi[msg[1]], xh, c_rows], lands, lands, along_x(4)
        if kind == "cx":
            n = ORDER.index(msg[1])
            return send_cx.at[n], recv_cx.at[n], recv_cx.at[n], along_x(4)
        if kind == "cy":
            _, g, s, d = msg
            n, lanes = (2, lane_half(s)) if d == 2 else (half_of(s), slice(None))
            target = recv_cy.at[g, n, :, :, lanes]
            return send_cy.at[g, n, :, :, lanes], target, target, along_y(s)
        if kind == "cz":
            n = msg[1]
            return send_cz.at[n], recv_cz.at[n], recv_cz.at[n], along_z(n)
        if kind == "xc":
            return send_cz.at[0], recv_cz.at[0], recv_cz.at[0], along_x(4)
        if kind in ("Ay", "Az", "Bz", "By"):
            rows = a_rows if kind[0] == "A" else b_rows
            if kind in ("Ay", "Bz"):
                _, s, h, part = msg
            else:
                _, off, s, h, part = msg
            size = NZ if kind[1] == "z" else NY
            if h == size // 2:
                part = half_of(s)
            if kind[1] == "y":
                oz = off if kind == "By" else 0
                here = q_part(rows, part, oz, wrap(-s * (h - 1), NY))
                there = q_part(rows, part, oz, wrap(-s * h, NY))
                return here, here, there, along_y(s)
            oy = off if kind == "Az" else 0
            here = q_part(rows, part, wrap(-s * (h - 1), NZ), oy)
            there = q_part(rows, part, wrap(-s * h, NZ), oy)
            return here, here, there, along_z(s)
        if kind in ("Ry", "RZ", "Rz", "RY"):
            _, s, h = msg
            last = h == (NY if kind[1] in "yY" else NZ) // 2
            rows = pl.ds(0, 16) if kind in ("Ry", "RZ") else pl.ds(16, 48)
            lanes = lane_half(s) if last else slice(None)
            n = NY if kind[1] in "yY" else NZ
            a, b = wrap(-s * (h - 1), n), wrap(-s * h, n)
            if kind == "Ry":
                here, there = r.at[z, yi[a], rows, lanes], r.at[z, yi[b], rows, lanes]
            elif kind == "Rz":
                here, there = r.at[zi[a], y, rows, lanes], r.at[zi[b], y, rows, lanes]
            elif kind == "RZ":
                here, there = r.at[zi[a], :, rows, lanes], r.at[zi[b], :, rows, lanes]
            else:
                here, there = r.at[:, yi[a], rows, lanes], r.at[:, yi[b], rows, lanes]
            return here, here, there, along_y(s) if n == NY else along_z(s)
        if kind == "vx":
            here = v16.at[pl.ds(0, K - 1), xh]
            return here, here, v16.at[pl.ds(0, K - 1), other], along_x(4)
        if kind == "hx":
            return hs.at[other], ht.at[xl, core, xh], ht.at[xl, core, other], along_x(4)
        if kind == "hl":
            here = ht.at[xl, core]
            return here, here, ht.at[1 - xl, core], along_x(2)
        if kind == "hc":
            here = ht.at[:, core]
            return here, here, ht.at[:, 1 - core], along_x(1)
        if kind in ("az", "ay", "xa"):
            slot = slot_a(msg)
            target = piece(recv_a, slot)
            src = piece(send_a, slot)
        elif kind in ("by", "bz", "xb"):
            slot = slot_b(msg)
            target = piece(recv_b, slot)
            src = piece(send_b, slot)
        if kind in ("xa", "xb"):
            return src, target, target, along_x(4)
        if kind in ("az", "by"):
            return src, target, target, along_z(msg[2]) if kind == "az" else along_y(msg[2])
        if kind in ("ay", "bz"):
            return src, target, target, along_y(msg[1]) if kind == "ay" else along_z(msg[1])
        k = msg[1]
        if kind == "g1z":
            here = gz.at[z]
            return here, here, gz.at[zi[-k + NZ if k > 3 else -k]], along_z(k)
        if kind == "g1y":
            here = gy.at[y]
            return here, here, gy.at[yi[-k + NY if k > 1 else -k]], along_y(k)
        if kind == "g2z":
            here = hz.at[z, pl.ds(0, 2)]
            return here, here, hz.at[zi[-k + NZ if k > 3 else -k], pl.ds(0, 2)], along_z(k)
        xa = 1 - xh if k & 4 else xh
        la = 1 - xl if k & 2 else xl
        ca = 1 - core if k & 1 else core
        mine, theirs = xh * 4 + xl * 2 + core, xa * 4 + la * 2 + ca
        if kind == "g1x":
            return gx.at[mine], gx.at[mine], gx.at[theirs], along_x(k)
        d = k // 8
        here = hw.at[y * 8 + mine, pl.ds(0, 2)]
        lands = hw.at[yi[-d + NY if d > 1 else -d] * 8 + theirs, pl.ds(0, 2)]
        return here, here, lands, along_w(k)

    started = []

    def send(msg):
        src, target, _, device = place(msg)
        n = index[msg]
        copy = pltpu.make_async_remote_copy(
            src_ref=src, dst_ref=target, send_sem=send_sem.at[n], recv_sem=recv_sem.at[n],
            device_id=device, device_id_type=MESH,
        )
        copy.start()
        started.append(copy)

    def receive(msg):
        _, _, lands, device = place(msg)
        n = index[msg]
        pltpu.make_async_remote_copy(
            src_ref=lands, dst_ref=lands, send_sem=send_sem.at[n], recv_sem=recv_sem.at[n],
            device_id=device, device_id_type=MESH,
        ).wait_recv()

    def fold(rows, buf, where, slots, out):
        for k in (0, 1):
            total = p[where[0], where[1], k, rows]
            for n, halved, s in slots:
                if not halved or half_of(s) == k:
                    total = total + buf[n, k].astype(F32)
            if out is None:
                p[where[0], where[1], k, rows] = total
            else:
                out[0][out[1], k] = total.astype(BF)

    def fold_a(where, msgs, out=None):
        fold(a_rows, recv_a, where, [slot_a(m) for m in msgs], out and (send_a, slot_a(out)[0]))

    def fold_b(where, msgs, out=None):
        fold(b_rows, recv_b, where, [slot_b(m) for m in msgs], out and (send_b, slot_b(out)[0]))

    def fold_c(plane, row, arrived, out=None):
        for h in (0, 1):
            lanes = pl.ds(h * (WID // 2), WID // 2)
            total = p[plane, row, xh, c_rows, lanes]
            for ref, s in arrived:
                if s is None or half_of(s) == h:
                    total = total + ref[:, lanes].astype(F32)
            if out is None:
                p[plane, row, xh, c_rows, lanes] = total
            else:
                out[:, lanes] = total.astype(BF)

    def lanes_of(plane):
        return pl.ds(pl.multiple_of(plane * (NY * 2 * BLK), 128), NY * 2 * BLK)

    def per_token(rows, k, part=None):
        if part is None:
            many, errors, hidden = 512, r[2 * k : 2 * k + 2], ht[k // 2, k % 2]
        else:
            many, errors = 256, r[2 * k + part]
            hidden = ht[k // 2, k % 2, :, :, 256 * part : 256 * (part + 1)]
        mapped = product(rows, errors.reshape(many, WID), 1, 1)
        n = rows.shape[0] // (2 * BLK)
        hidden = hidden.reshape(2 * BLK, many).astype(F32)
        return jnp.sum(mapped.reshape(n, 2 * BLK, many) * hidden[None], axis=1)

    def per_example(tokens):
        t = lax.broadcasted_iota(jnp.int32, (512, 128), 0)
        e = lax.broadcasted_iota(jnp.int32, (512, 128), 1)
        owner = (t // 64) * 4 + 2 * xh + lax.rem(t, 64) // EX_TOK
        marks = jnp.where(owner == lax.rem(e, 32), 1.0, 0.0).astype(BF)
        terms, rest = [], tokens
        for _ in range(3):
            terms.append(rest.astype(BF).astype(F32))
            rest = rest - terms[-1]
        sums = product(jnp.concatenate(terms, axis=0).astype(BF), marks, 1, 0)
        return sums[0:8] + sums[8:16] + sums[16:24]

    def work(name):
        kind = name[0]
        if kind == "start":
            pl.semaphore_wait(barrier, len(partners))
        elif kind == "vx":
            loads[3].wait()
            for n in range(K - 1):
                v16[n, xh] = basis_ref[n].astype(BF)
        elif kind == "hx":
            loads[2].wait()
            for which in (0, 1):
                cuts = [(2 * n + which) * 64 for n in range(8)]
                pieces = [hid_ref[:, at : at + 64] for at in cuts]
                hs[which] = jnp.concatenate(pieces, axis=1)
            ht[xl, core, xh] = hs[xh]
        elif kind == "gram":
            lane = lax.broadcasted_iota(jnp.int32, (8, 128), 1)
            table = jnp.zeros((8, 128), F32)
            for i in range(K):
                rows = [jnp.sum(basis_ref[j] * basis_ref[i], axis=0, keepdims=True) for j in range(K)]
                column = jnp.sum(jnp.concatenate(rows, axis=0), axis=1, keepdims=True)
                table = table + jnp.where(lane == i, column, 0.0)
            early[8:16] = table
            early[0:8] = jnp.zeros((8, 128), F32)
        elif kind == "load":
            loads[4].wait()
        elif kind == "m1":
            total = None
            for dz in PLANES[name[1]]:
                term = product(xv[:, lanes_of(zi[dz])], q[zi[dz]].reshape(NY * 2 * BLK, WID), 1, 0)
                total = term if total is None else total + term
            if name[1] == len(PLANES) - 1:
                img[...] = (acc[...] + total).astype(BF)
            else:
                acc[...] = total if name[1] == 0 else acc[...] + total
        elif kind == "xs":
            k = name[1]
            if k == 0:
                f = lax.broadcasted_iota(jnp.int32, (1280, 128), 0)
                at = lax.broadcasted_iota(jnp.int32, (1280, 128), 1)
                block = (f * 52429) >> 22
                inside = f - block * BLK - (ROWS_A + ROWS_B)
                hit = (inside >= 0) & ((block & 1) == other) & ((block >> 1) * ROWS_C + inside == at)
                select[...] = jnp.where(hit, 1.0, 0.0).astype(BF)
            columns = xv[:, 1280 * k : 1280 * (k + 1)]
            xc[:, 128 * k : 128 * (k + 1)] = product(columns, select[...], 1, 0).astype(BF)
        elif kind == "m1c":
            acc[...] = acc[...] + product(xc[...], qc[...].reshape(NZ * NY * ROWS_C, WID), 1, 0)
        elif kind == "img":
            pass
        elif kind == "m2":
            plane = zi[name[1]]
            p[plane] = product(xv[:, lanes_of(plane)], img[...], 0, 0).reshape(NY, 2, BLK, WID)
        elif kind == "az":
            dy = name[1]
            if name[2] == 4:
                fold_a((zi[4], yi[dy]), [], ("az", dy, 1, 4))
            elif name[2] == 0:
                fold_a((z, yi[dy]), [("az", dy, s, 1) for s in SIGNS])
            else:
                s, d = name[2:]
                fold_a((zi[s * d], yi[dy]), [("az", dy, s, d + 1)], ("az", dy, s, d))
        elif kind == "ay":
            if name[1] == 2 and len(name) == 2:
                fold_a((z, yi[2]), [], ("ay", 1, 2))
            else:
                s = name[1]
                fold_a((z, yi[s]), [("ay", s, 2)], ("ay", s, 1))
        elif kind == "xa":
            fold_a((z, y), [("ay", s, 1) for s in SIGNS])
            fold_a((z, y), [], ("xa",))
        elif kind == "by":
            dz = name[1]
            if len(name) == 4:
                s = name[2]
                fold_b((zi[dz], yi[s]), [("by", dz, s, 2)], ("by", dz, s, 1))
            elif name[2] == 2:
                fold_b((zi[dz], yi[2]), [], ("by", dz, 1, 2))
            else:
                fold_b((zi[dz], y), [("by", dz, s, 1) for s in SIGNS])
        elif kind == "bz":
            if len(name) == 2:
                fold_b((zi[4], y), [], ("bz", 1, 4))
            else:
                s, d = name[1:]
                fold_b((zi[s * d], y), [("bz", s, d + 1)], ("bz", s, d))
        elif kind == "xb":
            fold_b((z, y), [("bz", s, 1) for s in SIGNS])
            fold_b((z, y), [], ("xb",))
        elif kind == "cx":
            send_cx[ORDER.index(name[1])] = p[zi[name[1]], :, other, c_rows].astype(BF)
        elif kind == "cs":
            plane = zi[name[1]]
            arrived = recv_cx[ORDER.index(name[1])].astype(F32)
            p[plane, :, xh, c_rows] = p[plane, :, xh, c_rows] + arrived
        elif kind == "cy":
            g = name[1]
            for j, dz in enumerate(GROUPS[g]):
                if len(name) == 4:
                    s = name[2]
                    got = [(recv_cy.at[g, 2, j], s)]
                    fold_c(zi[dz], yi[s], got, send_cy.at[g, half_of(s), j])
                elif name[2] == 2:
                    fold_c(zi[dz], yi[2], [], send_cy.at[g, 2, j])
                else:
                    fold_c(zi[dz], y, [(recv_cy.at[g, n, j], None) for n in (0, 1)])
        elif kind == "cz":
            for dz in GROUPS[name[1]]:
                if dz:
                    fold_c(zi[dz], y, [], send_cz.at[dz % NZ])
        elif kind == "xc":
            fold_c(z, y, [(recv_cz.at[n], None) for n in range(1, NZ)])
            fold_c(z, y, [], send_cz.at[0])
        elif kind == "p8":
            k = name[1]
            if k == 0:
                v16[K - 1, other, pl.ds(0, ROWS_A + ROWS_B)] = q[z, y, other, pl.ds(0, ROWS_A + ROWS_B)]
                v16[K - 1, other, c_rows] = qc[z, y]
            half = pl.ds(256 * (k % 2), 256)
            tokens8[:, half] = per_token(v16[...].reshape(K * 2 * BLK, WID), k // 2, k % 2)
            if k % 2:
                sums = per_example(tokens8[...])
                lane = lax.broadcasted_iota(jnp.int32, (8, 128), 1)
                early[0:8] = early[0:8] + jnp.where(lane // 32 == k // 2, sums, 0.0)
        elif kind == "g1":
            gz[z] = early[...]

    def ring_sum(buf, n, rows=16):
        total = buf[0, 0:rows]
        for k in range(1, n):
            total = total + buf[k, 0:rows]
        return total

    for name in order:
        needs, _, _, sends = tasks[name]
        if name[0] != "start":
            for msg in needs:
                receive(msg)
        work(name)
        for msg in sends:
            send(msg)

    receive(("xa",))
    receive(("xb",))
    receive(("xc",))
    cur[xh, c_rows] = p[z, y, xh, c_rows] * (1.0 / TOKENS)
    cur[other, c_rows] = recv_cz[0].astype(F32) * (1.0 / TOKENS)
    for k in (0, 1):
        cur[k, a_rows] = (p[z, y, k, a_rows] + recv_a[31, k].astype(F32)) * (1.0 / TOKENS)
        cur[k, b_rows] = (p[z, y, k, b_rows] + recv_b[31, k].astype(F32)) * (1.0 / TOKENS)
    mine = cur[xh]
    rows = [jnp.sum(basis_ref[n] * mine, axis=0, keepdims=True) for n in range(K)]
    rows.append(jnp.sum(mine * mine, axis=0, keepdims=True))
    rows.append(jnp.zeros((7, WID), F32))
    sums = jnp.sum(jnp.concatenate(rows, axis=0), axis=1, keepdims=True)
    sub = lax.broadcasted_iota(jnp.int32, (16, 128), 0)
    lane = lax.broadcasted_iota(jnp.int32, (16, 128), 1)
    sums = jnp.sum(jnp.where(sub == lane, sums, 0.0), axis=0, keepdims=True)
    both = cur[...].reshape(2 * BLK, WID)
    high = both.astype(BF)
    pair = jnp.concatenate([high, (both - high.astype(F32)).astype(BF)], axis=0)
    tokens = [jnp.sum(per_token(pair, k), axis=0, keepdims=True) for k in range(4)]
    tokens = jnp.concatenate(tokens + [jnp.zeros((4, 512), F32)], axis=0)
    sub = lax.broadcasted_iota(jnp.int32, (8, 128), 0)
    lane = lax.broadcasted_iota(jnp.int32, (8, 128), 1)
    shown = jnp.where(lane // 32 == sub, per_example(tokens), 0.0)
    shown = jnp.sum(shown, axis=0, keepdims=True)
    hz[z, 0:1] = shown
    hz[z, 1:2] = sums
    for k in FAR:
        send(("g2z", k))
    own_ref[...] = mine
    for k in FAR:
        receive(("g1z", k))
    gy[y] = ring_sum(gz, NZ)
    for k in range(1, NY):
        send(("g1y", k))
    drain = list(started)
    for copy in drain[:-40]:
        copy.wait_send()
    for k in range(1, NZ):
        receive(("g2z", k))
    hw[y * 8 + xh * 4 + xl * 2 + core, 0:2] = ring_sum(hz, NZ, 2)
    for k in WIDE:
        send(("g2w", k))
    for copy in drain[-40:]:
        copy.wait_send()
    for k in range(1, NY):
        receive(("g1y", k))
    gx[xh * 4 + xl * 2 + core] = ring_sum(gy, NY)
    for k in range(1, 8):
        send(("g1x", k))
    for k in range(1, 8):
        receive(("g1x", k))
    first_ref[...] = ring_sum(gx, 8)
    for k in WIDE:
        receive(("g2w", k))
    second_ref[0:2] = ring_sum(hw, 32, 2)
    second_ref[2:8] = jnp.zeros((6, 128), F32)
    for copy in started[len(drain):]:
        copy.wait_send()


def finish(own_ref, first_ref, second_ref, basis_ref, new_ref, hess_ref, proj_ref):
    mean = 1.0 / (FF * D)
    first, second = first_ref[...], second_ref[...]
    sub = lax.broadcasted_iota(jnp.int32, (8, 128), 0)
    lane = lax.broadcasted_iota(jnp.int32, (8, 128), 1)
    row = second[1:2] * mean
    coeff = jnp.sum(jnp.where(sub == lane, row, 0.0), axis=1, keepdims=True)
    squared = jnp.sum(jnp.where(lane[0:1] == K, row, 0.0), axis=1, keepdims=True)
    row = jnp.where(lane[0:1] < K, row, 0.0)
    cross = jnp.sum(coeff * first[8:16], axis=0, keepdims=True) * row
    cross = jnp.sum(cross, axis=1, keepdims=True) * mean
    twice = 2.0 * jnp.sum(row * row, axis=1, keepdims=True)
    beta = jnp.sqrt(jnp.maximum(squared - twice + cross, squared * 1e-12))
    inverse = 1.0 / beta
    hess_ref[...] = jnp.where(lane[0:1] == K, beta, row)[:, 0 : K + 1]
    left = own_ref[...]
    for n in range(K):
        left = left - coeff[n : n + 1] * basis_ref[n]
    new_ref[0] = left * inverse
    last = (second[0:1] - jnp.sum(coeff * first[0:8], axis=0, keepdims=True)) * inverse
    scale = (FF * D) ** (-0.5)
    shown = jnp.concatenate([first[0:8], jnp.broadcast_to(last, (8, 128))], axis=0) * scale
    dp = lax.axis_index("dp")
    for n in range(4):
        @pl.when(dp == n)
        def _():
            proj_ref[...] = shown[0 : K + 1, n * 32 : (n + 1) * 32]


def local(train_hidden, index_hidden, index_resid, basis):
    tasks = build()
    order, _, _ = schedule(tasks)
    messages = [m for name in tasks for m in tasks[name][3]]
    messages += [("g1y", k) for k in range(1, NY)] + [("g1x", k) for k in range(1, 8)]
    messages += [("g2z", k) for k in FAR] + [("g2w", k) for k in WIDE]
    index = {m: n for n, m in enumerate(messages)}
    vmem = pltpu.VMEM
    whole = pl.BlockSpec(memory_space=pltpu.VMEM)
    call = pl.pallas_call(
        functools.partial(kernel, order, tasks, index),
        out_shape=(
            jax.ShapeDtypeStruct((BLK, WID), F32),
            jax.ShapeDtypeStruct((16, 128), F32),
            jax.ShapeDtypeStruct((8, 128), F32),
        ),
        in_specs=[pl.BlockSpec(memory_space=pl.ANY)] * 4,
        out_specs=(whole, whole, whole),
        scratch_shapes=[
            vmem((1024, FF), BF),
            vmem((NZ, NY, 2, BLK, WID), BF),
            vmem((NZ, NY, ROWS_C, WID), BF),
            vmem((1024, NZ * NY * ROWS_C), BF),
            vmem((1280, 128), BF),
            vmem((NZ, NY, 2, BLK, WID), F32),
            vmem((32, 2, ROWS_A, WID), BF),
            vmem((32, 2, ROWS_B, WID), BF),
            vmem((32, 2, ROWS_A, WID), BF),
            vmem((32, 2, ROWS_B, WID), BF),
            vmem((NZ, NY, ROWS_C, WID), BF),
            vmem((NZ, NY, ROWS_C, WID), BF),
            vmem((2, 3, 4, ROWS_C, WID), BF),
            vmem((2, 3, 4, ROWS_C, WID), BF),
            vmem((8, ROWS_C, WID), BF),
            vmem((8, ROWS_C, WID), BF),
            vmem((1024, WID), F32),
            vmem((1024, WID), BF),
            vmem((NZ, NY, 64, WID), BF),
            vmem((K, 2, BLK, WID), BF),
            vmem((2, 2, 2, BLK, WID), BF),
            vmem((2, BLK, WID), BF),
            vmem((2, BLK, WID), F32),
            vmem((16, 128), F32),
            vmem((8, 512), F32),
            vmem((K, BLK, WID), F32),
            vmem((BLK, 1024), BF),
            vmem((64, WID), BF),
            vmem((NZ, 16, 128), F32),
            vmem((NY, 16, 128), F32),
            vmem((8, 16, 128), F32),
            vmem((NZ, 8, 128), F32),
            vmem((32, 8, 128), F32),
            pltpu.SemaphoreType.DMA((5,)),
            pltpu.SemaphoreType.DMA((len(messages),)),
            pltpu.SemaphoreType.DMA((len(messages),)),
        ],
        compiler_params=pltpu.CompilerParams(
            collective_id=0, has_side_effects=True, vmem_limit_bytes=60 * 2**20
        ),
        cost_estimate=pl.CostEstimate(
            flops=14 * 10**9, bytes_accessed=13 * 10**6, transcendentals=0
        ),
        name="arnoldi",
    )
    own, first, second = call(train_hidden, index_hidden.T, index_resid, basis)
    new, hess, proj = pl.pallas_call(
        finish,
        out_shape=(
            jax.ShapeDtypeStruct((1, BLK, WID), F32),
            jax.ShapeDtypeStruct((1, K + 1), F32),
            jax.ShapeDtypeStruct((K + 1, 32), F32),
        ),
        in_specs=[whole] * 4,
        out_specs=(whole, whole, whole),
        name="finish",
    )(own, first, second, basis)
    return new, hess, proj.T


def solution(mesh):
    in_specs = (P("fsdp", None), P("dp", "fsdp"), P("fsdp", "dp"), P(None, "fsdp", "dp"))
    out_specs = (P(None, "fsdp", "dp"), P(), P("dp", None))
    return jax.shard_map(local, mesh=mesh, in_specs=in_specs, out_specs=out_specs, check_vma=False)
```

```python
import functools

import jax
import jax.numpy as jnp
from jax import lax
from jax.experimental import pallas as pl
from jax.experimental.pallas import tpu as pltpu
from jax.sharding import PartitionSpec as P

D = 2048
FF = 5120
TOKENS = 65536
EX_TOK = 32
K = 8
NZ, NY = 8, 4
BLK = 80
WID = 512
ROWS_A, ROWS_B, ROWS_C = 32, 32, 16
MESH = pl.DeviceIdType.MESH
BF = jnp.bfloat16
F32 = jnp.float32
SIGNS = (1, -1)
FAR = (4, 3, 5, 2, 6, 1, 7)
WIDE = sorted(
    range(1, 32), key=lambda k: -(min(k // 8, 4 - k // 8) + (0, 1, 2, 1)[(k >> 1) & 3]) * 2 - (k & 1)
)


def half_of(sign):
    return 0 if sign > 0 else 1


def wrap(delta, size):
    delta %= size
    return delta - size if delta > size // 2 else delta


def parts_of(kind, hop, own):
    if hop == 1 and own:
        return ("o", "t")
    return ("f",)


def link_of(msg):
    kind = msg[0]
    if kind in ("Az", "az"):
        return ("z", msg[2])
    if kind in ("Ay", "ay", "Ry", "RY", "Cy"):
        return ("y", msg[1])
    if kind == "cz":
        return ("z", 1 if msg[1] < 4 else -1)
    if kind in ("Bz", "bz", "Rz", "RZ", "Cz"):
        return ("z", msg[1])
    if kind in ("By", "by", "cy"):
        return ("y", msg[2])
    if kind in ("qx", "vx", "hx", "xa", "xb", "xc", "hl", "Cx", "cx"):
        return ("x", 0)
    return ("c", 0) if kind == "hc" else (kind, msg[1])


def kilobytes(msg):
    kind = msg[0]
    a, b = 2 * ROWS_A, 2 * ROWS_B
    if kind == "Ay":
        return a / 2 if msg[3] in ("o", "t") or msg[2] == 2 else a
    if kind == "Az":
        return a / 2 if msg[4] in ("o", "t") or msg[3] == 4 else a
    if kind == "Bz":
        return b / 2 if msg[3] in ("o", "t") or msg[2] == 4 else b
    if kind == "By":
        return b / 2 if msg[4] in ("o", "t") or msg[3] == 2 else b
    if kind == "az":
        return a / 2 if msg[3] == 4 else a
    if kind == "ay":
        return a / 2 if msg[2] == 2 else a
    if kind == "bz":
        return b / 2 if msg[2] == 4 else b
    if kind == "by":
        return b / 2 if msg[3] == 2 else b
    if kind in ("Ry", "Rz", "RZ", "RY", "Cz", "Cy"):
        full = {"Ry": 16, "Rz": 48, "RZ": 64, "RY": 384, "Cz": ROWS_C, "Cy": 8 * ROWS_C}[kind]
        return full / 2 if msg[2] == (4 if kind[1] in "zZ" else 2) else full
    if kind == "cz":
        return 2 * ROWS_C
    if kind == "cy":
        return 2 * ROWS_C if msg[3] == 2 else 4 * ROWS_C
    if kind in ("Cx", "cx"):
        return (8 if kind == "Cx" else 4) * ROWS_C
    return {"qx": 64, "xc": ROWS_C, "vx": 560, "hx": 80, "hl": 160, "hc": 320, "xa": a, "xb": b}.get(kind, 8)


def build():
    tasks = {}

    def task(name, needs=(), after=(), cost=0.0, sends=()):
        needs, sends = list(needs), list(sends)
        tasks[name] = (needs, list(after), cost + 0.01 * (len(needs) + len(sends)), sends)

    first = []
    for s in SIGNS:
        first += [("Bz", s, 1), ("Ay", s, 1)]
    for s in SIGNS:
        first += [("Az", 0, s, 1), ("By", 0, s, 1)]
    task(
        ("start",),
        cost=0.5,
        sends=[("qx",)] + [("Cz", s, 1) for s in SIGNS] + [m + ("o",) for m in first]
        + [("Rz", s, 1) for s in SIGNS] + [("Ry", s, 1) for s in SIGNS],
    )
    task(("qx",), [("qx",)], [("start",)], sends=[m + ("t",) for m in first])
    for s in SIGNS:
        task(
            ("Ay", s),
            [("Ay", s, 1, "o"), ("Ay", s, 1, "t")],
            [("qx",)],
            sends=[("Ay", s, 2, "f")] + [("Az", wrap(-s, NY), u, 1, "f") for u in SIGNS],
        )
    task(
        ("Ay2",),
        [("Ay", s, 2, "f") for s in SIGNS],
        [("Ay", s) for s in SIGNS],
        sends=[("Az", 2, u, 1, "f") for u in SIGNS],
    )
    for dy in (0, 1, -1, 2):
        for s in SIGNS:
            for h in (1, 2, 3):
                task(
                    ("Az", dy, s, h),
                    [("Az", dy, s, h, p) for p in parts_of("Az", h, dy == 0)],
                    sends=[("Az", dy, s, h + 1, "f")],
                )
    for s in SIGNS:
        for h in (1, 2, 3):
            task(
                ("Bz", s, h),
                [("Bz", s, h, p) for p in parts_of("Bz", h, True)],
                sends=[("Bz", s, h + 1, "f")] + [("By", wrap(-s * h, NZ), u, 1, "f") for u in SIGNS],
            )
    task(
        ("Bz4",), [("Bz", s, 4, "f") for s in SIGNS], sends=[("By", 4, u, 1, "f") for u in SIGNS]
    )
    for dz in range(-3, 5):
        for s in SIGNS:
            task(
                ("By", dz, s),
                [("By", dz, s, 1, p) for p in parts_of("By", 1, dz == 0)],
                sends=[("By", dz, s, 2, "f")],
            )
    for s in SIGNS:
        for h in (1, 2, 3):
            task(("Cz", s, h), [("Cz", s, h)], sends=[("Cz", s, h + 1)])
        task(("Cy", s), [("Cy", s, 1)], sends=[("Cx", wrap(-s, NY)), ("Cy", s, 2)])
    task(
        ("CY0",),
        [("Cz", s, 4) for s in SIGNS],
        [("Cz", s, h) for s in SIGNS for h in (1, 2, 3)],
        sends=[("Cx", 0)] + [("Cy", s, 1) for s in SIGNS],
    )
    task(("Cy2",), [("Cy", s, 2) for s in SIGNS], [("Cy", s) for s in SIGNS], sends=[("Cx", 2)])
    late = {
        0: [],
        1: [("Bz4",)],
        2: [("Az", dy, s, 2) for dy in (0, 1, -1, 2) for s in SIGNS],
        3: [("Az", dy, s, 3) for dy in (0, 1, -1, 2) for s in SIGNS]
        + [("By", dz, s) for dz in range(-3, 5) for s in SIGNS],
    }[LATE]
    for s in SIGNS:
        task(("Ry", s), [("Ry", s, 1)], sends=[("Ry", s, 2)])
        for h in (1, 2, 3):
            task(("Rz", s, h), [("Rz", s, h)], sends=[("Rz", s, h + 1)])
            task(("RZ", s, h), [("RZ", s, h)], sends=[("RZ", s, h + 1)])
        task(("RY", s), [("RY", s, 1)], sends=[("RY", s, 2)])
    task(
        ("RZ0",),
        [("Ry", s, 2) for s in SIGNS],
        [("Ry", s) for s in SIGNS] + late,
        sends=[("RZ", s, 1) for s in SIGNS],
    )
    task(
        ("RY0",),
        [("Rz", s, 4) for s in SIGNS],
        [("Rz", s, h) for s in SIGNS for h in (1, 2, 3)] + late,
        sends=[("RY", s, 1) for s in SIGNS],
    )
    task(("vx",), after=[("start",)], cost=0.25, sends=[("vx",)])
    task(("hx",), after=[("vx",)], cost=0.25, sends=[("hx",)])
    task(("hl",), [("hx",)], [("hx",), ("Cy2",)], sends=[("hl",)])
    task(("hc",), [("hl",)], [("hl",)], sends=[("hc",)])
    task(("gram",), after=[("vx",)], cost=0.8)
    for g, planes in enumerate(PLANES):
        needs, after = [], [("m1", g - 1)] if g else [("load",), ("CY0",), ("Cy2",)]
        if g == len(PLANES) - 1:
            after.append(("m1c",))
        for dz in planes:
            for s in SIGNS:
                needs.append(("By", dz, s, 2, "f"))
                after.append(("By", dz, s))
            if dz == 0:
                after += [("Ay", s) for s in SIGNS] + [("Ay2",)]
            elif dz == 4:
                needs += [("Az", dy, s, 4, "f") for dy in (0, 1, -1, 2) for s in SIGNS]
                after.append(("Bz4",))
            else:
                s = -1 if dz > 0 else 1
                after += [("Az", dy, s, abs(dz)) for dy in (0, 1, -1, 2)] + [("Bz", s, abs(dz))]
        task(("m1", g), needs, after, cost=1.1 * len(planes))
    task(("load",), after=[("start",)], cost=0.1)
    for k in range(4):
        task(("xs", k), after=[("load",)] + ([("xs", k - 1)] if k else []), cost=0.7)
    task(
        ("m1c",),
        [("Cx", dy) for dy in (0, 1, -1, 2)],
        [("CY0",), ("Cy2",), ("m1", 0), ("xs", 3)],
        cost=0.9,
    )
    task(("img",), after=[("m1", len(PLANES) - 1)], cost=0.0)
    for n, dz in enumerate(ORDER):
        task(("m2", dz), after=[("img",)] + ([("m2", ORDER[n - 1])] if n else []), cost=0.95)
    for dy in (0, 1, -1, 2):
        task(("az", dy, 4), after=[("m2", 4)], cost=0.04, sends=[("az", dy, s, 4) for s in SIGNS])
        for s in SIGNS:
            for d in (3, 2, 1):
                task(
                    ("az", dy, s, d),
                    [("az", dy, s, d + 1)],
                    [("m2", s * d)],
                    cost=0.04,
                    sends=[("az", dy, s, d)],
                )
        task(("az", dy, 0), [("az", dy, s, 1) for s in SIGNS], [("m2", 0)], cost=0.04)
    task(("ay", 2), after=[("az", 2, 0)], cost=0.04, sends=[("ay", s, 2) for s in SIGNS])
    for s in SIGNS:
        task(("ay", s, 1), [("ay", s, 2)], [("az", s, 0)], cost=0.04, sends=[("ay", s, 1)])
    task(
        ("xa",), [("ay", s, 1) for s in SIGNS], [("az", 0, 0)], cost=0.04, sends=[("xa",)]
    )
    for dz in range(-3, 5):
        task(("by", dz, 2), after=[("m2", dz)], cost=0.04, sends=[("by", dz, s, 2) for s in SIGNS])
        for s in SIGNS:
            task(
                ("by", dz, s, 1),
                [("by", dz, s, 2)],
                [("m2", dz)],
                cost=0.04,
                sends=[("by", dz, s, 1)],
            )
        task(("by", dz, 0), [("by", dz, s, 1) for s in SIGNS], [("m2", dz)], cost=0.06)
    task(("bz", 4), after=[("by", 4, 0)], cost=0.04, sends=[("bz", s, 4) for s in SIGNS])
    for s in SIGNS:
        for d in (3, 2, 1):
            task(
                ("bz", s, d),
                [("bz", s, d + 1)],
                [("by", s * d, 0)],
                cost=0.04,
                sends=[("bz", s, d)],
            )
    task(("xb",), [("bz", s, 1) for s in SIGNS], [("by", 0, 0)], cost=0.06, sends=[("xb",)])
    for n, dz in enumerate(ORDER):
        task(("cx", dz), after=[("m2", dz)], cost=0.04, sends=[("cx", dz)])
        task(("cs", dz), [("cx", dz)], [("m2", dz)], cost=0.04)
    for g in (0, 1):
        done = [("cs", dz) for dz in GROUPS[g]]
        task(("cy", g, 2), after=done, cost=0.04, sends=[("cy", g, s, 2) for s in SIGNS])
        for s in SIGNS:
            task(("cy", g, s, 1), [("cy", g, s, 2)], done, cost=0.04, sends=[("cy", g, s, 1)])
        task(("cy", g, 0), [("cy", g, s, 1) for s in SIGNS], done, cost=0.04)
    for g in (0, 1):
        sends = [("cz", dz % NZ) for dz in GROUPS[g] if dz]
        task(("cz", g), after=[("cy", g, 0)], cost=0.05, sends=sends)
    task(("xc",), [("cz", k) for k in FAR], [("cy", 1, 0)], cost=0.05, sends=[("xc",)])
    for k in range(8):
        needs, after = [], [("m2", ORDER[-1])]
        if k == 0:
            needs += [("RZ", s, 4) for s in SIGNS] + [("RY", s, 2) for s in SIGNS]
            needs += [("hc",), ("vx",)]
            after += [("RZ", s, h) for s in SIGNS for h in (1, 2, 3)] + [("RY", s) for s in SIGNS]
            after += [("RZ0",), ("RY0",), ("hc",), ("vx",), ("gram",)]
        else:
            after += [("p8", k - 1)]
        task(("p8", k), needs, after, cost=0.65)
    task(("g1",), after=[("p8", 7)], cost=0.1, sends=[("g1z", k) for k in FAR])
    return tasks


PLANES = ((0,), (1, -1), (2, -2), (3, -3), (4,))
ORDER = (4, 3, -3, 2, -2, 1, -1, 0)
BIAS = {
    "By": 10, "Bz": 10, "RZ": -10, "RZ0": -20, "Ry": 10, "Rz": -10, "ay": 2, "az": -5,
    "bz": -10, "cz": 5, "g1": -10, "hc": 2, "m1": -20, "m2": -5, "vx": -2, "xs": -20,
}
LATE, RATE, DELAY, CLS = 2, 46.0, 2.2, True
SLACK = {
    "Ry": 1, "Rz": 2, "RZ": 1.5, "RY": 3, "vx": 3, "hx": 1, "hl": 5, "hc": 0,
}
GROUPS = (ORDER[:4], ORDER[4:])


def schedule(tasks):
    rate = {"z": RATE, "y": RATE, "x": RATE - 1, "c": 400.0}
    delay = {"z": DELAY, "y": DELAY, "x": DELAY + 0.5, "c": 0.8}
    waits = {}
    followers = {name: [] for name in tasks}
    for name, (needs, after, _, _) in tasks.items():
        for msg in needs:
            waits.setdefault(msg, []).append(name)
        for other in after:
            followers[other].append(name)

    def cost_of(msg):
        axis = link_of(msg)[0]
        return kilobytes(msg) / rate.get(axis, 40.0) + delay.get(axis, 3.0)

    @functools.cache
    def rank(name):
        _, _, cost, sends = tasks[name]
        rest = [rank(f) for f in followers[name]]
        rest += [cost_of(m) + max([rank(w) for w in waits.get(m, ())], default=0) for m in sends]
        return cost + max(rest, default=0)

    now, free, arrives, done, order = 0.0, {}, {}, {}, []
    left = dict(tasks)
    while left:
        ready, soonest = [], None
        for name, (needs, after, cost, sends) in left.items():
            if any(a not in done for a in after) or any(m not in arrives for m in needs):
                continue
            at = max([arrives[m] for m in needs], default=0.0)
            if at <= now:
                heavy = CLS and cost >= 0.3 and not sends
                ready.append((heavy, -rank(name) - BIAS.get(name[0], 0.0), at, name))
            else:
                soonest = at if soonest is None else min(soonest, at)
        if not ready:
            now = soonest
            continue
        name = min(ready, key=lambda r: r[:3])[3]
        _, _, cost, sends = left.pop(name)
        now += cost
        done[name] = now
        order.append(name)
        for msg in sends:
            link = link_of(msg)
            axis = link[0]
            begin = max(now, free.get(link, 0.0))
            free[link] = begin + kilobytes(msg) / rate.get(axis, 40.0)
            arrives[msg] = free[link] + delay.get(axis, 3.0) + SLACK.get(msg[0], 0.0)
    return order, done, arrives


def product(a, b, ca, cb):
    return lax.dot_general(a, b, (((ca,), (cb,)), ((), ())), preferred_element_type=F32)


def kernel(
    order, tasks, index,
    x_hbm, hid_hbm, res_hbm, basis_hbm,
    own_ref, first_ref, second_ref,
    xv, q, qc, xc, select, p, send_a, send_b, recv_a, recv_b,
    send_cx, recv_cx, send_cy, recv_cy, send_cz, recv_cz, acc, img, r, v16, ht, hs, cur,
    early, tokens8, basis_ref, hid_ref, res_ref, gz, gy, gx, hz, hw, load_sem, send_sem, recv_sem,
):
    dp, fs = lax.axis_index("dp"), lax.axis_index("fsdp")
    z, y, xh = fs // 8, lax.rem(fs // 2, 4), lax.rem(fs, 2)
    xl, core = dp // 2, lax.rem(dp, 2)
    other = 1 - xh

    zi = {d: lax.rem(z + (d + NZ), NZ) for d in range(-3, 8)}
    zi[-4] = zi[4]
    yi = {d: lax.rem(y + (d + NY), NY) for d in range(-1, 4)}
    yi[-2] = yi[2]

    def fsdp(za, ya, xa):
        return (za * NY + ya) * 2 + xa

    def along_z(d):
        return (dp, fsdp(zi[d], y, xh))

    def along_y(d):
        return (dp, fsdp(z, yi[d], xh))

    def along_x(k):
        xa = 1 - xh if k & 4 else xh
        la = 1 - xl if k & 2 else xl
        ca = 1 - core if k & 1 else core
        return (la * 2 + ca, fsdp(z, y, xa))

    def along_w(k):
        bits = k & 7
        xa = 1 - xh if bits & 4 else xh
        la = 1 - xl if bits & 2 else xl
        ca = 1 - core if bits & 1 else core
        return (la * 2 + ca, fsdp(z, yi[k // 8], xa))

    partners = [along_z(d) for d in FAR] + [along_w(k) for k in WIDE]

    barrier = pltpu.get_barrier_semaphore()
    loads = [
        pltpu.make_async_copy(basis_hbm.at[K - 1], basis_ref.at[K - 1], load_sem.at[0]),
        pltpu.make_async_copy(res_hbm, res_ref, load_sem.at[1]),
        pltpu.make_async_copy(hid_hbm, hid_ref, load_sem.at[2]),
        pltpu.make_async_copy(
            basis_hbm.at[pl.ds(0, K - 1)], basis_ref.at[pl.ds(0, K - 1)], load_sem.at[3]
        ),
        pltpu.make_async_copy(x_hbm, xv, load_sem.at[4]),
    ]
    for load in loads:
        load.start()
    for device in partners:
        pl.semaphore_signal(barrier, inc=1, device_id=device, device_id_type=MESH)
    loads[0].wait()
    loads[1].wait()
    q[:, :, other, pl.ds(ROWS_A + ROWS_B, ROWS_C)] = jnp.zeros((NZ, NY, ROWS_C, WID), BF)
    narrow = basis_ref[K - 1].astype(BF)
    q[z, y, xh] = narrow
    v16[K - 1, xh] = narrow
    r[z, y] = res_ref[...]

    def q_part(rows, part, oz, oy):
        at = q.at[zi[oz], yi[oy]]
        which = {"f": slice(None), "o": xh, "t": other}.get(part, part)
        return at.at[which, rows]

    a_rows, b_rows = pl.ds(0, ROWS_A), pl.ds(ROWS_A, ROWS_B)
    c_rows = pl.ds(ROWS_A + ROWS_B, ROWS_C)

    def lane_half(sign):
        return pl.ds(half_of(sign) * (WID // 2), WID // 2)

    def slot_a(msg):
        if msg[0] == "az":
            _, dy, s, d = msg
            base = {0: 0, 1: 7, -1: 14, 2: 21}[dy]
            return base + (6 if d == 4 else (d - 1) * 2 + half_of(s)), d == 4, s
        if msg[0] == "ay":
            _, s, d = msg
            return 28 + (2 if d == 2 else half_of(s)), d == 2, s
        return 31, False, 1

    def slot_b(msg):
        if msg[0] == "by":
            _, dz, s, d = msg
            return (dz + 3) * 3 + (2 if d == 2 else half_of(s)), d == 2, s
        if msg[0] == "bz":
            _, s, d = msg
            return 24 + (6 if d == 4 else (d - 1) * 2 + half_of(s)), d == 4, s
        return 31, False, 1

    def piece(buf, slot):
        n, halved, s = slot
        return buf.at[n, half_of(s)] if halved else buf.at[n]

    def place(msg):
        kind = msg[0]
        if kind == "qx":
            rows = pl.ds(0, ROWS_A + ROWS_B)
            here = q.at[z, y, xh, rows]
            return here, here, q.at[z, y, other, rows], along_x(4)
        if kind == "Cz":
            _, s, h = msg
            lanes = lane_half(s) if h == 4 else slice(None)
            here = q.at[zi[wrap(-s * (h - 1), NZ)], y, xh, c_rows, lanes]
            return here, here, q.at[zi[wrap(-s * h, NZ)], y, xh, c_rows, lanes], along_z(s)
        if kind == "Cy":
            _, s, h = msg
            lanes = lane_half(s) if h == 2 else slice(None)
            here = q.at[:, yi[wrap(-s * (h - 1), NY)], xh, c_rows, lanes]
            return here, here, q.at[:, yi[wrap(-s * h, NY)], xh, c_rows, lanes], along_y(s)
        if kind == "Cx":
            lands = qc.at[:, yi[msg[1]]]
            return q.at[:, yi[msg[1]], xh, c_rows], lands, lands, along_x(4)
        if kind == "cx":
            n = ORDER.index(msg[1])
            return send_cx.at[n], recv_cx.at[n], recv_cx.at[n], along_x(4)
        if kind == "cy":
            _, g, s, d = msg
            n, lanes = (2, lane_half(s)) if d == 2 else (half_of(s), slice(None))
            target = recv_cy.at[g, n, :, :, lanes]
            return send_cy.at[g, n, :, :, lanes], target, target, along_y(s)
        if kind == "cz":
            n = msg[1]
            return send_cz.at[n], recv_cz.at[n], recv_cz.at[n], along_z(n)
        if kind == "xc":
            return send_cz.at[0], recv_cz.at[0], recv_cz.at[0], along_x(4)
        if kind in ("Ay", "Az", "Bz", "By"):
            rows = a_rows if kind[0] == "A" else b_rows
            if kind in ("Ay", "Bz"):
                _, s, h, part = msg
            else:
                _, off, s, h, part = msg
            size = NZ if kind[1] == "z" else NY
            if h == size // 2:
                part = half_of(s)
            if kind[1] == "y":
                oz = off if kind == "By" else 0
                here = q_part(rows, part, oz, wrap(-s * (h - 1), NY))
                there = q_part(rows, part, oz, wrap(-s * h, NY))
                return here, here, there, along_y(s)
            oy = off if kind == "Az" else 0
            here = q_part(rows, part, wrap(-s * (h - 1), NZ), oy)
            there = q_part(rows, part, wrap(-s * h, NZ), oy)
            return here, here, there, along_z(s)
        if kind in ("Ry", "RZ", "Rz", "RY"):
            _, s, h = msg
            last = h == (NY if kind[1] in "yY" else NZ) // 2
            rows = pl.ds(0, 16) if kind in ("Ry", "RZ") else pl.ds(16, 48)
            lanes = lane_half(s) if last else slice(None)
            n = NY if kind[1] in "yY" else NZ
            a, b = wrap(-s * (h - 1), n), wrap(-s * h, n)
            if kind == "Ry":
                here, there = r.at[z, yi[a], rows, lanes], r.at[z, yi[b], rows, lanes]
            elif kind == "Rz":
                here, there = r.at[zi[a], y, rows, lanes], r.at[zi[b], y, rows, lanes]
            elif kind == "RZ":
                here, there = r.at[zi[a], :, rows, lanes], r.at[zi[b], :, rows, lanes]
            else:
                here, there = r.at[:, yi[a], rows, lanes], r.at[:, yi[b], rows, lanes]
            return here, here, there, along_y(s) if n == NY else along_z(s)
        if kind == "vx":
            here = v16.at[pl.ds(0, K - 1), xh]
            return here, here, v16.at[pl.ds(0, K - 1), other], along_x(4)
        if kind == "hx":
            return hs.at[other], ht.at[xl, core, xh], ht.at[xl, core, other], along_x(4)
        if kind == "hl":
            here = ht.at[xl, core]
            return here, here, ht.at[1 - xl, core], along_x(2)
        if kind == "hc":
            here = ht.at[:, core]
            return here, here, ht.at[:, 1 - core], along_x(1)
        if kind in ("az", "ay", "xa"):
            slot = slot_a(msg)
            target = piece(recv_a, slot)
            src = piece(send_a, slot)
        elif kind in ("by", "bz", "xb"):
            slot = slot_b(msg)
            target = piece(recv_b, slot)
            src = piece(send_b, slot)
        if kind in ("xa", "xb"):
            return src, target, target, along_x(4)
        if kind in ("az", "by"):
            return src, target, target, along_z(msg[2]) if kind == "az" else along_y(msg[2])
        if kind in ("ay", "bz"):
            return src, target, target, along_y(msg[1]) if kind == "ay" else along_z(msg[1])
        k = msg[1]
        if kind == "g1z":
            here = gz.at[z]
            return here, here, gz.at[zi[-k + NZ if k > 3 else -k]], along_z(k)
        if kind == "g1y":
            here = gy.at[y]
            return here, here, gy.at[yi[-k + NY if k > 1 else -k]], along_y(k)
        if kind == "g2z":
            here = hz.at[z, pl.ds(0, 2)]
            return here, here, hz.at[zi[-k + NZ if k > 3 else -k], pl.ds(0, 2)], along_z(k)
        xa = 1 - xh if k & 4 else xh
        la = 1 - xl if k & 2 else xl
        ca = 1 - core if k & 1 else core
        mine, theirs = xh * 4 + xl * 2 + core, xa * 4 + la * 2 + ca
        if kind == "g1x":
            return gx.at[mine], gx.at[mine], gx.at[theirs], along_x(k)
        d = k // 8
        here = hw.at[y * 8 + mine, pl.ds(0, 2)]
        lands = hw.at[yi[-d + NY if d > 1 else -d] * 8 + theirs, pl.ds(0, 2)]
        return here, here, lands, along_w(k)

    started = []

    def send(msg):
        src, target, _, device = place(msg)
        n = index[msg]
        copy = pltpu.make_async_remote_copy(
            src_ref=src, dst_ref=target, send_sem=send_sem.at[n], recv_sem=recv_sem.at[n],
            device_id=device, device_id_type=MESH,
        )
        copy.start()
        started.append(copy)

    def receive(msg):
        _, _, lands, device = place(msg)
        n = index[msg]
        pltpu.make_async_remote_copy(
            src_ref=lands, dst_ref=lands, send_sem=send_sem.at[n], recv_sem=recv_sem.at[n],
            device_id=device, device_id_type=MESH,
        ).wait_recv()

    def fold(rows, buf, where, slots, out):
        for k in (0, 1):
            total = p[where[0], where[1], k, rows]
            for n, halved, s in slots:
                if not halved or half_of(s) == k:
                    total = total + buf[n, k].astype(F32)
            if out is None:
                p[where[0], where[1], k, rows] = total
            else:
                out[0][out[1], k] = total.astype(BF)

    def fold_a(where, msgs, out=None):
        fold(a_rows, recv_a, where, [slot_a(m) for m in msgs], out and (send_a, slot_a(out)[0]))

    def fold_b(where, msgs, out=None):
        fold(b_rows, recv_b, where, [slot_b(m) for m in msgs], out and (send_b, slot_b(out)[0]))

    def fold_c(plane, row, arrived, out=None):
        for h in (0, 1):
            lanes = pl.ds(h * (WID // 2), WID // 2)
            total = p[plane, row, xh, c_rows, lanes]
            for ref, s in arrived:
                if s is None or half_of(s) == h:
                    total = total + ref[:, lanes].astype(F32)
            if out is None:
                p[plane, row, xh, c_rows, lanes] = total
            else:
                out[:, lanes] = total.astype(BF)

    def lanes_of(plane):
        return pl.ds(pl.multiple_of(plane * (NY * 2 * BLK), 128), NY * 2 * BLK)

    def per_token(rows, k, part=None):
        if part is None:
            many, errors, hidden = 512, r[2 * k : 2 * k + 2], ht[k // 2, k % 2]
        else:
            many, errors = 256, r[2 * k + part]
            hidden = ht[k // 2, k % 2, :, :, 256 * part : 256 * (part + 1)]
        mapped = product(rows, errors.reshape(many, WID), 1, 1)
        n = rows.shape[0] // (2 * BLK)
        hidden = hidden.reshape(2 * BLK, many).astype(F32)
        return jnp.sum(mapped.reshape(n, 2 * BLK, many) * hidden[None], axis=1)

    def per_example(tokens):
        t = lax.broadcasted_iota(jnp.int32, (512, 128), 0)
        e = lax.broadcasted_iota(jnp.int32, (512, 128), 1)
        owner = (t // 64) * 4 + 2 * xh + lax.rem(t, 64) // EX_TOK
        marks = jnp.where(owner == lax.rem(e, 32), 1.0, 0.0).astype(BF)
        terms, rest = [], tokens
        for _ in range(3):
            terms.append(rest.astype(BF).astype(F32))
            rest = rest - terms[-1]
        sums = product(jnp.concatenate(terms, axis=0).astype(BF), marks, 1, 0)
        return sums[0:8] + sums[8:16] + sums[16:24]

    def work(name):
        kind = name[0]
        if kind == "start":
            pl.semaphore_wait(barrier, len(partners))
        elif kind == "vx":
            loads[3].wait()
            for n in range(K - 1):
                v16[n, xh] = basis_ref[n].astype(BF)
        elif kind == "hx":
            loads[2].wait()
            for which in (0, 1):
                cuts = [(2 * n + which) * 64 for n in range(8)]
                pieces = [hid_ref[:, at : at + 64] for at in cuts]
                hs[which] = jnp.concatenate(pieces, axis=1)
            ht[xl, core, xh] = hs[xh]
        elif kind == "gram":
            lane = lax.broadcasted_iota(jnp.int32, (8, 128), 1)
            table = jnp.zeros((8, 128), F32)
            for i in range(K):
                rows = [jnp.sum(basis_ref[j] * basis_ref[i], axis=0, keepdims=True) for j in range(K)]
                column = jnp.sum(jnp.concatenate(rows, axis=0), axis=1, keepdims=True)
                table = table + jnp.where(lane == i, column, 0.0)
            early[8:16] = table
            early[0:8] = jnp.zeros((8, 128), F32)
        elif kind == "load":
            loads[4].wait()
        elif kind == "m1":
            total = None
            for dz in PLANES[name[1]]:
                term = product(xv[:, lanes_of(zi[dz])], q[zi[dz]].reshape(NY * 2 * BLK, WID), 1, 0)
                total = term if total is None else total + term
            if name[1] == len(PLANES) - 1:
                img[...] = (acc[...] + total).astype(BF)
            else:
                acc[...] = total if name[1] == 0 else acc[...] + total
        elif kind == "xs":
            k = name[1]
            if k == 0:
                f = lax.broadcasted_iota(jnp.int32, (1280, 128), 0)
                at = lax.broadcasted_iota(jnp.int32, (1280, 128), 1)
                block = (f * 52429) >> 22
                inside = f - block * BLK - (ROWS_A + ROWS_B)
                hit = (inside >= 0) & ((block & 1) == other) & ((block >> 1) * ROWS_C + inside == at)
                select[...] = jnp.where(hit, 1.0, 0.0).astype(BF)
            columns = xv[:, 1280 * k : 1280 * (k + 1)]
            xc[:, 128 * k : 128 * (k + 1)] = product(columns, select[...], 1, 0).astype(BF)
        elif kind == "m1c":
            acc[...] = acc[...] + product(xc[...], qc[...].reshape(NZ * NY * ROWS_C, WID), 1, 0)
        elif kind == "img":
            pass
        elif kind == "m2":
            plane = zi[name[1]]
            p[plane] = product(xv[:, lanes_of(plane)], img[...], 0, 0).reshape(NY, 2, BLK, WID)
        elif kind == "az":
            dy = name[1]
            if name[2] == 4:
                fold_a((zi[4], yi[dy]), [], ("az", dy, 1, 4))
            elif name[2] == 0:
                fold_a((z, yi[dy]), [("az", dy, s, 1) for s in SIGNS])
            else:
                s, d = name[2:]
                fold_a((zi[s * d], yi[dy]), [("az", dy, s, d + 1)], ("az", dy, s, d))
        elif kind == "ay":
            if name[1] == 2 and len(name) == 2:
                fold_a((z, yi[2]), [], ("ay", 1, 2))
            else:
                s = name[1]
                fold_a((z, yi[s]), [("ay", s, 2)], ("ay", s, 1))
        elif kind == "xa":
            fold_a((z, y), [("ay", s, 1) for s in SIGNS])
            fold_a((z, y), [], ("xa",))
        elif kind == "by":
            dz = name[1]
            if len(name) == 4:
                s = name[2]
                fold_b((zi[dz], yi[s]), [("by", dz, s, 2)], ("by", dz, s, 1))
            elif name[2] == 2:
                fold_b((zi[dz], yi[2]), [], ("by", dz, 1, 2))
            else:
                fold_b((zi[dz], y), [("by", dz, s, 1) for s in SIGNS])
        elif kind == "bz":
            if len(name) == 2:
                fold_b((zi[4], y), [], ("bz", 1, 4))
            else:
                s, d = name[1:]
                fold_b((zi[s * d], y), [("bz", s, d + 1)], ("bz", s, d))
        elif kind == "xb":
            fold_b((z, y), [("bz", s, 1) for s in SIGNS])
            fold_b((z, y), [], ("xb",))
        elif kind == "cx":
            send_cx[ORDER.index(name[1])] = p[zi[name[1]], :, other, c_rows].astype(BF)
        elif kind == "cs":
            plane = zi[name[1]]
            arrived = recv_cx[ORDER.index(name[1])].astype(F32)
            p[plane, :, xh, c_rows] = p[plane, :, xh, c_rows] + arrived
        elif kind == "cy":
            g = name[1]
            for j, dz in enumerate(GROUPS[g]):
                if len(name) == 4:
                    s = name[2]
                    got = [(recv_cy.at[g, 2, j], s)]
                    fold_c(zi[dz], yi[s], got, send_cy.at[g, half_of(s), j])
                elif name[2] == 2:
                    fold_c(zi[dz], yi[2], [], send_cy.at[g, 2, j])
                else:
                    fold_c(zi[dz], y, [(recv_cy.at[g, n, j], None) for n in (0, 1)])
        elif kind == "cz":
            for dz in GROUPS[name[1]]:
                if dz:
                    fold_c(zi[dz], y, [], send_cz.at[dz % NZ])
        elif kind == "xc":
            fold_c(z, y, [(recv_cz.at[n], None) for n in range(1, NZ)])
            fold_c(z, y, [], send_cz.at[0])
        elif kind == "p8":
            k = name[1]
            if k == 0:
                v16[K - 1, other, pl.ds(0, ROWS_A + ROWS_B)] = q[z, y, other, pl.ds(0, ROWS_A + ROWS_B)]
                v16[K - 1, other, c_rows] = qc[z, y]
            half = pl.ds(256 * (k % 2), 256)
            tokens8[:, half] = per_token(v16[...].reshape(K * 2 * BLK, WID), k // 2, k % 2)
            if k % 2:
                sums = per_example(tokens8[...])
                lane = lax.broadcasted_iota(jnp.int32, (8, 128), 1)
                early[0:8] = early[0:8] + jnp.where(lane // 32 == k // 2, sums, 0.0)
        elif kind == "g1":
            gz[z] = early[...]

    def ring_sum(buf, n, rows=16):
        total = buf[0, 0:rows]
        for k in range(1, n):
            total = total + buf[k, 0:rows]
        return total

    for name in order:
        needs, _, _, sends = tasks[name]
        if name[0] != "start":
            for msg in needs:
                receive(msg)
        work(name)
        for msg in sends:
            send(msg)

    for k in FAR:
        receive(("g1z", k))
    gy[y] = ring_sum(gz, NZ)
    for k in range(1, NY):
        send(("g1y", k))
    receive(("xa",))
    receive(("xb",))
    receive(("xc",))
    for k in range(1, NY):
        receive(("g1y", k))
    gx[xh * 4 + xl * 2 + core] = ring_sum(gy, NY)
    for k in range(1, 8):
        send(("g1x", k))
    cur[xh, c_rows] = p[z, y, xh, c_rows] * (1.0 / TOKENS)
    cur[other, c_rows] = recv_cz[0].astype(F32) * (1.0 / TOKENS)
    for k in (0, 1):
        cur[k, a_rows] = (p[z, y, k, a_rows] + recv_a[31, k].astype(F32)) * (1.0 / TOKENS)
        cur[k, b_rows] = (p[z, y, k, b_rows] + recv_b[31, k].astype(F32)) * (1.0 / TOKENS)
    mine = cur[xh]
    rows = [jnp.sum(basis_ref[n] * mine, axis=0, keepdims=True) for n in range(K)]
    rows.append(jnp.sum(mine * mine, axis=0, keepdims=True))
    rows.append(jnp.zeros((7, WID), F32))
    sums = jnp.sum(jnp.concatenate(rows, axis=0), axis=1, keepdims=True)
    sub = lax.broadcasted_iota(jnp.int32, (16, 128), 0)
    lane = lax.broadcasted_iota(jnp.int32, (16, 128), 1)
    sums = jnp.sum(jnp.where(sub == lane, sums, 0.0), axis=0, keepdims=True)
    both = cur[...].reshape(2 * BLK, WID)
    high = both.astype(BF)
    pair = jnp.concatenate([high, (both - high.astype(F32)).astype(BF)], axis=0)
    tokens = [jnp.sum(per_token(pair, k), axis=0, keepdims=True) for k in range(4)]
    tokens = jnp.concatenate(tokens + [jnp.zeros((4, 512), F32)], axis=0)
    sub = lax.broadcasted_iota(jnp.int32, (8, 128), 0)
    lane = lax.broadcasted_iota(jnp.int32, (8, 128), 1)
    shown = jnp.where(lane // 32 == sub, per_example(tokens), 0.0)
    shown = jnp.sum(shown, axis=0, keepdims=True)
    hz[z, 0:1] = shown
    hz[z, 1:2] = sums
    for k in FAR:
        send(("g2z", k))
    own_ref[...] = mine
    drain = list(started)
    for copy in drain[:-40]:
        copy.wait_send()
    for k in range(1, NZ):
        receive(("g2z", k))
    hw[y * 8 + xh * 4 + xl * 2 + core, 0:2] = ring_sum(hz, NZ, 2)
    for k in WIDE:
        send(("g2w", k))
    for copy in drain[-40:]:
        copy.wait_send()
    for k in range(1, 8):
        receive(("g1x", k))
    first_ref[...] = ring_sum(gx, 8)
    for k in WIDE:
        receive(("g2w", k))
    second_ref[0:2] = ring_sum(hw, 32, 2)
    second_ref[2:8] = jnp.zeros((6, 128), F32)
    for copy in started[len(drain):]:
        copy.wait_send()


def finish(own_ref, first_ref, second_ref, basis_ref, new_ref, hess_ref, proj_ref):
    mean = 1.0 / (FF * D)
    first, second = first_ref[...], second_ref[...]
    sub = lax.broadcasted_iota(jnp.int32, (8, 128), 0)
    lane = lax.broadcasted_iota(jnp.int32, (8, 128), 1)
    row = second[1:2] * mean
    coeff = jnp.sum(jnp.where(sub == lane, row, 0.0), axis=1, keepdims=True)
    squared = jnp.sum(jnp.where(lane[0:1] == K, row, 0.0), axis=1, keepdims=True)
    row = jnp.where(lane[0:1] < K, row, 0.0)
    cross = jnp.sum(coeff * first[8:16], axis=0, keepdims=True) * row
    cross = jnp.sum(cross, axis=1, keepdims=True) * mean
    twice = 2.0 * jnp.sum(row * row, axis=1, keepdims=True)
    beta = jnp.sqrt(jnp.maximum(squared - twice + cross, squared * 1e-12))
    inverse = 1.0 / beta
    hess_ref[...] = jnp.where(lane[0:1] == K, beta, row)[:, 0 : K + 1]
    left = own_ref[...]
    for n in range(K):
        left = left - coeff[n : n + 1] * basis_ref[n]
    new_ref[0] = left * inverse
    last = (second[0:1] - jnp.sum(coeff * first[0:8], axis=0, keepdims=True)) * inverse
    scale = (FF * D) ** (-0.5)
    shown = jnp.concatenate([first[0:8], jnp.broadcast_to(last, (8, 128))], axis=0) * scale
    dp = lax.axis_index("dp")
    for n in range(4):
        @pl.when(dp == n)
        def _():
            proj_ref[...] = shown[0 : K + 1, n * 32 : (n + 1) * 32]


def local(train_hidden, index_hidden, index_resid, basis):
    tasks = build()
    order, _, _ = schedule(tasks)
    messages = [m for name in tasks for m in tasks[name][3]]
    messages += [("g1y", k) for k in range(1, NY)] + [("g1x", k) for k in range(1, 8)]
    messages += [("g2z", k) for k in FAR] + [("g2w", k) for k in WIDE]
    index = {m: n for n, m in enumerate(messages)}
    vmem = pltpu.VMEM
    whole = pl.BlockSpec(memory_space=pltpu.VMEM)
    call = pl.pallas_call(
        functools.partial(kernel, order, tasks, index),
        out_shape=(
            jax.ShapeDtypeStruct((BLK, WID), F32),
            jax.ShapeDtypeStruct((16, 128), F32),
            jax.ShapeDtypeStruct((8, 128), F32),
        ),
        in_specs=[pl.BlockSpec(memory_space=pl.ANY)] * 4,
        out_specs=(whole, whole, whole),
        scratch_shapes=[
            vmem((1024, FF), BF),
            vmem((NZ, NY, 2, BLK, WID), BF),
            vmem((NZ, NY, ROWS_C, WID), BF),
            vmem((1024, NZ * NY * ROWS_C), BF),
            vmem((1280, 128), BF),
            vmem((NZ, NY, 2, BLK, WID), F32),
            vmem((32, 2, ROWS_A, WID), BF),
            vmem((32, 2, ROWS_B, WID), BF),
            vmem((32, 2, ROWS_A, WID), BF),
            vmem((32, 2, ROWS_B, WID), BF),
            vmem((NZ, NY, ROWS_C, WID), BF),
            vmem((NZ, NY, ROWS_C, WID), BF),
            vmem((2, 3, 4, ROWS_C, WID), BF),
            vmem((2, 3, 4, ROWS_C, WID), BF),
            vmem((8, ROWS_C, WID), BF),
            vmem((8, ROWS_C, WID), BF),
            vmem((1024, WID), F32),
            vmem((1024, WID), BF),
            vmem((NZ, NY, 64, WID), BF),
            vmem((K, 2, BLK, WID), BF),
            vmem((2, 2, 2, BLK, WID), BF),
            vmem((2, BLK, WID), BF),
            vmem((2, BLK, WID), F32),
            vmem((16, 128), F32),
            vmem((8, 512), F32),
            vmem((K, BLK, WID), F32),
            vmem((BLK, 1024), BF),
            vmem((64, WID), BF),
            vmem((NZ, 16, 128), F32),
            vmem((NY, 16, 128), F32),
            vmem((8, 16, 128), F32),
            vmem((NZ, 8, 128), F32),
            vmem((32, 8, 128), F32),
            pltpu.SemaphoreType.DMA((5,)),
            pltpu.SemaphoreType.DMA((len(messages),)),
            pltpu.SemaphoreType.DMA((len(messages),)),
        ],
        compiler_params=pltpu.CompilerParams(
            collective_id=0, has_side_effects=True, vmem_limit_bytes=60 * 2**20
        ),
        cost_estimate=pl.CostEstimate(
            flops=14 * 10**9, bytes_accessed=13 * 10**6, transcendentals=0
        ),
        name="arnoldi",
    )
    own, first, second = call(train_hidden, index_hidden.T, index_resid, basis)
    new, hess, proj = pl.pallas_call(
        finish,
        out_shape=(
            jax.ShapeDtypeStruct((1, BLK, WID), F32),
            jax.ShapeDtypeStruct((1, K + 1), F32),
            jax.ShapeDtypeStruct((K + 1, 32), F32),
        ),
        in_specs=[whole] * 4,
        out_specs=(whole, whole, whole),
        name="finish",
    )(own, first, second, basis)
    return new, hess, proj.T


def solution(mesh):
    in_specs = (P("fsdp", None), P("dp", "fsdp"), P("fsdp", "dp"), P(None, "fsdp", "dp"))
    out_specs = (P(None, "fsdp", "dp"), P(), P("dp", None))
    return jax.shard_map(local, mesh=mesh, in_specs=in_specs, out_specs=out_specs, check_vma=False)
```
